256 devices in a mesh: gx: 16 (over z, core), gy: 4 (over x), gz: 4 (over y).
Axes of the slice: x: 4, y: 4, z: 8, core: 2. Of those that a mesh axis runs over, the one named last changes fastest.
Arguments:
- velocity: float32 [3, 64, 128, 2048], P(None, 'gz', 'gy', 'gx'), may hold values from 0.2 to 1.5
- adjoint: float32 [3, 64, 128, 2048], P(None, 'gz', 'gy', 'gx'), may hold values from -6 to 6
- pressure: float32 [64, 128, 2048], P('gz', 'gy', 'gx'), may hold values from -6 to 6
- viscosity: float32 [64, 128, 2048], P('gz', 'gy', 'gx'), may hold values from 0.02 to 0.2
- disk_cells: int32 [131072], P(('gx', 'gy', 'gz')), may hold values from 0 to 65535, as said below
- disk_turbine: int32 [131072], P(('gx', 'gy', 'gz')), may hold values from 0 to 1023, as said below
- disk_weight: float32 [131072], P(('gx', 'gy', 'gz')), may hold values from 0.01 to 0.03
- disk_dweight: float32 [2, 131072], P(None, ('gx', 'gy', 'gz')), may hold values from -0.75 to 0.75
- yaw: float32 [1024], P(('gx', 'gy', 'gz')), may hold values from -0.5 to 0.5
- thrust_coef: float32 [1024], P(('gx', 'gy', 'gz')), may hold values from 0.6 to 0.9
- owner_slot: int32 [1024], replicated, may hold values from 0 to 1023, each once
Outputs:
- velocity_next: float32 [3, 64, 128, 2048], P(None, 'gz', 'gy', 'gx')
- adjoint_next: float32 [3, 64, 128, 2048], P(None, 'gz', 'gy', 'gx')
- pressure_next: float32 [64, 128, 2048], P('gz', 'gy', 'gx')
- yaw_grad: float32 [1024], P(('gx', 'gy', 'gz'))
- position_grad: float32 [2, 1024], P(None, ('gx', 'gy', 'gz'))
The draws below stay inside these ranges and needn't reach their ends.
Inputs may be any that keep to these rules, and one draw needn't show every extreme that they name: `disk_cells`: a cell of the entry's own device tile. `disk_turbine`: every turbine has entries; turbine t belongs to the column of tiles number t // (4 * 4), numbered bx * 4 + by, and its entries lie on the tiles of that column or of the columns just before and after it streamwise.
All inputs are finite; a program needn't handle non-finite values.
Results may differ from the reference program's by a relative error of at most 0.00027.
Values sent between devices are 32-bit elements; how exact they have to be, the bound alone decides.
No kernel may reach another device: no remote copies, remote signals or barrier semaphores. Data moves between devices by JAX's collectives and lax.ppermute only.
A program may use at most 64 MiB of HBM per device.

```python
import math
import jax
import jax.numpy as jnp

CX = 128
CY = 32
CZ = 16
DISK_DEV = 512
TURB_DEV = 4
SWEEPS = 8
NX = 2048
NY = 128
NZ = 64
TURBINES = 1024
ENTRIES = 131072
N_GX = 16
N_GY = 4
N_GZ = 4


def disk_layout(key):
    entry = jnp.arange(ENTRIES, dtype=jnp.int32)
    local = entry % DISK_DEV
    device = entry // DISK_DEV
    block_x = device // (N_GY * N_GZ)
    block_y = device // N_GZ % N_GY
    column = block_x * N_GY + block_y
    columns = N_GX * N_GY
    per_column = TURB_DEV * N_GZ
    keys = jax.random.split(key, 10)
    side = jax.random.randint(keys[0], (ENTRIES,), 0, 8)
    first = jax.random.randint(keys[1], (ENTRIES,), 0, per_column)
    second = jax.random.randint(keys[2], (ENTRIES,), 0, per_column)
    up_count = jax.random.randint(keys[6], (columns,), 0, 4)[column]
    down_count = jax.random.randint(keys[7], (columns,), 0, 4)[column]
    shift = jax.random.randint(keys[8], (columns,), 0, per_column)[column]
    skewed = jax.random.randint(keys[9], (columns,), 0, 2)[column]
    seeded = local < per_column
    drawn = jnp.where(skewed == 1, jnp.minimum(first, second), first)
    member = jnp.where(seeded, local, (drawn + shift) % per_column)
    upstream = (side < up_count) & (block_x > 0) & jnp.logical_not(seeded)
    downstream = (side >= 8 - down_count) & (block_x < N_GX - 1) & jnp.logical_not(seeded)
    column_x = block_x - upstream.astype(jnp.int32) + downstream.astype(jnp.int32)
    turbine = (column_x * N_GY + block_y) * per_column + member
    spread_x = max(CX // (2 * per_column), 1)
    jitter_x = jax.random.randint(keys[3], (ENTRIES,), 0, spread_x)
    centre_x = member * CX // per_column + jitter_x
    cell_i = jnp.where(upstream, jitter_x, jnp.where(downstream, CX - 1 - jitter_x, centre_x))
    spread_y = max(CY // 4, 1)
    cell_j = (member % 4 * CY // 4 + jax.random.randint(keys[4], (ENTRIES,), 0, spread_y)) % CY
    cell_k = jax.random.randint(keys[5], (ENTRIES,), 0, CZ)
    cells = (cell_k * CY + cell_j) * CX + cell_i
    cells = jnp.where(local == 0, 0, cells)
    cells = jnp.where(local == DISK_DEV - 1, CX * CY * CZ - 1, cells)
    return (cells.astype(jnp.int32), turbine.astype(jnp.int32))


def draw_disk_cells(key, part):
    cells, turbine = disk_layout(key)
    return cells


def draw_disk_turbine(key, part):
    cells, turbine = disk_layout(key)
    return turbine


def block_levels(rng, shape, cuts, low, top_value):
    level = 1.0
    for dim, blocks in cuts:
        draws = jax.random.uniform(jax.random.fold_in(jax.random.fold_in(rng, 6), dim), (blocks,), jnp.float32, low / len(cuts), top_value / len(cuts))
        level = level * jnp.repeat(jnp.exp(draws), shape[dim] // blocks).reshape((-1,) + (1,) * (len(shape) - 1 - dim))
    return level


def bell_draw(own_key, extent, scale, most, cuts=(), kind=jnp.bfloat16):
    result = scale * jax.random.normal(own_key, extent, jnp.float32)
    if cuts:
        result = result * block_levels(own_key, extent, cuts, -0.22, 0.18)
    return jnp.clip(result, -most, most).astype(kind)


def setup_inputs(seed: int = 0) -> dict:
    splits = jax.random.split(jax.random.key(seed), 12)
    velocity = jnp.clip(0.2 + 1.3 * jax.random.uniform(splits[0], (3, NZ, NY, NX), jnp.float32) ** block_levels(splits[0], (3, NZ, NY, NX), ((1, 4), (2, 4), (3, 16)), -0.2, 0.2), 0.2, 1.5)
    adjoint = bell_draw(splits[1], (3, NZ, NY, NX), 1.0, 6.0, ((1, 4), (2, 4), (3, 16)), jnp.float32)
    pressure = bell_draw(splits[2], (NZ, NY, NX), 1.0, 6.0, ((0, 4), (1, 4), (2, 16)), jnp.float32)
    viscosity = jnp.clip(jnp.exp(math.log(0.2) - 2.3025851 * jax.random.uniform(splits[3], (NZ, NY, NX), jnp.float32) ** block_levels(splits[3], (NZ, NY, NX), ((0, 4), (1, 4), (2, 16)), -0.2, 0.2)), 0.02, 0.2)
    disk_cells = draw_disk_cells(jax.random.fold_in(splits[11], 71), 0)
    disk_turbine = draw_disk_turbine(jax.random.fold_in(splits[11], 71), 0)
    disk_weight = jnp.clip(jnp.exp(math.log(0.03) - 1.0986123 * jax.random.uniform(splits[6], (ENTRIES,), jnp.float32) ** block_levels(splits[6], (ENTRIES,), ((0, 256),), -0.2, 0.2)), 0.01, 0.03)
    disk_dweight = bell_draw(splits[7], (2, ENTRIES), 0.05, 0.75, ((1, 256),), jnp.float32)
    yaw = jnp.clip(jax.random.uniform(splits[8], (TURBINES,), jnp.float32, -0.5, 0.5) * block_levels(splits[8], (TURBINES,), ((0, 256),), -0.4, 0.0), -0.5, 0.5)
    thrust_coef = jnp.clip(0.6 + 0.29999995 * jax.random.uniform(splits[9], (TURBINES,), jnp.float32) ** block_levels(splits[9], (TURBINES,), ((0, 256),), -0.2, 0.2), 0.6, 0.9)
    owner_slot = jax.random.permutation(splits[10], TURBINES).astype(jnp.int32)
    return dict(velocity=velocity, adjoint=adjoint, pressure=pressure, viscosity=viscosity, disk_cells=disk_cells, disk_turbine=disk_turbine, disk_weight=disk_weight, disk_dweight=disk_dweight, yaw=yaw, thrust_coef=thrust_coef, owner_slot=owner_slot)


DT = 0.2


def pad3(field):
    return jnp.pad(field, [(0, 0)] * (field.ndim - 3) + [(1, 1)] * 3)


def inner(padded):
    return padded[..., 1:-1, 1:-1, 1:-1]


def neighbour_sum(padded):
    total = padded[..., 2:, 1:-1, 1:-1] + padded[..., :-2, 1:-1, 1:-1]
    total = total + padded[..., 1:-1, 2:, 1:-1] + padded[..., 1:-1, :-2, 1:-1]
    return total + padded[..., 1:-1, 1:-1, 2:] + padded[..., 1:-1, 1:-1, :-2]


def advance(padded_flow, padded_dual, viscosity, force, source):
    centre = inner(padded_flow)
    lap_flow = neighbour_sum(padded_flow) - 6.0 * centre
    upwind = centre - padded_flow[:, 1:-1, 1:-1, :-2]
    predicted = centre + DT * (viscosity * lap_flow - upwind + force)
    dual = inner(padded_dual)
    lap_dual = neighbour_sum(padded_dual) - 6.0 * dual
    downwind = padded_dual[:, 1:-1, 1:-1, 2:] - dual
    return predicted, dual + DT * (viscosity * lap_dual + downwind + source)


def divergence(padded):
    total = padded[0, 1:-1, 1:-1, 2:] - padded[0, 1:-1, 1:-1, :-2]
    total = total + padded[1, 1:-1, 2:, 1:-1] - padded[1, 1:-1, :-2, 1:-1]
    total = total + padded[2, 2:, 1:-1, 1:-1] - padded[2, :-2, 1:-1, 1:-1]
    return 0.5 * total


def gradient(padded):
    return 0.5 * jnp.stack([padded[1:-1, 1:-1, 2:] - padded[1:-1, 1:-1, :-2],
                            padded[1:-1, 2:, 1:-1] - padded[1:-1, :-2, 1:-1],
                            padded[2:, 1:-1, 1:-1] - padded[:-2, 1:-1, 1:-1]])


def turbine_terms(inflow, yaw, thrust_coef):
    speed, dual_x, dual_y = inflow[0], inflow[1], inflow[2]
    cosine = jnp.cos(yaw)
    sine = jnp.sin(yaw)
    magnitude = jnp.abs(speed)
    force = 0.5 * thrust_coef * speed * magnitude * cosine * cosine
    weighting = 1.5 * thrust_coef * speed * magnitude * cosine ** 3
    yaw_grad = -1.5 * thrust_coef * magnitude ** 3 * cosine * cosine * sine + force * (sine * dual_x - cosine * dual_y)
    return force * cosine, force * sine, weighting, yaw_grad


def reference(velocity, adjoint, pressure, viscosity, disk_cells, disk_turbine, disk_weight, disk_dweight, yaw, thrust_coef, owner_slot):
    device = jnp.arange(ENTRIES, dtype=jnp.int32) // DISK_DEV
    block_x = device // (N_GY * N_GZ)
    block_y = (device // N_GZ) % N_GY
    block_z = device % N_GZ
    cell_k = disk_cells // (CY * CX)
    cell_j = (disk_cells // CX) % CY
    cell_i = disk_cells % CX
    global_cell = ((block_z * CZ + cell_k) * NY + block_y * CY + cell_j) * NX + block_x * CX + cell_i
    global_cell = global_cell.astype(jnp.int32)
    slots = owner_slot[disk_turbine]
    flow_flat = velocity.reshape(3, -1)
    dual_flat = adjoint.reshape(3, -1)
    flow_x = flow_flat[0, global_cell]
    dual_x = dual_flat[0, global_cell]
    dual_y = dual_flat[1, global_cell]
    values = disk_weight[:, None] * jnp.stack([flow_x, dual_x, dual_y], 1)
    inflow = jax.ops.segment_sum(values, slots, TURBINES).T
    force_cos, force_sin, weighting, yaw_grad = turbine_terms(inflow, yaw, thrust_coef)
    cells = NX * NY * NZ
    empty = jnp.zeros((cells,), jnp.float32)
    force_x = empty.at[global_cell].add(-disk_weight * force_cos[slots])
    force_y = empty.at[global_cell].add(-disk_weight * force_sin[slots])
    source_x = empty.at[global_cell].add(disk_weight * weighting[slots])
    force = jnp.stack([force_x, force_y, empty]).reshape(3, NZ, NY, NX)
    source = jnp.stack([source_x, empty, empty]).reshape(3, NZ, NY, NX)
    entry_term = weighting[slots] * flow_x - force_cos[slots] * dual_x - force_sin[slots] * dual_y
    position_grad = jax.ops.segment_sum((disk_dweight * entry_term[None]).T, slots, TURBINES).T
    predicted, adjoint_next = advance(pad3(velocity), pad3(adjoint), viscosity, force, source)
    div = divergence(pad3(predicted))
    phi = -div / (6.0 * DT)
    for sweep in range(SWEEPS - 1):
        phi = (neighbour_sum(pad3(phi)) - div / DT) / 6.0
    velocity_next = predicted - DT * gradient(pad3(phi))
    return velocity_next, adjoint_next, pressure + phi, yaw_grad, position_grad
```

```python
import functools

import jax
import jax.numpy as jnp
from jax import lax
from jax.experimental import pallas as pl
from jax.experimental.pallas import tpu as pltpu
from jax.sharding import PartitionSpec as P

SWEEPS = 8
DT = 0.2
F32 = jnp.float32
BF16 = jnp.bfloat16
CZ, CY, CX = 16, 32, 128
KJ = CZ * CY
H = 8
EZ, EY = CZ + 2 * H, CY + 2 * H
SZ = CZ + 2
PER = 16
WIN = 64
YAW = 112
NN = (((1,), (0,)), ((), ()))
NT = (((1,), (1,)), ((), ()))
TN = (((0,), (0,)), ((), ()))


def iota(shape, dim):
    return lax.broadcasted_iota(jnp.int32, shape, dim)


def pieces(x, count):
    parts = []
    for _ in range(count):
        head = x.astype(BF16)
        parts.append(head)
        x = x - head.astype(F32)
    return parts


def dots(left, right, dims):
    total = None
    for a in left:
        for b in right:
            term = lax.dot_general(a, b, dims, preferred_element_type=F32)
            total = term if total is None else total + term
    return total


def onehot(mask):
    return jnp.where(mask, 1.0, 0.0).astype(BF16)


def roll(x, shift, axis):
    return pltpu.roll(x, shift % x.shape[axis], axis)


def entry_onehots(cells):
    row = lax.shift_right_logical(cells, 7)
    lane = jnp.bitwise_and(cells, CX - 1)
    count = cells.shape[1]
    rows = onehot(iota((KJ, count), 0) == row)
    lanes = iota((CX, count), 0) == lane
    return rows, lanes


def window_lane(turbine, bx, n_gy):
    column_x = lax.shift_right_logical(turbine, 4) // n_gy
    return WIN + (column_x - bx + 1) * PER + jnp.bitwise_and(turbine, PER - 1)


def lookup(table_ref, turbine):
    count = turbine.shape[1]
    table = table_ref[...]
    owner = lax.shift_right_logical(table, 2).astype(F32)
    which = jnp.bitwise_and(table, 3).astype(F32)
    rows = table.shape[0]
    high = lax.shift_right_logical(turbine, 7)
    low = onehot(iota((CX, count), 0) == jnp.bitwise_and(turbine, CX - 1))
    keep = iota((rows, count), 0) == high
    out = []
    for part in (owner, which):
        picked = dots([part.astype(BF16)], [low], NN)
        picked = jnp.sum(jnp.where(keep, picked, 0.0), axis=0, keepdims=True)
        out.append(picked.astype(jnp.int32))
    return out


def entry_kernel(
    n_dev, n_gy, pos_ref, yaw_ref, ct_ref, vel_ref, adj_ref, cells_ref, turb_ref, weight_ref, dweight_ref, owner_ref,
    pay_ref, xr_ref, xl_ref, yr_ref, yl_ref, zr_ref, zl_ref,
):
    bx = pos_ref[0]
    cells, turbine, weight = cells_ref[...], turb_ref[...], weight_ref[...]
    count = cells.shape[1]
    rows, lanes = entry_onehots(cells)

    gathered = []
    for ref, comp in ((vel_ref, 0), (adj_ref, 0), (adj_ref, 1)):
        field = pieces(ref[comp].reshape(KJ, CX), 2)
        at_row = dots(field, [rows], TN)
        gathered.append(jnp.sum(jnp.where(lanes, at_row, 0.0), axis=0, keepdims=True))
    factors = [weight, dweight_ref[0:1, :], dweight_ref[1:2, :]]
    values = [f * g for f in factors for g in gathered]

    sub = iota((PER, count), 0)
    stacked = jnp.zeros((PER, count), F32)
    for v, value in enumerate(values):
        stacked = jnp.where(sub == v, value, stacked)
    owner, which = lookup(owner_ref, turbine)
    per_slot = jnp.concatenate(
        [jnp.where(which == i, stacked, 0.0) for i in range(4)] + [jnp.zeros((CX - 4 * PER, count), F32)], axis=0
    )
    to_owner = onehot(iota((n_dev, count), 0) == owner)
    payload = dots([to_owner], pieces(per_slot, 3), NT)

    in_window = onehot(iota((CX, count), 0) == window_lane(turbine, bx, n_gy))
    speed = jnp.broadcast_to(values[0], (8, count))
    shared = dots(pieces(speed, 3), [in_window], NT)[0:1, :]
    lane = iota((1, CX), 1)
    for i in range(4):
        shared = jnp.where(lane == YAW + i, yaw_ref[i], shared)
        shared = jnp.where(lane == YAW + 4 + i, ct_ref[i], shared)
    pay_ref[...] = payload + shared

    lane = iota((CY, CX), 1)
    right = jnp.zeros((CY, CX), F32)
    left = jnp.zeros((CY, CX), F32)
    for f in range(6):
        ref, comp = (vel_ref, f) if f < 3 else (adj_ref, f - 3)

        def body(z, carry, ref=ref, comp=comp, f=f):
            right, left = carry
            plane = ref[comp, z]
            at = f * CZ + z
            right = jnp.where(lane == at, pltpu.roll(plane, at + 1, 1), right)
            left = jnp.where(lane == at, pltpu.roll(plane, at, 1), left)
            return right, left

        right, left = lax.fori_loop(0, CZ, body, (right, left), unroll=4)
        yr_ref[f * CZ:(f + 1) * CZ, :] = ref[comp, :, CY - 1, :]
        yl_ref[f * CZ:(f + 1) * CZ, :] = ref[comp, :, 0, :]
        zr_ref[f] = ref[comp, CZ - 1]
        zl_ref[f] = ref[comp, 0]
    xr_ref[...] = right
    xl_ref[...] = left


def turbine_terms(speed, yaw, thrust_coef):
    cosine = jnp.cos(yaw)
    sine = jnp.sin(yaw)
    magnitude = jnp.abs(speed)
    force = 0.5 * thrust_coef * speed * magnitude * cosine * cosine
    weighting = 1.5 * thrust_coef * speed * magnitude * cosine * cosine * cosine
    return cosine, sine, magnitude, force, weighting


def owner_outputs(got, yaw_ref, ct_ref, yaw_out, pos_out):
    total = jnp.sum(got, axis=0, keepdims=True)
    total = jnp.broadcast_to(total, (8, CX))
    lane = iota((8, CX), 1)
    yaw = jnp.zeros((8, CX), F32)
    ct = jnp.zeros((8, CX), F32)
    for i in range(4):
        yaw = jnp.where(lane == i * PER, yaw_ref[i], yaw)
        ct = jnp.where(lane == i * PER, ct_ref[i], ct)

    def at(v):
        return roll(total, -v, 1)

    speed, dual_x, dual_y = total, at(1), at(2)
    cosine, sine, magnitude, force, weighting = turbine_terms(speed, yaw, ct)
    yaw_grad = -1.5 * ct * magnitude * magnitude * magnitude * cosine * cosine * sine + force * (
        sine * dual_x - cosine * dual_y
    )
    grads = [yaw_grad]
    for r in range(2):
        grads.append(weighting * at(3 + 3 * r) - force * cosine * at(4 + 3 * r) - force * sine * at(5 + 3 * r))
    packed = []
    for grad in grads:
        out = jnp.zeros((8, CX), F32)
        for i in range(4):
            out = jnp.where(lane == i, roll(grad, -(PER - 1) * i, 1), out)
        packed.append(out)
    yaw_out[...] = packed[0][0:1, 0:4]
    pos_out[0:1, :] = packed[1][0:1, 0:4]
    pos_out[1:2, :] = packed[2][0:1, 0:4]


def window_terms(got, n_dev, n_gx, n_gy, n_gz, bx, by, owner_ref):
    lane = iota((1, CX), 1)
    inside = jnp.logical_and(lane >= WIN, lane < WIN + 3 * PER)
    row = iota((n_dev, CX), 0)
    speed = jnp.zeros((1, CX), F32)
    for delta in range(-2, 3):
        base = ((bx + delta) * n_gy + by) * n_gz
        keep = jnp.logical_and(row >= base, row < base + n_gz)
        part = jnp.sum(jnp.where(keep, got, 0.0), axis=0, keepdims=True)
        part = jnp.broadcast_to(jnp.where(inside, part, 0.0), (8, CX))
        speed = speed + roll(part, delta * PER, 1)[0:1, :]
    speed = jnp.where(inside, speed, 0.0)

    table = owner_ref[...]
    sub = iota(table.shape, 0)
    slots = jnp.zeros((1, CX), jnp.int32)
    for j in range(3):
        column_x = jnp.clip(bx - 1 + j, 0, n_gx - 1)
        first = (column_x * n_gy + by) * PER
        picked = jnp.sum(jnp.where(sub == first // CX, table, 0), axis=0, keepdims=True)
        picked = jnp.broadcast_to(picked, (8, CX))
        moved = pltpu.roll(picked, jnp.bitwise_and(WIN + PER * j - first, CX - 1), 1)[0:1, :]
        here = jnp.logical_and(lane >= WIN + PER * j, lane < WIN + PER * (j + 1))
        slots = jnp.where(here, moved, slots)
    owner = onehot(iota((n_dev, CX), 0) == lax.shift_right_logical(slots, 2))
    which = jnp.bitwise_and(slots, 3)
    found = dots(pieces(got, 3), [owner], TN)
    yaw = jnp.zeros((1, CX), F32)
    ct = jnp.zeros((1, CX), F32)
    for i in range(4):
        yaw = jnp.where(which == i, found[YAW + i:YAW + i + 1, :], yaw)
        ct = jnp.where(which == i, found[YAW + 4 + i:YAW + 5 + i, :], ct)
    cosine, sine, magnitude, force, weighting = turbine_terms(speed, yaw, ct)
    keep = lambda x: jnp.where(inside, x, 0.0)
    return keep(force * cosine), keep(force * sine), keep(weighting)


def flow_kernel(
    dims, pos_ref, yaw_ref, ct_ref, vel_ref, adj_ref, visc_ref, cells_ref, turb_ref, weight_ref, owner_ref, got_ref,
    xlo_ref, xhi_ref, ylo_ref, yhi_ref, zlo_ref, zhi_ref,
    pred_ref, dual_ref, yaw_out, pos_out, dm_ref, ds_ref, xr_ref, xl_ref,
    field_ref,
):
    n_dev, n_gx, n_gy, n_gz = dims
    bx, by, bz = pos_ref[0], pos_ref[1], pos_ref[2]
    got = got_ref[...]
    owner_outputs(got, yaw_ref, ct_ref, yaw_out, pos_out)
    terms = window_terms(got, n_dev, n_gx, n_gy, n_gz, bx, by, owner_ref)

    cells, turbine, weight = cells_ref[...], turb_ref[...], weight_ref[...]
    count = cells.shape[1]
    rows, lanes = entry_onehots(cells)
    in_window = onehot(iota((CX, count), 0) == window_lane(turbine, bx, n_gy))
    stacked = jnp.concatenate([jnp.broadcast_to(t, (8, CX)) for t in terms], axis=0)
    per_entry = dots(pieces(stacked, 3), [in_window], NN)
    for c in range(3):
        value = per_entry[8 * c:8 * c + 1, :] * weight
        if c < 2:
            value = -value
        spread = jnp.where(lanes, value, 0.0)
        field_ref[c] = dots([rows], pieces(spread, 2), NT).reshape(CZ, CY, CX)

    in_lo_x = jnp.where(bx > 0, 1.0, 0.0)
    in_hi_x = jnp.where(bx < n_gx - 1, 1.0, 0.0)
    in_lo_y = jnp.where(by > 0, 1.0, 0.0)
    in_hi_y = jnp.where(by < n_gy - 1, 1.0, 0.0)
    in_lo_z = jnp.where(bz > 0, 1.0, 0.0)
    in_hi_z = jnp.where(bz < n_gz - 1, 1.0, 0.0)
    lane = iota((CY, CX), 1)
    sub = iota((CY, CX), 0)
    face_lo = xlo_ref[...] * in_lo_x
    face_hi = xhi_ref[...] * in_hi_x
    for f in range(6):
        ref, comp = (vel_ref, f) if f < 3 else (adj_ref, f - 3)
        out = pred_ref if f < 3 else dual_ref

        def body(z, carry, ref=ref, out=out, comp=comp, f=f):
            plane = ref[comp, z]
            below = jnp.where(z > 0, ref[comp, jnp.maximum(z - 1, 0)], zlo_ref[f] * in_lo_z)
            above = jnp.where(z < CZ - 1, ref[comp, jnp.minimum(z + 1, CZ - 1)], zhi_ref[f] * in_hi_z)
            at = f * CZ + z
            row_lo = ylo_ref[pl.ds(at, 1), :] * in_lo_y
            row_hi = yhi_ref[pl.ds(at, 1), :] * in_hi_y
            south = jnp.where(sub == 0, row_lo, roll(plane, 1, 0))
            north = jnp.where(sub == CY - 1, row_hi, roll(plane, -1, 0))
            west = jnp.where(lane == 0, pltpu.roll(face_lo, jnp.bitwise_and(CX - at, CX - 1), 1), roll(plane, 1, 1))
            east = jnp.where(lane == CX - 1, pltpu.roll(face_hi, CX - 1 - at, 1), roll(plane, -1, 1))
            lap = above + below + north + south + east + west - 6.0 * plane
            rate = visc_ref[z] * lap
            if f < 3:
                rate = rate - (plane - west)
                if f < 2:
                    rate = rate + field_ref[f, z]
            else:
                rate = rate + (east - plane)
                if f == 3:
                    rate = rate + field_ref[2, z]
            out[comp, z] = plane + DT * rate
            return carry

        lax.fori_loop(0, CZ, body, 0, unroll=2)

    zero = jnp.zeros((H, CX), F32)
    edge_hi = iota((H, CX), 0) == H - 1
    edge_lo = iota((H, CX), 0) == 0

    def div_body(z, carry):
        p0, p1 = pred_ref[0, z], pred_ref[1, z]
        up = jnp.where(z < CZ - 1, pred_ref[2, jnp.minimum(z + 1, CZ - 1)], 0.0)
        down = jnp.where(z > 0, pred_ref[2, jnp.maximum(z - 1, 0)], 0.0)
        west, east = roll(p0, 1, 1), roll(p0, -1, 1)
        div = jnp.where(lane == CX - 1, 0.0, east) - jnp.where(lane == 0, 0.0, west)
        north = jnp.where(sub == CY - 1, 0.0, roll(p1, -1, 0))
        south = jnp.where(sub == 0, 0.0, roll(p1, 1, 0))
        div = 0.5 * (div + north - south + up - down)
        dm_ref[z + 1, 0:H] = jnp.where(edge_hi, 0.5 * p1[0:1, :], 0.0)
        dm_ref[z + 1, H:H + CY] = div
        dm_ref[z + 1, H + CY:EY] = jnp.where(edge_lo, -0.5 * p1[CY - 1:CY, :], 0.0)
        side = jnp.where(lane == CX - 1, 0.5 * east, jnp.where(lane == 0, -0.5 * west, 0.0))
        ds_ref[z + 1, 0:H] = zero
        ds_ref[z + 1, H:H + CY] = side
        ds_ref[z + 1, H + CY:EY] = zero
        return carry

    lax.fori_loop(0, CZ, div_body, 0, unroll=2)
    for index, value in ((0, 0.5 * pred_ref[2, 0]), (SZ - 1, -0.5 * pred_ref[2, CZ - 1])):
        dm_ref[index, 0:H] = zero
        dm_ref[index, H:H + CY] = value
        dm_ref[index, H + CY:EY] = zero
        ds_ref[index] = jnp.zeros((EY, CX), F32)

    wide = iota((EY, CX), 1)
    for tile in range(3):
        xr_ref[tile] = jnp.zeros((EY, CX), F32)
        xl_ref[tile] = jnp.zeros((EY, CX), F32)

    def pack_body(z, carry):
        tile = lax.shift_right_logical(z, 3)
        group = jnp.bitwise_and(z, 7)
        main, side = dm_ref[z], ds_ref[z]
        mine = lax.shift_right_logical(wide, 4) == group
        shift = jnp.bitwise_and(H + 16 * group, CX - 1)
        right = pltpu.roll(jnp.where(wide < H, side, main), shift, 1)
        left = pltpu.roll(jnp.where(wide < H, main, side), shift, 1)
        xr_ref[tile] = jnp.where(mine, right, xr_ref[tile])
        xl_ref[tile] = jnp.where(mine, left, xl_ref[tile])
        return carry

    lax.fori_loop(0, SZ, pack_body, 0, unroll=2)


def x_kernel(dims, pos_ref, dm_ref, ds_ref, lo_ref, hi_ref, om_ref, os_ref, up_ref, down_ref):
    n_dev, n_gx, n_gy, n_gz = dims
    bx = pos_ref[0]
    in_lo = jnp.where(bx > 0, 1.0, 0.0)
    in_hi = jnp.where(bx < n_gx - 1, 1.0, 0.0)
    lane = iota((EY, CX), 1)
    head, tail = lane < H, lane >= CX - H
    row = iota((H, CX), 1)
    for k in (18, 19, 20, 21, 22, 23, 24, 25, 26):
        up_ref[k] = jnp.zeros((H, CX), F32)
        down_ref[k] = jnp.zeros((H, CX), F32)

    def body(z, carry):
        tile = lax.shift_right_logical(z, 3)
        group = jnp.bitwise_and(z, 7)
        shift = jnp.bitwise_and(CX - H - 16 * group, CX - 1)
        lo = pltpu.roll(lo_ref[tile] * in_lo, shift, 1)
        hi = pltpu.roll(hi_ref[tile] * in_hi, shift, 1)
        main = dm_ref[z] + jnp.where(head, lo, jnp.where(tail, hi, 0.0))
        side = ds_ref[z] + jnp.where(tail, lo, jnp.where(head, hi, 0.0))
        om_ref[z] = main
        os_ref[z] = side
        up_ref[z] = main[CY:CY + H]
        down_ref[z] = main[H:2 * H]
        mine = lax.shift_right_logical(row, 4) == group
        fold = jnp.bitwise_and(H + 16 * group, CX - 1)
        up_ref[21 + tile] = jnp.where(mine, pltpu.roll(side[CY:CY + H], fold, 1), up_ref[21 + tile])
        down_ref[21 + tile] = jnp.where(mine, pltpu.roll(side[H:2 * H], fold, 1), down_ref[21 + tile])
        up_ref[18 + tile, pl.ds(group, 1), :] = main[H + CY:H + CY + 1]
        up_ref[24 + tile, pl.ds(group, 1), :] = side[H + CY:H + CY + 1]
        down_ref[18 + tile, pl.ds(group, 1), :] = main[H - 1:H]
        down_ref[24 + tile, pl.ds(group, 1), :] = side[H - 1:H]
        return carry

    lax.fori_loop(0, SZ, body, 0, unroll=2)


def y_kernel(dims, pos_ref, dm_ref, ds_ref, lo_ref, hi_ref, om_ref, os_ref, up_ref, down_ref):
    n_dev, n_gx, n_gy, n_gz = dims
    by = pos_ref[1]
    in_lo = jnp.where(by > 0, 1.0, 0.0)
    in_hi = jnp.where(by < n_gy - 1, 1.0, 0.0)
    lane = iota((H, CX), 1)
    sub = iota((H, CX), 0)
    ends = jnp.logical_or(lane < H, lane >= CX - H)

    def body(z, carry):
        tile = lax.shift_right_logical(z, 3)
        group = jnp.bitwise_and(z, 7)
        shift = jnp.bitwise_and(CX - H - 16 * group, CX - 1)
        main, side = dm_ref[z], ds_ref[z]
        lo_side = jnp.where(ends, pltpu.roll(lo_ref[21 + tile] * in_lo, shift, 1), 0.0)
        hi_side = jnp.where(ends, pltpu.roll(hi_ref[21 + tile] * in_hi, shift, 1), 0.0)
        lo_row = lo_ref[18 + tile, pl.ds(group, 1), :] * in_lo
        hi_row = hi_ref[18 + tile, pl.ds(group, 1), :] * in_hi
        lo_srow = lo_ref[24 + tile, pl.ds(group, 1), :] * in_lo
        hi_srow = hi_ref[24 + tile, pl.ds(group, 1), :] * in_hi
        for given, out, first, last, row_lo, row_hi in (
            (main, om_ref, lo_ref[z] * in_lo, hi_ref[z] * in_hi, lo_row, hi_row),
            (side, os_ref, lo_side, hi_side, lo_srow, hi_srow),
        ):
            out[z, 0:H] = given[0:H] + first
            out[z, H:2 * H] = given[H:2 * H] + jnp.where(sub == 0, row_lo, 0.0)
            out[z, 2 * H:CY] = given[2 * H:CY]
            out[z, CY:CY + H] = given[CY:CY + H] + jnp.where(sub == H - 1, row_hi, 0.0)
            out[z, CY + H:EY] = given[CY + H:EY] + last
        return carry

    lax.fori_loop(0, SZ, body, 0, unroll=2)

    wide = iota((EY, CX), 1)
    folded_up = jnp.where(wide >= 112, roll(os_ref[SZ - 1], 120, 1), 0.0)
    folded_down = jnp.where(wide >= 112, roll(os_ref[0], 120, 1), 0.0)
    up_ref[H] = om_ref[SZ - 1]
    down_ref[H] = om_ref[0]
    for g in range(8):
        up_ref[g] = om_ref[CZ - H + 1 + g]
        down_ref[g] = om_ref[1 + g]
        mine = jnp.logical_and(wide >= 14 * g, wide < 14 * (g + 1))
        folded_up = jnp.where(mine, roll(os_ref[CZ - H + 1 + g], 14 * g + 7, 1), folded_up)
        folded_down = jnp.where(mine, roll(os_ref[1 + g], 14 * g + 7, 1), folded_down)
    up_ref[H + 1] = folded_up
    down_ref[H + 1] = folded_down


def sweep_kernel(dims, pos_ref, dm_ref, ds_ref, lo_ref, hi_ref, pred_ref, pres_ref, vel_out, pres_out, b_ref, phi_ref):
    n_dev, n_gx, n_gy, n_gz = dims
    bx, by, bz = pos_ref[0], pos_ref[1], pos_ref[2]
    in_lo_z = jnp.where(bz > 0, 1.0, 0.0)
    in_hi_z = jnp.where(bz < n_gz - 1, 1.0, 0.0)
    scale = 1.0 / DT
    lane = iota((EY, CX), 1)
    sub = iota((EY, CX), 0)
    first, last = lane == 0, lane == CX - 1
    outside = jnp.logical_or(
        jnp.logical_and(sub < H, by == 0), jnp.logical_and(sub >= H + CY, by == n_gy - 1)
    )
    side_out = jnp.logical_or(
        jnp.logical_and(lane >= CX - H, bx == 0), jnp.logical_and(lane < H, bx == n_gx - 1)
    )
    coef = jnp.where(outside, 0.0, 1.0 / 6.0)
    side_coef = jnp.where(side_out, 0.0, coef)

    for g in range(H):
        b_ref[0, g] = lo_ref[g] * (in_lo_z * scale)
        b_ref[0, H + CZ + g] = hi_ref[g] * (in_hi_z * scale)
        keep = jnp.logical_or(lane < 7, lane >= CX - 7)
        lo = jnp.where(keep, roll(lo_ref[H + 1], -(14 * g + 7), 1), 0.0)
        hi = jnp.where(keep, roll(hi_ref[H + 1], -(14 * g + 7), 1), 0.0)
        b_ref[1, g] = lo * (in_lo_z * scale)
        b_ref[1, H + CZ + g] = hi * (in_hi_z * scale)

    def own_body(z, carry):
        b_ref[0, z + H] = dm_ref[z + 1] * scale
        b_ref[1, z + H] = ds_ref[z + 1] * scale
        return carry

    lax.fori_loop(0, CZ, own_body, 0)
    keep = jnp.logical_or(lane < H, lane >= CX - H)
    lo_side = jnp.where(keep, roll(lo_ref[H + 1], -120, 1), 0.0)
    hi_side = jnp.where(keep, roll(hi_ref[H + 1], -120, 1), 0.0)
    b_ref[0, H - 1] = b_ref[0, H - 1] + dm_ref[0] * (in_lo_z * scale)
    b_ref[1, H - 1] = b_ref[1, H - 1] + ds_ref[0] * (in_lo_z * scale)
    b_ref[0, H + CZ] = b_ref[0, H + CZ] + dm_ref[SZ - 1] * (in_hi_z * scale)
    b_ref[1, H + CZ] = b_ref[1, H + CZ] + ds_ref[SZ - 1] * (in_hi_z * scale)
    b_ref[0, H] = b_ref[0, H] + lo_ref[H] * (in_lo_z * scale)
    b_ref[1, H] = b_ref[1, H] + lo_side * (in_lo_z * scale)
    b_ref[0, H + CZ - 1] = b_ref[0, H + CZ - 1] + hi_ref[H] * (in_hi_z * scale)
    b_ref[1, H + CZ - 1] = b_ref[1, H + CZ - 1] + hi_side * (in_hi_z * scale)

    def start_body(z, carry):
        phi_ref[0, 0, z] = -b_ref[0, z] * coef
        phi_ref[0, 1, z] = -b_ref[1, z] * side_coef
        return carry

    lax.fori_loop(0, EZ, start_body, 0, unroll=2)

    for step in range(1, SWEEPS):
        src, dst = (step - 1) % 2, step % 2

        def body(z, carry, src=src, dst=dst):
            inside = jnp.where(z < H, in_lo_z, jnp.where(z >= H + CZ, in_hi_z, 1.0))
            main, side = phi_ref[src, 0, z], phi_ref[src, 1, z]
            main_w, side_w = roll(main, 1, 1), roll(side, 1, 1)
            main_e, side_e = roll(main, -1, 1), roll(side, -1, 1)
            total = phi_ref[src, 0, z + 1] + phi_ref[src, 0, z - 1] + roll(main, 1, 0) + roll(main, -1, 0)
            total = total + jnp.where(first, side_w, main_w) + jnp.where(last, side_e, main_e)
            phi_ref[dst, 0, z] = (total - b_ref[0, z]) * (coef * inside)
            total = phi_ref[src, 1, z + 1] + phi_ref[src, 1, z - 1] + roll(side, 1, 0) + roll(side, -1, 0)
            total = total + jnp.where(first, main_w, side_w) + jnp.where(last, main_e, side_e)
            phi_ref[dst, 1, z] = (total - b_ref[1, z]) * (side_coef * inside)
            return carry

        lax.fori_loop(step, EZ - step, body, 0)

    end = (SWEEPS - 1) % 2
    own = slice(H, H + CY)

    def final_body(z, carry):
        main, side = phi_ref[end, 0, z + H], phi_ref[end, 1, z + H]
        west = jnp.where(first, roll(side, 1, 1), roll(main, 1, 1))[own]
        east = jnp.where(last, roll(side, -1, 1), roll(main, -1, 1))[own]
        south, north = roll(main, 1, 0)[own], roll(main, -1, 0)[own]
        below, above = phi_ref[end, 0, z + H - 1][own], phi_ref[end, 0, z + H + 1][own]
        vel_out[0, z] = pred_ref[0, z] - DT * 0.5 * (east - west)
        vel_out[1, z] = pred_ref[1, z] - DT * 0.5 * (north - south)
        vel_out[2, z] = pred_ref[2, z] - DT * 0.5 * (above - below)
        pres_out[z] = pres_ref[z] + main[own]
        return carry

    lax.fori_loop(0, CZ, final_body, 0)


def swap(up, down, axis):
    count = lax.axis_size(axis)
    forward = [(i, (i + 1) % count) for i in range(count)]
    backward = [(j, i) for i, j in forward]
    return lax.ppermute(up, axis, forward), lax.ppermute(down, axis, backward)


def shape(*dims):
    return jax.ShapeDtypeStruct(dims, F32)


SMEM = pl.BlockSpec(memory_space=pltpu.SMEM)
VMEM = pl.BlockSpec(memory_space=pltpu.VMEM)


def call(kernel, scalars, arrays, outs, scratch=()):
    return pl.pallas_call(
        kernel,
        out_shape=outs,
        in_specs=[SMEM] * len(scalars) + [VMEM] * len(arrays),
        out_specs=jax.tree.map(lambda _: VMEM, outs),
        scratch_shapes=list(scratch),
        compiler_params=pltpu.CompilerParams(vmem_limit_bytes=24 * 1024 * 1024),
    )(*scalars, *arrays)


def shards(
    velocity, adjoint, pressure, viscosity, disk_cells, disk_turbine, disk_weight, disk_dweight, yaw, thrust_coef, owner_slot,
):
    axes = ("gx", "gy", "gz")
    n_gx, n_gy, n_gz = (lax.axis_size(a) for a in axes)
    n_dev = n_gx * n_gy * n_gz
    dims = (n_dev, n_gx, n_gy, n_gz)
    pos = jnp.stack([lax.axis_index(a) for a in axes]).astype(jnp.int32)
    turbines = owner_slot.shape[0]
    if turbines % CX:
        owner_slot = jnp.pad(owner_slot, (0, CX - turbines % CX))
    owner = owner_slot.reshape(-1, CX)
    cells, turbine, weight = (a.reshape(1, -1) for a in (disk_cells, disk_turbine, disk_weight))

    payload, xr, xl, yr, yl, zr, zl = call(
        functools.partial(entry_kernel, n_dev, n_gy),
        (pos, yaw, thrust_coef),
        (velocity, adjoint, cells, turbine, weight, disk_dweight, owner),
        (
            shape(n_dev, CX), shape(CY, CX), shape(CY, CX), shape(6 * CZ, CX), shape(6 * CZ, CX),
            shape(6, CY, CX), shape(6, CY, CX),
        ),
    )
    xlo, xhi = swap(xr, xl, "gx")
    ylo, yhi = swap(yr, yl, "gy")
    zlo, zhi = swap(zr, zl, "gz")
    got = lax.all_to_all(payload, axes, 0, 0, tiled=True)

    predicted, adjoint_next, yaw_grad, position_grad, dm, ds, xr, xl = call(
        functools.partial(flow_kernel, dims),
        (pos, yaw, thrust_coef),
        (velocity, adjoint, viscosity, cells, turbine, weight, owner, got, xlo, xhi, ylo, yhi, zlo, zhi),
        (
            shape(3, CZ, CY, CX), shape(3, CZ, CY, CX), shape(1, 4), shape(2, 4), shape(SZ, EY, CX), shape(SZ, EY, CX),
            shape(3, EY, CX), shape(3, EY, CX),
        ),
        (pltpu.VMEM((3, CZ, CY, CX), F32),),
    )
    lo, hi = swap(xr, xl, "gx")
    dm, ds, up, down = call(
        functools.partial(x_kernel, dims), (pos,), (dm, ds, lo, hi),
        (shape(SZ, EY, CX), shape(SZ, EY, CX), shape(27, H, CX), shape(27, H, CX)),
    )
    lo, hi = swap(up, down, "gy")
    dm, ds, up, down = call(
        functools.partial(y_kernel, dims), (pos,), (dm, ds, lo, hi),
        (shape(SZ, EY, CX), shape(SZ, EY, CX), shape(H + 2, EY, CX), shape(H + 2, EY, CX)),
    )
    lo, hi = swap(up, down, "gz")
    velocity_next, pressure_next = call(
        functools.partial(sweep_kernel, dims), (pos,), (dm, ds, lo, hi, predicted, pressure),
        (shape(3, CZ, CY, CX), shape(CZ, CY, CX)),
        (pltpu.VMEM((2, EZ, EY, CX), F32), pltpu.VMEM((2, 2, EZ, EY, CX), F32)),
    )
    return velocity_next, adjoint_next, pressure_next, yaw_grad.reshape(-1), position_grad


def solution(mesh):
    axes = ("gx", "gy", "gz")
    grid = P(None, "gz", "gy", "gx")
    cell = P("gz", "gy", "gx")
    flat = P(axes)
    return jax.shard_map(
        shards,
        mesh=mesh,
        in_specs=(grid, grid, cell, cell, flat, flat, flat, P(None, axes), flat, flat, P()),
        out_specs=(grid, grid, cell, flat, P(None, axes)),
        check_vma=False,
    )
```

```python
import functools

import jax
import jax.numpy as jnp
from jax import lax
from jax.experimental import pallas as pl
from jax.experimental.pallas import tpu as pltpu
from jax.sharding import PartitionSpec as P

SWEEPS = 8
DT = 0.2
F32 = jnp.float32
BF16 = jnp.bfloat16
CZ, CY, CX = 16, 32, 128
KJ = CZ * CY
H = 8
EZ, EY = CZ + 2 * H, CY + 2 * H
SZ = CZ + 2
TILES = EY // H
PADR = 8
PER = 16
WIN = 64
YAW = 112
NN = (((1,), (0,)), ((), ()))
NT = (((1,), (1,)), ((), ()))
TN = (((0,), (0,)), ((), ()))


def iota(shape, dim):
    return lax.broadcasted_iota(jnp.int32, shape, dim)


def pieces(x, count):
    parts = []
    for _ in range(count):
        head = x.astype(BF16)
        parts.append(head)
        x = x - head.astype(F32)
    return parts


def dots(left, right, dims):
    total = None
    for a in left:
        for b in right:
            term = lax.dot_general(a, b, dims, preferred_element_type=F32)
            total = term if total is None else total + term
    return total


def onehot(mask):
    return jnp.where(mask, 1.0, 0.0).astype(BF16)


def roll(x, shift, axis):
    return pltpu.roll(x, shift % x.shape[axis], axis)


def entry_onehots(cells):
    row = lax.shift_right_logical(cells, 7)
    lane = jnp.bitwise_and(cells, CX - 1)
    count = cells.shape[1]
    rows = onehot(iota((KJ, count), 0) == row)
    lanes = iota((CX, count), 0) == lane
    return rows, lanes


def window_lane(turbine, bx, n_gy):
    column_x = lax.shift_right_logical(turbine, 4) // n_gy
    return WIN + (column_x - bx + 1) * PER + jnp.bitwise_and(turbine, PER - 1)


def lookup(table_ref, turbine):
    count = turbine.shape[1]
    table = table_ref[...]
    owner = lax.shift_right_logical(table, 2).astype(F32)
    which = jnp.bitwise_and(table, 3).astype(F32)
    rows = table.shape[0]
    high = lax.shift_right_logical(turbine, 7)
    low = onehot(iota((CX, count), 0) == jnp.bitwise_and(turbine, CX - 1))
    keep = iota((rows, count), 0) == high
    out = []
    for part in (owner, which):
        picked = dots([part.astype(BF16)], [low], NN)
        picked = jnp.sum(jnp.where(keep, picked, 0.0), axis=0, keepdims=True)
        out.append(picked.astype(jnp.int32))
    return out


def entry_kernel(
    n_dev, n_gy, pos_ref, yaw_ref, ct_ref, vel_hbm, adj_hbm, cells_ref, turb_ref, weight_ref, dweight_ref, owner_ref,
    pay_ref, xr_ref, xl_ref, yr_ref, yl_ref, zr_ref, zl_ref, fld_ref, sems,
):
    order = (0, 3, 4, 1, 2, 5)
    copies = {}
    for f in order:
        hbm = vel_hbm.at[f] if f < 3 else adj_hbm.at[f - 3]
        copies[f] = pltpu.make_async_copy(hbm, fld_ref.at[f], sems.at[f])
        copies[f].start()
    bx = pos_ref[0]
    cells, turbine, weight = cells_ref[...], turb_ref[...], weight_ref[...]
    count = cells.shape[1]
    rows, lanes = entry_onehots(cells)
    owner, which = lookup(owner_ref, turbine)
    to_owner = onehot(iota((n_dev, count), 0) == owner)
    in_window = onehot(iota((CX, count), 0) == window_lane(turbine, bx, n_gy))

    gathered = []
    for f in order[:3]:
        copies[f].wait()
        field = pieces(fld_ref[f].reshape(KJ, CX), 2)
        at_row = dots(field, [rows], TN)
        gathered.append(jnp.sum(jnp.where(lanes, at_row, 0.0), axis=0, keepdims=True))
    factors = [weight, dweight_ref[0:1, :], dweight_ref[1:2, :]]
    values = [f * g for f in factors for g in gathered]

    sub = iota((PER, count), 0)
    stacked = jnp.zeros((PER, count), F32)
    for v, value in enumerate(values):
        stacked = jnp.where(sub == v, value, stacked)
    per_slot = jnp.concatenate(
        [jnp.where(which == i, stacked, 0.0) for i in range(4)] + [jnp.zeros((CX - 4 * PER, count), F32)], axis=0
    )
    payload = dots([to_owner], pieces(per_slot, 2), NT)

    speed = jnp.broadcast_to(values[0], (8, count))
    shared = dots(pieces(speed, 2), [in_window], NT)[0:1, :]
    lane = iota((1, CX), 1)
    for i in range(4):
        shared = jnp.where(lane == YAW + i, yaw_ref[i], shared)
        shared = jnp.where(lane == YAW + 4 + i, ct_ref[i], shared)
    pay_ref[...] = payload + shared

    for f in order[3:]:
        copies[f].wait()
    lane = iota((H, CX), 1)
    for t in range(CY // H):
        at = slice(H * t, H * t + H)
        right = jnp.zeros((H, CX), F32)
        left = jnp.zeros((H, CX), F32)
        for f in range(6):
            for z in range(CZ):
                tile = fld_ref[f, z, at]
                spot = lane == f * CZ + z
                right = jnp.where(spot, roll(tile, f * CZ + z + 1, 1), right)
                left = jnp.where(spot, roll(tile, f * CZ + z, 1), left)
        xr_ref[at] = right
        xl_ref[at] = left
    for f in range(6):
        yr_ref[f * CZ:(f + 1) * CZ, :] = fld_ref[f, :, CY - 1, :]
        yl_ref[f * CZ:(f + 1) * CZ, :] = fld_ref[f, :, 0, :]
        zr_ref[f] = fld_ref[f, CZ - 1]
        zl_ref[f] = fld_ref[f, 0]


def turbine_terms(speed, yaw, thrust_coef):
    cosine = jnp.cos(yaw)
    sine = jnp.sin(yaw)
    magnitude = jnp.abs(speed)
    force = 0.5 * thrust_coef * speed * magnitude * cosine * cosine
    weighting = 1.5 * thrust_coef * speed * magnitude * cosine * cosine * cosine
    return cosine, sine, magnitude, force, weighting


def owner_outputs(got, yaw_ref, ct_ref, yaw_out, pos_out):
    total = jnp.sum(got, axis=0, keepdims=True)
    total = jnp.broadcast_to(total, (8, CX))
    lane = iota((8, CX), 1)
    yaw = jnp.zeros((8, CX), F32)
    ct = jnp.zeros((8, CX), F32)
    for i in range(4):
        yaw = jnp.where(lane == i * PER, yaw_ref[i], yaw)
        ct = jnp.where(lane == i * PER, ct_ref[i], ct)

    def at(v):
        return roll(total, -v, 1)

    speed, dual_x, dual_y = total, at(1), at(2)
    cosine, sine, magnitude, force, weighting = turbine_terms(speed, yaw, ct)
    yaw_grad = -1.5 * ct * magnitude * magnitude * magnitude * cosine * cosine * sine + force * (
        sine * dual_x - cosine * dual_y
    )
    grads = [yaw_grad]
    for r in range(2):
        grads.append(weighting * at(3 + 3 * r) - force * cosine * at(4 + 3 * r) - force * sine * at(5 + 3 * r))
    packed = []
    for grad in grads:
        out = jnp.zeros((8, CX), F32)
        for i in range(4):
            out = jnp.where(lane == i, roll(grad, -(PER - 1) * i, 1), out)
        packed.append(out)
    yaw_out[...] = packed[0][0:1, 0:4]
    pos_out[0:1, :] = packed[1][0:1, 0:4]
    pos_out[1:2, :] = packed[2][0:1, 0:4]


def window_terms(got, n_dev, n_gx, n_gy, n_gz, bx, by, owner_ref):
    lane = iota((1, CX), 1)
    inside = jnp.logical_and(lane >= WIN, lane < WIN + 3 * PER)
    row = iota((n_dev, CX), 0)
    speed = jnp.zeros((1, CX), F32)
    for delta in range(-2, 3):
        base = ((bx + delta) * n_gy + by) * n_gz
        keep = jnp.logical_and(row >= base, row < base + n_gz)
        part = jnp.sum(jnp.where(keep, got, 0.0), axis=0, keepdims=True)
        part = jnp.broadcast_to(jnp.where(inside, part, 0.0), (8, CX))
        speed = speed + roll(part, delta * PER, 1)[0:1, :]
    speed = jnp.where(inside, speed, 0.0)

    table = owner_ref[...]
    sub = iota(table.shape, 0)
    slots = jnp.zeros((1, CX), jnp.int32)
    for j in range(3):
        column_x = jnp.clip(bx - 1 + j, 0, n_gx - 1)
        first = (column_x * n_gy + by) * PER
        picked = jnp.sum(jnp.where(sub == first // CX, table, 0), axis=0, keepdims=True)
        picked = jnp.broadcast_to(picked, (8, CX))
        moved = pltpu.roll(picked, jnp.bitwise_and(WIN + PER * j - first, CX - 1), 1)[0:1, :]
        here = jnp.logical_and(lane >= WIN + PER * j, lane < WIN + PER * (j + 1))
        slots = jnp.where(here, moved, slots)
    owner = onehot(iota((n_dev, CX), 0) == lax.shift_right_logical(slots, 2))
    which = jnp.bitwise_and(slots, 3)
    found = dots(pieces(got, 3), [owner], TN)
    yaw = jnp.zeros((1, CX), F32)
    ct = jnp.zeros((1, CX), F32)
    for i in range(4):
        yaw = jnp.where(which == i, found[YAW + i:YAW + i + 1, :], yaw)
        ct = jnp.where(which == i, found[YAW + 4 + i:YAW + 5 + i, :], ct)
    cosine, sine, magnitude, force, weighting = turbine_terms(speed, yaw, ct)
    keep = lambda x: jnp.where(inside, x, 0.0)
    return keep(force * cosine), keep(force * sine), keep(weighting)


def edges(pos_ref, dims):
    n_dev, n_gx, n_gy, n_gz = dims
    out = []
    for k, count in enumerate((n_gx, n_gy, n_gz)):
        out.append(jnp.where(pos_ref[k] > 0, 1.0, 0.0))
        out.append(jnp.where(pos_ref[k] < count - 1, 1.0, 0.0))
    return out


def tile_rows(t):
    return slice(H * t, H * t + H)


def south_of(ref, index, t, sub):
    if t > 0:
        return ref[index + (slice(H * t - 1, H * t + H - 1),)]
    return jnp.where(sub == 0, 0.0, roll(ref[index + (tile_rows(0),)], 1, 0))


def north_of(ref, index, t, sub):
    if t < CY // H - 1:
        return ref[index + (slice(H * t + 1, H * t + H + 1),)]
    return jnp.where(sub == H - 1, 0.0, roll(ref[index + (tile_rows(t),)], -1, 0))


def base_kernel(
    dims, pos_ref, vel_ref, adj_ref, visc_ref, cells_ref, turb_ref, weight_ref, owner_ref, got_ref,
    pred_ref, dual_ref, field_ref,
):
    n_dev, n_gx, n_gy, n_gz = dims
    bx, by = pos_ref[0], pos_ref[1]
    terms = window_terms(got_ref[...], n_dev, n_gx, n_gy, n_gz, bx, by, owner_ref)
    cells, turbine, weight = cells_ref[...], turb_ref[...], weight_ref[...]
    count = cells.shape[1]
    rows, lanes = entry_onehots(cells)
    in_window = onehot(iota((CX, count), 0) == window_lane(turbine, bx, n_gy))
    stacked = jnp.concatenate([jnp.broadcast_to(t, (8, CX)) for t in terms], axis=0)
    per_entry = dots(pieces(stacked, 2), [in_window], NN)
    for c in range(3):
        value = per_entry[8 * c:8 * c + 1, :] * weight
        if c < 2:
            value = -value
        spread = jnp.where(lanes, value, 0.0)
        field_ref[c] = dots([rows], pieces(spread, 2), NT).reshape(CZ, CY, CX)

    lane = iota((H, CX), 1)
    sub = iota((H, CX), 0)
    zero = jnp.zeros((H, CX), F32)
    for t in range(CY // H):
        at = tile_rows(t)
        for f in range(6):
            ref, comp = (vel_ref, f) if f < 3 else (adj_ref, f - 3)
            out = pred_ref if f < 3 else dual_ref
            below, tile = zero, ref[comp, 0, at]
            for z in range(CZ):
                above = ref[comp, z + 1, at] if z < CZ - 1 else zero
                south, north = south_of(ref, (comp, z), t, sub), north_of(ref, (comp, z), t, sub)
                west = jnp.where(lane == 0, 0.0, roll(tile, 1, 1))
                east = jnp.where(lane == CX - 1, 0.0, roll(tile, -1, 1))
                lap = (above + below) + (north + south) + (east + west) - 6.0 * tile
                rate = visc_ref[z, at] * lap
                rate = rate + (west - tile if f < 3 else east - tile)
                if f < 2:
                    rate = rate + field_ref[f, z, at]
                if f == 3:
                    rate = rate + field_ref[2, z, at]
                out[comp, z, at] = tile + DT * rate
                below, tile = tile, above


def add_faces(f, first, out, given, visc_ref, bounds, xlo_ref, xhi_ref, ylo_ref, yhi_ref, zlo_ref, zhi_ref):
    lo_x, hi_x, lo_y, hi_y, lo_z, hi_z = bounds
    lane = iota((H, CX), 1)
    sub = iota((H, CX), 0)
    flow = f < 3
    comp = f - first
    for t in range(CY // H):
        at = tile_rows(t)
        face_lo, face_hi = xlo_ref[at] * lo_x, xhi_ref[at] * hi_x
        for z in range(CZ):
            spot = f * CZ + z
            west = jnp.where(lane == 0, roll(face_lo, -spot, 1), 0.0)
            east = jnp.where(lane == CX - 1, roll(face_hi, CX - 1 - spot, 1), 0.0)
            lap = west + east
            if t == 0:
                lap = lap + jnp.where(sub == 0, ylo_ref[spot:spot + 1, :] * lo_y, 0.0)
            if t == CY // H - 1:
                lap = lap + jnp.where(sub == H - 1, yhi_ref[spot:spot + 1, :] * hi_y, 0.0)
            if z == 0:
                lap = lap + zlo_ref[f, at] * lo_z
            if z == CZ - 1:
                lap = lap + zhi_ref[f, at] * hi_z
            out[comp, z, at] = given[comp, z, at] + DT * (visc_ref[z, at] * lap + (west if flow else east))


def fold_shift(z):
    return H + 16 * (z % 8)


def flow_kernel(
    dims, pos_ref, base_ref, visc_ref, xlo_ref, xhi_ref, ylo_ref, yhi_ref, zlo_ref, zhi_ref,
    pred_ref, dm_ref, ds_ref, xr_ref, xl_ref,
):
    bounds = edges(pos_ref, dims)
    for f in range(3):
        add_faces(f, 0, pred_ref, base_ref, visc_ref, bounds, xlo_ref, xhi_ref, ylo_ref, yhi_ref, zlo_ref, zhi_ref)
    lane = iota((H, CX), 1)
    sub = iota((H, CX), 0)
    zero = jnp.zeros((H, CX), F32)
    for r in range(EY // H):
        at = tile_rows(r)
        t = r - 1
        inside = 0 <= t < CY // H
        for k in range(SZ):
            z = k - 1
            main, side = zero, zero
            if inside and 0 <= z < CZ:
                own = tile_rows(t)
                p0 = pred_ref[0, z, own]
                west, east = roll(p0, 1, 1), roll(p0, -1, 1)
                div = jnp.where(lane == CX - 1, 0.0, east) - jnp.where(lane == 0, 0.0, west)
                div = div + (north_of(pred_ref, (1, z), t, sub) - south_of(pred_ref, (1, z), t, sub))
                if z < CZ - 1:
                    div = div + pred_ref[2, z + 1, own]
                if z > 0:
                    div = div - pred_ref[2, z - 1, own]
                main = 0.5 * div
                side = jnp.where(lane == CX - 1, 0.5 * east, jnp.where(lane == 0, -0.5 * west, 0.0))
            elif inside:
                main = 0.5 * pred_ref[2, 0, tile_rows(t)] if z < 0 else -0.5 * pred_ref[2, CZ - 1, tile_rows(t)]
            elif 0 <= z < CZ and t < 0:
                main = jnp.where(sub == H - 1, 0.5 * roll(pred_ref[1, z, 0:H], -1, 0), 0.0)
            elif 0 <= z < CZ:
                main = jnp.where(sub == 0, -0.5 * roll(pred_ref[1, z, CY - H:CY], 1, 0), 0.0)
            dm_ref[k, at] = main
            ds_ref[k, at] = side
    for r in range(EY // H):
        at = tile_rows(r)
        right, left = [zero] * 3, [zero] * 3
        for k in range(SZ):
            if not 0 < r < EY // H - 1 and not 0 < k < SZ - 1:
                continue
            main, side = dm_ref[k, at], ds_ref[k, at]
            g = k % 8
            mine = jnp.logical_and(lane >= 16 * g, lane < 16 * g + 16)
            right[k // 8] = jnp.where(mine, roll(jnp.where(lane < H, side, main), fold_shift(k), 1), right[k // 8])
            left[k // 8] = jnp.where(mine, roll(jnp.where(lane < H, main, side), fold_shift(k), 1), left[k // 8])
        for i in range(3):
            xr_ref[i, at] = right[i]
            xl_ref[i, at] = left[i]


def dual_kernel(
    dims, pos_ref, yaw_ref, ct_ref, base_ref, visc_ref, got_ref, xlo_ref, xhi_ref, ylo_ref, yhi_ref, zlo_ref, zhi_ref,
    dual_out, yaw_out, pos_out, dual_ref, sems,
):
    bounds = edges(pos_ref, dims)
    copies = []
    for f in range(3, 6):
        add_faces(f, 3, dual_ref, base_ref, visc_ref, bounds, xlo_ref, xhi_ref, ylo_ref, yhi_ref, zlo_ref, zhi_ref)
        copies.append(pltpu.make_async_copy(dual_ref.at[f - 3], dual_out.at[f - 3], sems.at[f - 3]))
        copies[-1].start()
    owner_outputs(got_ref[...], yaw_ref, ct_ref, yaw_out, pos_out)
    for copy in copies:
        copy.wait()


def x_kernel(dims, pos_ref, dm_ref, ds_ref, lo_ref, hi_ref, om_ref, os_ref, up_ref, down_ref):
    in_lo, in_hi = edges(pos_ref, dims)[0:2]
    lane = iota((H, CX), 1)
    head, tail = lane < H, lane >= CX - H
    zero = jnp.zeros((H, CX), F32)
    for r in range(EY // H):
        at = tile_rows(r)
        lows = [lo_ref[i, at] * in_lo for i in range(3)]
        highs = [hi_ref[i, at] * in_hi for i in range(3)]
        for z in range(SZ):
            lo = roll(lows[z // 8], -fold_shift(z), 1)
            hi = roll(highs[z // 8], -fold_shift(z), 1)
            om_ref[z, at] = dm_ref[z, at] + jnp.where(head, lo, jnp.where(tail, hi, 0.0))
            os_ref[z, at] = ds_ref[z, at] + jnp.where(tail, lo, jnp.where(head, hi, 0.0))
    for out, row, edge in ((up_ref, CY, H + CY), (down_ref, H, H - 1)):
        for i in range(3):
            fold = zero
            out[18 + i] = zero
            out[24 + i] = zero
            for g in range(min(8, SZ - 8 * i)):
                z = 8 * i + g
                out[z] = om_ref[z, row:row + H]
                mine = jnp.logical_and(lane >= 16 * g, lane < 16 * g + 16)
                fold = jnp.where(mine, roll(os_ref[z, row:row + H], fold_shift(z), 1), fold)
                out[18 + i, g:g + 1] = om_ref[z, edge:edge + 1]
                out[24 + i, g:g + 1] = os_ref[z, edge:edge + 1]
            out[21 + i] = fold


def y_kernel(dims, pos_ref, dm_ref, ds_ref, lo_ref, hi_ref, om_ref, os_ref, up_ref, down_ref):
    in_lo, in_hi = edges(pos_ref, dims)[2:4]
    lane = iota((H, CX), 1)
    sub = iota((H, CX), 0)
    ends = jnp.logical_or(lane < H, lane >= CX - H)
    zero = jnp.zeros((H, CX), F32)
    last = EY // H - 1
    for r in range(EY // H):
        at = tile_rows(r)
        up_fold, down_fold = zero, zero
        for z in range(SZ):
            tile, g = z // 8, z % 8
            main, side = dm_ref[z, at], ds_ref[z, at]
            if r == 0:
                main = main + lo_ref[z] * in_lo
                side = side + jnp.where(ends, roll(lo_ref[21 + tile], -fold_shift(z), 1) * in_lo, 0.0)
            if r == 1:
                main = main + jnp.where(sub == 0, lo_ref[18 + tile, g:g + 1, :] * in_lo, 0.0)
                side = side + jnp.where(sub == 0, lo_ref[24 + tile, g:g + 1, :] * in_lo, 0.0)
            if r == last - 1:
                main = main + jnp.where(sub == H - 1, hi_ref[18 + tile, g:g + 1, :] * in_hi, 0.0)
                side = side + jnp.where(sub == H - 1, hi_ref[24 + tile, g:g + 1, :] * in_hi, 0.0)
            if r == last:
                main = main + hi_ref[z] * in_hi
                side = side + jnp.where(ends, roll(hi_ref[21 + tile], -fold_shift(z), 1) * in_hi, 0.0)
            om_ref[z, at] = main
            os_ref[z, at] = side
            if z >= CZ - H + 1:
                i = z - (CZ - H + 1)
                up_ref[i, at] = main
                shift = 14 * i + 7 if i < H else 120
                mine = jnp.logical_and(lane >= 14 * i, lane < (14 * i + 14 if i < H else CX))
                up_fold = jnp.where(mine, roll(side, shift, 1), up_fold)
            if z <= H:
                i = z - 1 if z > 0 else H
                down_ref[i, at] = main
                shift = 14 * i + 7 if i < H else 120
                mine = jnp.logical_and(lane >= 14 * i, lane < (14 * i + 14 if i < H else CX))
                down_fold = jnp.where(mine, roll(side, shift, 1), down_fold)
        up_ref[H + 1, at] = up_fold
        down_ref[H + 1, at] = down_fold


def sweep_kernel(dims, pos_ref, dm_ref, ds_ref, lo_ref, hi_ref, pred_ref, pres_ref, vel_out, pres_out, b_ref, phi_ref, vel_buf, pres_buf, sems):
    n_dev, n_gx, n_gy, n_gz = dims
    bx, by, bz = pos_ref[0], pos_ref[1], pos_ref[2]
    in_lo_z = jnp.where(bz > 0, 1.0, 0.0)
    in_hi_z = jnp.where(bz < n_gz - 1, 1.0, 0.0)
    scale = 1.0 / DT
    lane = iota((H, CX), 1)
    first, last = lane == 0, lane == CX - 1
    side_in = jnp.where(jnp.logical_or(jnp.logical_and(lane >= CX - H, bx == 0), jnp.logical_and(lane < H, bx == n_gx - 1)), 0.0, 1.0)
    lo_y = jnp.where(by > 0, 1.0 / 6.0, 0.0)
    hi_y = jnp.where(by < n_gy - 1, 1.0 / 6.0, 0.0)
    full = jnp.full((H, CX), 1.0 / 6.0, F32)
    coefs = [jnp.full((H, CX), lo_y, F32)] + [full] * (TILES - 2) + [jnp.full((H, CX), hi_y, F32)]
    sides = [c * side_in for c in coefs]
    zero = jnp.zeros((H, CX), F32)
    near = jnp.logical_or(lane < 7, lane >= CX - 7)
    ends = jnp.logical_or(lane < H, lane >= CX - H)
    lo_scale, hi_scale = in_lo_z * scale, in_hi_z * scale
    for z in range(EZ):
        for part in range(2):
            for buf in range(2):
                phi_ref[buf, part, z, 0:PADR] = zero
                phi_ref[buf, part, z, PADR + EY:PADR + EY + PADR] = zero
    for t in range(TILES):
        rows = slice(8 * t, 8 * t + 8)
        out = slice(PADR + 8 * t, PADR + 8 * t + 8)
        folded = (lo_ref[H + 1, rows] * lo_scale, hi_ref[H + 1, rows] * hi_scale)
        for z in range(EZ):
            if z < H or z >= H + CZ:
                halo, g, fold, factor = (lo_ref, z, folded[0], lo_scale) if z < H else (hi_ref, z - H - CZ, folded[1], hi_scale)
                main = halo[g, rows] * factor
                side = jnp.where(near, roll(fold, -(14 * g + 7), 1), 0.0)
                if z in (H - 1, H + CZ):
                    k = 0 if z < H else SZ - 1
                    main = main + dm_ref[k, rows] * factor
                    side = side + ds_ref[k, rows] * factor
            else:
                main, side = dm_ref[z - H + 1, rows] * scale, ds_ref[z - H + 1, rows] * scale
                if z in (H, H + CZ - 1):
                    halo, fold, factor = (lo_ref, folded[0], lo_scale) if z == H else (hi_ref, folded[1], hi_scale)
                    main = main + halo[H, rows] * factor
                    side = side + jnp.where(ends, roll(fold, -120, 1), 0.0)
            b_ref[0, z, rows] = main
            b_ref[1, z, rows] = side
            phi_ref[0, 0, z, out] = -main * coefs[t]
            phi_ref[0, 1, z, out] = -side * sides[t]

    for step in range(1, SWEEPS):
        src, dst = (step - 1) % 2, step % 2
        carry = []
        for t in range(TILES):
            at = slice(PADR + 8 * t, PADR + 8 * t + 8)
            carry += [phi_ref[src, k, step - 1 + i, at] for k in range(2) for i in range(2)]
        for z in range(step, EZ - step):
            factor = in_lo_z if z < H else in_hi_z if z >= H + CZ else None
            new = []
            for t in range(TILES):
                below, main, sbelow, side = carry[4 * t:4 * t + 4]
                at = slice(PADR + 8 * t, PADR + 8 * t + 8)
                up = slice(PADR + 8 * t + 1, PADR + 8 * t + 9)
                down = slice(PADR + 8 * t - 1, PADR + 8 * t + 7)
                rows = slice(8 * t, 8 * t + 8)
                above, sabove = phi_ref[src, 0, z + 1, at], phi_ref[src, 1, z + 1, at]
                mw, sw = roll(main, 1, 1), roll(side, 1, 1)
                me, se = roll(main, -1, 1), roll(side, -1, 1)
                total = (above + below) + (phi_ref[src, 0, z, up] + phi_ref[src, 0, z, down])
                total = total + (jnp.where(first, sw, mw) + jnp.where(last, se, me))
                cm, cs = (coefs[t], sides[t]) if factor is None else (coefs[t] * factor, sides[t] * factor)
                phi_ref[dst, 0, z, at] = (total - b_ref[0, z, rows]) * cm
                total = (sabove + sbelow) + (phi_ref[src, 1, z, up] + phi_ref[src, 1, z, down])
                total = total + (jnp.where(first, mw, sw) + jnp.where(last, me, se))
                phi_ref[dst, 1, z, at] = (total - b_ref[1, z, rows]) * cs
                new += [main, above, side, sabove]
            carry = new

    end = (SWEEPS - 1) % 2
    CH = 4
    copies = []
    for c in range(CZ // CH):
        for z in range(c * CH, (c + 1) * CH):
            for t in range(CY // 8):
                at = slice(PADR + H + 8 * t, PADR + H + 8 * t + 8)
                up = slice(PADR + H + 8 * t + 1, PADR + H + 8 * t + 9)
                down = slice(PADR + H + 8 * t - 1, PADR + H + 8 * t + 7)
                rows = slice(8 * t, 8 * t + 8)
                main, side = phi_ref[end, 0, z + H, at], phi_ref[end, 1, z + H, at]
                west = jnp.where(first, roll(side, 1, 1), roll(main, 1, 1))
                east = jnp.where(last, roll(side, -1, 1), roll(main, -1, 1))
                south, north = phi_ref[end, 0, z + H, down], phi_ref[end, 0, z + H, up]
                below, above = phi_ref[end, 0, z + H - 1, at], phi_ref[end, 0, z + H + 1, at]
                vel_buf[0, z, rows] = pred_ref[0, z, rows] - DT * 0.5 * (east - west)
                vel_buf[1, z, rows] = pred_ref[1, z, rows] - DT * 0.5 * (north - south)
                vel_buf[2, z, rows] = pred_ref[2, z, rows] - DT * 0.5 * (above - below)
                pres_buf[z, rows] = pres_ref[z, rows] + main
        part = pl.ds(c * CH, CH)
        for k in range(3):
            copies.append(pltpu.make_async_copy(vel_buf.at[k, part], vel_out.at[k, part], sems.at[4 * c + k]))
        copies.append(pltpu.make_async_copy(pres_buf.at[part], pres_out.at[part], sems.at[4 * c + 3]))
        for copy in copies[-4:]:
            copy.start()
    for copy in copies:
        copy.wait()

def swap(up, down, axis):
    count = lax.axis_size(axis)
    forward = [(i, (i + 1) % count) for i in range(count)]
    backward = [(j, i) for i, j in forward]
    return lax.ppermute(up, axis, forward), lax.ppermute(down, axis, backward)


def shape(*dims):
    return jax.ShapeDtypeStruct(dims, F32)


SMEM = pl.BlockSpec(memory_space=pltpu.SMEM)
VMEM = pl.BlockSpec(memory_space=pltpu.VMEM)


ANY = pl.BlockSpec(memory_space=pl.ANY)
MIB = 1024 * 1024
ENTRY_LIMIT = 60


def call(kernel, scalars, arrays, outs, scratch=(), in_specs=None, out_specs=None, limit=24, cost=0):
    return pl.pallas_call(
        kernel,
        out_shape=outs,
        in_specs=[SMEM] * len(scalars) + list(in_specs or [VMEM] * len(arrays)),
        out_specs=out_specs or [VMEM] * len(outs),
        scratch_shapes=list(scratch),
        compiler_params=pltpu.CompilerParams(vmem_limit_bytes=limit * MIB),
        cost_estimate=pl.CostEstimate(flops=cost, bytes_accessed=cost // 64, transcendentals=0) if cost else None,
    )(*scalars, *arrays)


def shards(
    velocity, adjoint, pressure, viscosity, disk_cells, disk_turbine, disk_weight, disk_dweight, yaw, thrust_coef, owner_slot,
):
    axes = ("gx", "gy", "gz")
    n_gx, n_gy, n_gz = (lax.axis_size(a) for a in axes)
    n_dev = n_gx * n_gy * n_gz
    dims = (n_dev, n_gx, n_gy, n_gz)
    pos = jnp.stack([lax.axis_index(a) for a in axes]).astype(jnp.int32)
    turbines = owner_slot.shape[0]
    if turbines % CX:
        owner_slot = jnp.pad(owner_slot, (0, CX - turbines % CX))
    owner = owner_slot.reshape(-1, CX)
    cells, turbine, weight = (a.reshape(1, -1) for a in (disk_cells, disk_turbine, disk_weight))

    payload, xr, xl, yr, yl, zr, zl = call(
        functools.partial(entry_kernel, n_dev, n_gy),
        (pos, yaw, thrust_coef),
        (velocity, adjoint, cells, turbine, weight, disk_dweight, owner),
        (
            shape(n_dev, CX), shape(CY, CX), shape(CY, CX), shape(6 * CZ, CX), shape(6 * CZ, CX),
            shape(6, CY, CX), shape(6, CY, CX),
        ),
        (pltpu.VMEM((6, CZ, CY, CX), F32), pltpu.SemaphoreType.DMA((6,))),
        [ANY, ANY] + [VMEM] * 5,
        limit=ENTRY_LIMIT,
    )
    got = lax.all_to_all(payload, axes, 0, 0, tiled=True)
    xlo, xhi = swap(xr, xl, "gx")
    ylo, yhi = swap(yr, yl, "gy")
    xlo, zl = lax.optimization_barrier((xlo, zl))
    zlo, zhi = swap(zr, zl, "gz")
    faces = (xlo, xhi, ylo, yhi, zlo, zhi)

    pred_base, dual_base = call(
        functools.partial(base_kernel, dims),
        (pos,),
        (velocity, adjoint, viscosity, cells, turbine, weight, owner, got),
        (shape(3, CZ, CY, CX), shape(3, CZ, CY, CX)),
        (pltpu.VMEM((3, CZ, CY, CX), F32),),
        cost=1 << 30,
    )
    predicted, dm, ds, xr, xl = call(
        functools.partial(flow_kernel, dims),
        (pos,),
        (pred_base, viscosity) + faces,
        (shape(3, CZ, CY, CX), shape(SZ, EY, CX), shape(SZ, EY, CX), shape(3, EY, CX), shape(3, EY, CX)),
    )
    lo, hi = swap(xr, xl, "gx")
    adjoint_next, yaw_grad, position_grad = call(
        functools.partial(dual_kernel, dims),
        (pos, yaw, thrust_coef),
        (dual_base, viscosity, got) + faces,
        (shape(3, CZ, CY, CX), shape(1, 4), shape(2, 4)),
        (pltpu.VMEM((3, CZ, CY, CX), F32), pltpu.SemaphoreType.DMA((3,))),
        out_specs=[ANY, VMEM, VMEM],
        cost=1 << 29,
    )
    dm, ds, up, down = call(
        functools.partial(x_kernel, dims), (pos,), (dm, ds, lo, hi),
        (shape(SZ, EY, CX), shape(SZ, EY, CX), shape(27, H, CX), shape(27, H, CX)),
    )
    lo, hi = swap(up, down, "gy")
    dm, ds, up, down = call(
        functools.partial(y_kernel, dims), (pos,), (dm, ds, lo, hi),
        (shape(SZ, EY, CX), shape(SZ, EY, CX), shape(H + 2, EY, CX), shape(H + 2, EY, CX)),
    )
    lo, hi = swap(up, down, "gz")
    velocity_next, pressure_next = call(
        functools.partial(sweep_kernel, dims), (pos,), (dm, ds, lo, hi, predicted, pressure),
        (shape(3, CZ, CY, CX), shape(CZ, CY, CX)),
        (
            pltpu.VMEM((2, EZ, EY, CX), F32), pltpu.VMEM((2, 2, EZ, EY + 2 * PADR, CX), F32),
            pltpu.VMEM((3, CZ, CY, CX), F32), pltpu.VMEM((CZ, CY, CX), F32), pltpu.SemaphoreType.DMA((16,)),
        ),
        out_specs=[ANY, ANY],
    )
    return velocity_next, adjoint_next, pressure_next, yaw_grad.reshape(-1), position_grad


def solution(mesh):
    axes = ("gx", "gy", "gz")
    grid = P(None, "gz", "gy", "gx")
    cell = P("gz", "gy", "gx")
    flat = P(axes)
    return jax.shard_map(
        shards,
        mesh=mesh,
        in_specs=(grid, grid, cell, cell, flat, flat, flat, P(None, axes), flat, flat, P()),
        out_specs=(grid, grid, cell, flat, P(None, axes)),
        check_vma=False,
    )
```

```python
import functools

import jax
import jax.numpy as jnp
from jax import lax
from jax.experimental import pallas as pl
from jax.experimental.pallas import tpu as pltpu
from jax.sharding import PartitionSpec as P

SWEEPS = 8
DT = 0.2
F32 = jnp.float32
BF16 = jnp.bfloat16
CZ, CY, CX = 16, 32, 128
KJ = CZ * CY
H = 8
EZ, EY = CZ + 2 * H, CY + 2 * H
SZ = CZ + 2
TILES = EY // H
PADR = 8
PER = 16
WIN = 64
YAW = 112
NN = (((1,), (0,)), ((), ()))
NT = (((1,), (1,)), ((), ()))
TN = (((0,), (0,)), ((), ()))


def iota(shape, dim):
    return lax.broadcasted_iota(jnp.int32, shape, dim)


def pieces(x, count):
    parts = []
    for _ in range(count):
        head = x.astype(BF16)
        parts.append(head)
        x = x - head.astype(F32)
    return parts


def dots(left, right, dims):
    total = None
    for a in left:
        for b in right:
            term = lax.dot_general(a, b, dims, preferred_element_type=F32)
            total = term if total is None else total + term
    return total


def onehot(mask):
    return jnp.where(mask, 1.0, 0.0).astype(BF16)


def roll(x, shift, axis):
    return pltpu.roll(x, shift % x.shape[axis], axis)


def entry_onehots(cells):
    row = lax.shift_right_logical(cells, 7)
    lane = jnp.bitwise_and(cells, CX - 1)
    count = cells.shape[1]
    rows = onehot(iota((KJ, count), 0) == row)
    lanes = iota((CX, count), 0) == lane
    return rows, lanes


def window_lane(turbine, bx, n_gy):
    column_x = lax.shift_right_logical(turbine, 4) // n_gy
    return WIN + (column_x - bx + 1) * PER + jnp.bitwise_and(turbine, PER - 1)


def lookup(table_ref, turbine):
    count = turbine.shape[1]
    table = table_ref[...]
    owner = lax.shift_right_logical(table, 2).astype(F32)
    which = jnp.bitwise_and(table, 3).astype(F32)
    rows = table.shape[0]
    high = lax.shift_right_logical(turbine, 7)
    low = onehot(iota((CX, count), 0) == jnp.bitwise_and(turbine, CX - 1))
    keep = iota((rows, count), 0) == high
    out = []
    for part in (owner, which):
        picked = dots([part.astype(BF16)], [low], NN)
        picked = jnp.sum(jnp.where(keep, picked, 0.0), axis=0, keepdims=True)
        out.append(picked.astype(jnp.int32))
    return out


def entry_kernel(
    n_dev, n_gy, pos_ref, yaw_ref, ct_ref, vel_hbm, adj_hbm, cells_ref, turb_ref, weight_ref, dweight_ref, owner_ref,
    pay_ref, xr_ref, xl_ref, yr_ref, yl_ref, zr_ref, zl_ref, fld_ref, out_ref, sems,
):
    order = (0, 3, 4, 1, 2, 5)
    copies = {}
    for f in order:
        hbm = vel_hbm.at[f] if f < 3 else adj_hbm.at[f - 3]
        copies[f] = pltpu.make_async_copy(hbm, fld_ref.at[f], sems.at[f])
        copies[f].start()
    bx = pos_ref[0]
    cells, turbine, weight = cells_ref[...], turb_ref[...], weight_ref[...]
    count = cells.shape[1]
    rows, lanes = entry_onehots(cells)
    owner, which = lookup(owner_ref, turbine)
    to_owner = onehot(iota((n_dev, count), 0) == owner)
    in_window = onehot(iota((CX, count), 0) == window_lane(turbine, bx, n_gy))

    columns = []
    for f in order[:3]:
        copies[f].wait()
        columns += pieces(fld_ref[f].reshape(KJ, CX), 2)
    at_row = dots([jnp.concatenate(columns, axis=1)], [rows], TN)
    gathered = []
    for k in range(3):
        both = at_row[2 * k * CX:(2 * k + 1) * CX] + at_row[(2 * k + 1) * CX:(2 * k + 2) * CX]
        gathered.append(jnp.sum(jnp.where(lanes, both, 0.0), axis=0, keepdims=True))
    factors = [weight, dweight_ref[0:1, :], dweight_ref[1:2, :]]
    values = [f * g for f in factors for g in gathered]

    sub = iota((PER, count), 0)
    stacked = jnp.zeros((PER, count), F32)
    for v, value in enumerate(values):
        stacked = jnp.where(sub == v, value, stacked)
    per_slot = jnp.concatenate(
        [jnp.where(which == i, stacked, 0.0) for i in range(4)] + [jnp.zeros((CX - 4 * PER, count), F32)], axis=0
    )
    payload = dots([to_owner], pieces(per_slot, 2), NT)

    speed = jnp.broadcast_to(values[0], (8, count))
    shared = dots(pieces(speed, 2), [in_window], NT)[0:1, :]
    lane = iota((1, CX), 1)
    for i in range(4):
        shared = jnp.where(lane == YAW + i, yaw_ref[i], shared)
        shared = jnp.where(lane == YAW + 4 + i, ct_ref[i], shared)
    out_ref[...] = payload + shared
    leaving = pltpu.make_async_copy(out_ref, pay_ref, sems.at[6])
    leaving.start()

    for f in order[3:]:
        copies[f].wait()
    lane = iota((H, CX), 1)
    for t in range(CY // H):
        at = slice(H * t, H * t + H)
        right = jnp.zeros((H, CX), F32)
        left = jnp.zeros((H, CX), F32)
        for f in range(6):
            for z in range(CZ):
                tile = fld_ref[f, z, at]
                spot = lane == f * CZ + z
                right = jnp.where(spot, roll(tile, f * CZ + z + 1, 1), right)
                left = jnp.where(spot, roll(tile, f * CZ + z, 1), left)
        xr_ref[at] = right
        xl_ref[at] = left
    for f in range(6):
        yr_ref[f * CZ:(f + 1) * CZ, :] = fld_ref[f, :, CY - 1, :]
        yl_ref[f * CZ:(f + 1) * CZ, :] = fld_ref[f, :, 0, :]
        zr_ref[f] = fld_ref[f, CZ - 1]
        zl_ref[f] = fld_ref[f, 0]
    leaving.wait()


def turbine_terms(speed, yaw, thrust_coef):
    cosine = jnp.cos(yaw)
    sine = jnp.sin(yaw)
    magnitude = jnp.abs(speed)
    force = 0.5 * thrust_coef * speed * magnitude * cosine * cosine
    weighting = 1.5 * thrust_coef * speed * magnitude * cosine * cosine * cosine
    return cosine, sine, magnitude, force, weighting


def owner_outputs(got, yaw_ref, ct_ref, yaw_out, pos_out):
    total = jnp.sum(got, axis=0, keepdims=True)
    total = jnp.broadcast_to(total, (8, CX))
    lane = iota((8, CX), 1)
    yaw = jnp.zeros((8, CX), F32)
    ct = jnp.zeros((8, CX), F32)
    for i in range(4):
        yaw = jnp.where(lane == i * PER, yaw_ref[i], yaw)
        ct = jnp.where(lane == i * PER, ct_ref[i], ct)

    def at(v):
        return roll(total, -v, 1)

    speed, dual_x, dual_y = total, at(1), at(2)
    cosine, sine, magnitude, force, weighting = turbine_terms(speed, yaw, ct)
    yaw_grad = -1.5 * ct * magnitude * magnitude * magnitude * cosine * cosine * sine + force * (
        sine * dual_x - cosine * dual_y
    )
    grads = [yaw_grad]
    for r in range(2):
        grads.append(weighting * at(3 + 3 * r) - force * cosine * at(4 + 3 * r) - force * sine * at(5 + 3 * r))
    packed = []
    for grad in grads:
        out = jnp.zeros((8, CX), F32)
        for i in range(4):
            out = jnp.where(lane == i, roll(grad, -(PER - 1) * i, 1), out)
        packed.append(out)
    yaw_out[...] = packed[0][0:1, 0:4]
    pos_out[0:1, :] = packed[1][0:1, 0:4]
    pos_out[1:2, :] = packed[2][0:1, 0:4]


def window_terms(got, n_dev, n_gx, n_gy, n_gz, bx, by, owner_ref):
    lane = iota((1, CX), 1)
    inside = jnp.logical_and(lane >= WIN, lane < WIN + 3 * PER)
    row = iota((n_dev, CX), 0)
    speed = jnp.zeros((1, CX), F32)
    for delta in range(-2, 3):
        base = ((bx + delta) * n_gy + by) * n_gz
        keep = jnp.logical_and(row >= base, row < base + n_gz)
        part = jnp.sum(jnp.where(keep, got, 0.0), axis=0, keepdims=True)
        part = jnp.broadcast_to(jnp.where(inside, part, 0.0), (8, CX))
        speed = speed + roll(part, delta * PER, 1)[0:1, :]
    speed = jnp.where(inside, speed, 0.0)

    table = owner_ref[...]
    sub = iota(table.shape, 0)
    slots = jnp.zeros((1, CX), jnp.int32)
    for j in range(3):
        column_x = jnp.clip(bx - 1 + j, 0, n_gx - 1)
        first = (column_x * n_gy + by) * PER
        picked = jnp.sum(jnp.where(sub == first // CX, table, 0), axis=0, keepdims=True)
        picked = jnp.broadcast_to(picked, (8, CX))
        moved = pltpu.roll(picked, jnp.bitwise_and(WIN + PER * j - first, CX - 1), 1)[0:1, :]
        here = jnp.logical_and(lane >= WIN + PER * j, lane < WIN + PER * (j + 1))
        slots = jnp.where(here, moved, slots)
    owner = onehot(iota((n_dev, CX), 0) == lax.shift_right_logical(slots, 2))
    which = jnp.bitwise_and(slots, 3)
    found = dots(pieces(got, 3), [owner], TN)
    yaw = jnp.zeros((1, CX), F32)
    ct = jnp.zeros((1, CX), F32)
    for i in range(4):
        yaw = jnp.where(which == i, found[YAW + i:YAW + i + 1, :], yaw)
        ct = jnp.where(which == i, found[YAW + 4 + i:YAW + 5 + i, :], ct)
    cosine, sine, magnitude, force, weighting = turbine_terms(speed, yaw, ct)
    keep = lambda x: jnp.where(inside, x, 0.0)
    return keep(force * cosine), keep(force * sine), keep(weighting)


def edges(pos_ref, dims):
    n_dev, n_gx, n_gy, n_gz = dims
    out = []
    for k, count in enumerate((n_gx, n_gy, n_gz)):
        out.append(jnp.where(pos_ref[k] > 0, 1.0, 0.0))
        out.append(jnp.where(pos_ref[k] < count - 1, 1.0, 0.0))
    return out


def tile_rows(t):
    return slice(H * t, H * t + H)


def south_of(ref, index, t, sub):
    if t > 0:
        return ref[index + (slice(H * t - 1, H * t + H - 1),)]
    return jnp.where(sub == 0, 0.0, roll(ref[index + (tile_rows(0),)], 1, 0))


def north_of(ref, index, t, sub):
    if t < CY // H - 1:
        return ref[index + (slice(H * t + 1, H * t + H + 1),)]
    return jnp.where(sub == H - 1, 0.0, roll(ref[index + (tile_rows(t),)], -1, 0))


def base_kernel(
    dims, pos_ref, vel_ref, adj_ref, visc_ref, cells_ref, turb_ref, weight_ref, owner_ref, got_ref,
    pred_ref, dual_ref, field_ref,
):
    n_dev, n_gx, n_gy, n_gz = dims
    bx, by = pos_ref[0], pos_ref[1]
    terms = window_terms(got_ref[...], n_dev, n_gx, n_gy, n_gz, bx, by, owner_ref)
    cells, turbine, weight = cells_ref[...], turb_ref[...], weight_ref[...]
    count = cells.shape[1]
    rows, lanes = entry_onehots(cells)
    in_window = onehot(iota((CX, count), 0) == window_lane(turbine, bx, n_gy))
    stacked = jnp.concatenate([jnp.broadcast_to(t, (8, CX)) for t in terms], axis=0)
    per_entry = dots(pieces(stacked, 2), [in_window], NN)
    for c in range(3):
        value = per_entry[8 * c:8 * c + 1, :] * weight
        if c < 2:
            value = -value
        spread = jnp.where(lanes, value, 0.0)
        field_ref[c] = dots([rows], pieces(spread, 2), NT).reshape(CZ, CY, CX)

    lane = iota((H, CX), 1)
    sub = iota((H, CX), 0)
    zero = jnp.zeros((H, CX), F32)
    for t in range(CY // H):
        at = tile_rows(t)
        for f in range(6):
            ref, comp = (vel_ref, f) if f < 3 else (adj_ref, f - 3)
            out = pred_ref if f < 3 else dual_ref
            below, tile = zero, ref[comp, 0, at]
            for z in range(CZ):
                above = ref[comp, z + 1, at] if z < CZ - 1 else zero
                south, north = south_of(ref, (comp, z), t, sub), north_of(ref, (comp, z), t, sub)
                west = jnp.where(lane == 0, 0.0, roll(tile, 1, 1))
                east = jnp.where(lane == CX - 1, 0.0, roll(tile, -1, 1))
                lap = (above + below) + (north + south) + (east + west) - 6.0 * tile
                rate = visc_ref[z, at] * lap
                rate = rate + (west - tile if f < 3 else east - tile)
                if f < 2:
                    rate = rate + field_ref[f, z, at]
                if f == 3:
                    rate = rate + field_ref[2, z, at]
                out[comp, z, at] = tile + DT * rate
                below, tile = tile, above


def add_faces(f, first, out, given, visc_ref, bounds, xlo_ref, xhi_ref, ylo_ref, yhi_ref, zlo_ref, zhi_ref):
    lo_x, hi_x, lo_y, hi_y, lo_z, hi_z = bounds
    lane = iota((H, CX), 1)
    sub = iota((H, CX), 0)
    flow = f < 3
    comp = f - first
    for t in range(CY // H):
        at = tile_rows(t)
        face_lo, face_hi = xlo_ref[at] * lo_x, xhi_ref[at] * hi_x
        for z in range(CZ):
            spot = f * CZ + z
            west = jnp.where(lane == 0, roll(face_lo, -spot, 1), 0.0)
            east = jnp.where(lane == CX - 1, roll(face_hi, CX - 1 - spot, 1), 0.0)
            lap = west + east
            if t == 0:
                lap = lap + jnp.where(sub == 0, ylo_ref[spot:spot + 1, :] * lo_y, 0.0)
            if t == CY // H - 1:
                lap = lap + jnp.where(sub == H - 1, yhi_ref[spot:spot + 1, :] * hi_y, 0.0)
            if z == 0:
                lap = lap + zlo_ref[f, at] * lo_z
            if z == CZ - 1:
                lap = lap + zhi_ref[f, at] * hi_z
            out[comp, z, at] = given[comp, z, at] + DT * (visc_ref[z, at] * lap + (west if flow else east))


def fold_shift(z):
    return H + 16 * (z % 8)


def flow_kernel(
    dims, pos_ref, base_ref, visc_ref, xlo_ref, xhi_ref, ylo_ref, yhi_ref, zlo_ref, zhi_ref,
    pred_ref, dm_ref, ds_ref, xr_ref, xl_ref,
):
    bounds = edges(pos_ref, dims)
    for f in range(3):
        add_faces(f, 0, pred_ref, base_ref, visc_ref, bounds, xlo_ref, xhi_ref, ylo_ref, yhi_ref, zlo_ref, zhi_ref)
    lane = iota((H, CX), 1)
    sub = iota((H, CX), 0)
    zero = jnp.zeros((H, CX), F32)
    for r in range(EY // H):
        at = tile_rows(r)
        t = r - 1
        inside = 0 <= t < CY // H
        for k in range(SZ):
            z = k - 1
            main, side = zero, zero
            if inside and 0 <= z < CZ:
                own = tile_rows(t)
                p0 = pred_ref[0, z, own]
                west, east = roll(p0, 1, 1), roll(p0, -1, 1)
                div = jnp.where(lane == CX - 1, 0.0, east) - jnp.where(lane == 0, 0.0, west)
                div = div + (north_of(pred_ref, (1, z), t, sub) - south_of(pred_ref, (1, z), t, sub))
                if z < CZ - 1:
                    div = div + pred_ref[2, z + 1, own]
                if z > 0:
                    div = div - pred_ref[2, z - 1, own]
                main = 0.5 * div
                side = jnp.where(lane == CX - 1, 0.5 * east, jnp.where(lane == 0, -0.5 * west, 0.0))
            elif inside:
                main = 0.5 * pred_ref[2, 0, tile_rows(t)] if z < 0 else -0.5 * pred_ref[2, CZ - 1, tile_rows(t)]
            elif 0 <= z < CZ and t < 0:
                main = jnp.where(sub == H - 1, 0.5 * roll(pred_ref[1, z, 0:H], -1, 0), 0.0)
            elif 0 <= z < CZ:
                main = jnp.where(sub == 0, -0.5 * roll(pred_ref[1, z, CY - H:CY], 1, 0), 0.0)
            dm_ref[k, at] = main
            ds_ref[k, at] = side
    for r in range(EY // H):
        at = tile_rows(r)
        right, left = [zero] * 3, [zero] * 3
        for k in range(SZ):
            if not 0 < r < EY // H - 1 and not 0 < k < SZ - 1:
                continue
            main, side = dm_ref[k, at], ds_ref[k, at]
            g = k % 8
            mine = jnp.logical_and(lane >= 16 * g, lane < 16 * g + 16)
            right[k // 8] = jnp.where(mine, roll(jnp.where(lane < H, side, main), fold_shift(k), 1), right[k // 8])
            left[k // 8] = jnp.where(mine, roll(jnp.where(lane < H, main, side), fold_shift(k), 1), left[k // 8])
        for i in range(3):
            xr_ref[i, at] = right[i]
            xl_ref[i, at] = left[i]


def dual_kernel(
    dims, pos_ref, yaw_ref, ct_ref, base_ref, visc_ref, got_ref, xlo_ref, xhi_ref, ylo_ref, yhi_ref, zlo_ref, zhi_ref,
    dual_out, yaw_out, pos_out, dual_ref, sems,
):
    bounds = edges(pos_ref, dims)
    copies = []
    for f in range(3, 6):
        add_faces(f, 3, dual_ref, base_ref, visc_ref, bounds, xlo_ref, xhi_ref, ylo_ref, yhi_ref, zlo_ref, zhi_ref)
        copies.append(pltpu.make_async_copy(dual_ref.at[f - 3], dual_out.at[f - 3], sems.at[f - 3]))
        copies[-1].start()
    owner_outputs(got_ref[...], yaw_ref, ct_ref, yaw_out, pos_out)
    for copy in copies:
        copy.wait()


def x_kernel(dims, pos_ref, dm_ref, ds_ref, lo_ref, hi_ref, om_ref, os_ref, up_ref, down_ref):
    in_lo, in_hi = edges(pos_ref, dims)[0:2]
    lane = iota((H, CX), 1)
    head, tail = lane < H, lane >= CX - H
    zero = jnp.zeros((H, CX), F32)
    for r in range(EY // H):
        at = tile_rows(r)
        lows = [lo_ref[i, at] * in_lo for i in range(3)]
        highs = [hi_ref[i, at] * in_hi for i in range(3)]
        for z in range(SZ):
            lo = roll(lows[z // 8], -fold_shift(z), 1)
            hi = roll(highs[z // 8], -fold_shift(z), 1)
            om_ref[z, at] = dm_ref[z, at] + jnp.where(head, lo, jnp.where(tail, hi, 0.0))
            os_ref[z, at] = ds_ref[z, at] + jnp.where(tail, lo, jnp.where(head, hi, 0.0))
    for out, row, edge in ((up_ref, CY, H + CY), (down_ref, H, H - 1)):
        for i in range(3):
            fold = zero
            out[18 + i] = zero
            out[24 + i] = zero
            for g in range(min(8, SZ - 8 * i)):
                z = 8 * i + g
                out[z] = om_ref[z, row:row + H]
                mine = jnp.logical_and(lane >= 16 * g, lane < 16 * g + 16)
                fold = jnp.where(mine, roll(os_ref[z, row:row + H], fold_shift(z), 1), fold)
                out[18 + i, g:g + 1] = om_ref[z, edge:edge + 1]
                out[24 + i, g:g + 1] = os_ref[z, edge:edge + 1]
            out[21 + i] = fold


def y_kernel(dims, pos_ref, dm_ref, ds_ref, lo_ref, hi_ref, om_ref, os_ref, up_ref, down_ref):
    in_lo, in_hi = edges(pos_ref, dims)[2:4]
    lane = iota((H, CX), 1)
    sub = iota((H, CX), 0)
    ends = jnp.logical_or(lane < H, lane >= CX - H)
    zero = jnp.zeros((H, CX), F32)
    last = EY // H - 1
    for r in range(EY // H):
        at = tile_rows(r)
        up_fold, down_fold = zero, zero
        for z in range(SZ):
            tile, g = z // 8, z % 8
            main, side = dm_ref[z, at], ds_ref[z, at]
            if r == 0:
                main = main + lo_ref[z] * in_lo
                side = side + jnp.where(ends, roll(lo_ref[21 + tile], -fold_shift(z), 1) * in_lo, 0.0)
            if r == 1:
                main = main + jnp.where(sub == 0, lo_ref[18 + tile, g:g + 1, :] * in_lo, 0.0)
                side = side + jnp.where(sub == 0, lo_ref[24 + tile, g:g + 1, :] * in_lo, 0.0)
            if r == last - 1:
                main = main + jnp.where(sub == H - 1, hi_ref[18 + tile, g:g + 1, :] * in_hi, 0.0)
                side = side + jnp.where(sub == H - 1, hi_ref[24 + tile, g:g + 1, :] * in_hi, 0.0)
            if r == last:
                main = main + hi_ref[z] * in_hi
                side = side + jnp.where(ends, roll(hi_ref[21 + tile], -fold_shift(z), 1) * in_hi, 0.0)
            om_ref[z, at] = main
            os_ref[z, at] = side
            if z >= CZ - H + 1:
                i = z - (CZ - H + 1)
                up_ref[i, at] = main
                shift = 14 * i + 7 if i < H else 120
                mine = jnp.logical_and(lane >= 14 * i, lane < (14 * i + 14 if i < H else CX))
                up_fold = jnp.where(mine, roll(side, shift, 1), up_fold)
            if z <= H:
                i = z - 1 if z > 0 else H
                down_ref[i, at] = main
                shift = 14 * i + 7 if i < H else 120
                mine = jnp.logical_and(lane >= 14 * i, lane < (14 * i + 14 if i < H else CX))
                down_fold = jnp.where(mine, roll(side, shift, 1), down_fold)
        up_ref[H + 1, at] = up_fold
        down_ref[H + 1, at] = down_fold


def pre_planes(level):
    return (H + 1 + level, H + CZ - 1 - level) if level < SWEEPS - 1 else (0, 0)


def pre_index(level, z):
    return sum(CZ - 2 - 2 * i for i in range(level)) + z - pre_planes(level)[0]


PRE = sum(CZ - 2 - 2 * i for i in range(SWEEPS - 1))


def padded_rows(t, shift=0):
    return slice(PADR + H * t + shift, PADR + H * t + H + shift)


def coefficients(pos_ref, dims):
    lo_x, hi_x, lo_y, hi_y, lo_z, hi_z = edges(pos_ref, dims)
    lane = iota((H, CX), 1)
    low, high = jnp.where(lane >= CX - H, lo_x, 1.0), jnp.where(lane < H, hi_x, 1.0)
    main = [jnp.full((H, CX), 1.0 / 6.0, F32)] * TILES
    main[0] = main[0] * lo_y
    main[-1] = main[-1] * hi_y
    return main, [c * (low * high) for c in main]


def relax(planes, get, put, rhs, weights):
    lane = iota((H, CX), 1)
    first, last = lane == 0, lane == CX - 1
    z0 = planes[0]
    carry = [[get(k, z0 - 1 + i, padded_rows(t)) for k in range(2) for i in range(2)] for t in range(TILES)]
    for z in planes:
        main_weight, side_weight = weights(z)
        for t in range(TILES):
            below, main, side_below, side = carry[t]
            at, up, down = padded_rows(t), padded_rows(t, 1), padded_rows(t, -1)
            above, side_above = get(0, z + 1, at), get(1, z + 1, at)
            main_w, side_w = roll(main, 1, 1), roll(side, 1, 1)
            main_e, side_e = roll(main, -1, 1), roll(side, -1, 1)
            total = (above + below) + (get(0, z, up) + get(0, z, down))
            total = total + (jnp.where(first, side_w, main_w) + jnp.where(last, side_e, main_e))
            put(0, z, at, (total - rhs(0, z, tile_rows(t))) * main_weight[t])
            total = (side_above + side_below) + (get(1, z, up) + get(1, z, down))
            total = total + (jnp.where(first, main_w, side_w) + jnp.where(last, main_e, side_e))
            put(1, z, at, (total - rhs(1, z, tile_rows(t))) * side_weight[t])
            carry[t] = [main, above, side, side_above]


def inner_kernel(dims, pos_ref, dm_ref, ds_ref, pre_ref):
    main_coef, side_coef = coefficients(pos_ref, dims)
    scale = 1.0 / DT
    zero = jnp.zeros((H, CX), F32)
    for i in range(PRE):
        for part in range(2):
            pre_ref[i, part, 0:PADR] = zero
            pre_ref[i, part, PADR + EY:PADR + EY + PADR] = zero

    def rhs(part, z, rows):
        return (ds_ref if part else dm_ref)[z - H + 1, rows] * scale

    for z in range(*pre_planes(0)):
        for t in range(TILES):
            pre_ref[pre_index(0, z), 0, padded_rows(t)] = -rhs(0, z, tile_rows(t)) * main_coef[t]
            pre_ref[pre_index(0, z), 1, padded_rows(t)] = -rhs(1, z, tile_rows(t)) * side_coef[t]
    for level in range(1, SWEEPS - 1):
        def get(part, z, rows, level=level):
            return pre_ref[pre_index(level - 1, z), part, rows]

        def put(part, z, rows, value, level=level):
            pre_ref[pre_index(level, z), part, rows] = value

        relax(range(*pre_planes(level)), get, put, rhs, lambda z: (main_coef, side_coef))


def sweep_kernel(
    dims, pos_ref, dm_ref, ds_ref, pre_ref, lo_ref, hi_ref, pred_ref, pres_ref, vel_out, pres_out,
    b_ref, phi_ref, vel_buf, pres_buf, sems,
):
    lo_z, hi_z = edges(pos_ref, dims)[4:6]
    main_coef, side_coef = coefficients(pos_ref, dims)
    scale = 1.0 / DT
    lane = iota((H, CX), 1)
    first, last = lane == 0, lane == CX - 1
    zero = jnp.zeros((H, CX), F32)
    near = jnp.logical_or(lane < H - 1, lane >= CX - H + 1)
    ends = jnp.logical_or(lane < H, lane >= CX - H)
    lo_scale, hi_scale = lo_z * scale, hi_z * scale
    low_coef = [[c * lo_z for c in main_coef], [c * lo_z for c in side_coef]]
    high_coef = [[c * hi_z for c in main_coef], [c * hi_z for c in side_coef]]

    def weights(z):
        return low_coef if z < H else high_coef if z >= H + CZ else (main_coef, side_coef)

    outer = list(range(pre_planes(0)[0])) + list(range(pre_planes(0)[1], EZ))
    place = {z: i for i, z in enumerate(outer)}

    for z in range(EZ):
        for part in range(2):
            for buf in range(2):
                phi_ref[buf, part, z, 0:PADR] = zero
                phi_ref[buf, part, z, PADR + EY:PADR + EY + PADR] = zero
    for t in range(TILES):
        rows = tile_rows(t)
        folded = (lo_ref[H + 1, rows] * lo_scale, hi_ref[H + 1, rows] * hi_scale)
        for z in outer:
            low = z < EZ // 2
            halo, fold, factor = (lo_ref, folded[0], lo_scale) if low else (hi_ref, folded[1], hi_scale)
            if z < H or z >= H + CZ:
                g = z if low else z - H - CZ
                main = halo[g, rows] * factor
                side = jnp.where(near, roll(fold, -(14 * g + 7), 1), 0.0)
                if z in (H - 1, H + CZ):
                    k = 0 if low else SZ - 1
                    main = main + dm_ref[k, rows] * factor
                    side = side + ds_ref[k, rows] * factor
            else:
                main = dm_ref[z - H + 1, rows] * scale + halo[H, rows] * factor
                side = ds_ref[z - H + 1, rows] * scale + jnp.where(ends, roll(fold, -120, 1), 0.0)
            b_ref[0, place[z], rows] = main
            b_ref[1, place[z], rows] = side
            cm, cs = weights(z)
            phi_ref[0, 0, z, padded_rows(t)] = -main * cm[t]
            phi_ref[0, 1, z, padded_rows(t)] = -side * cs[t]

    def rhs(part, z, rows):
        if z in place:
            return b_ref[part, place[z], rows]
        return (ds_ref if part else dm_ref)[z - H + 1, rows] * scale

    def reader(level):
        known = range(*pre_planes(level))

        def get(part, z, rows):
            if z in known:
                return pre_ref[pre_index(level, z), part, rows]
            return phi_ref[level % 2, part, z, rows]

        return get

    for level in range(1, SWEEPS):
        lo, hi = pre_planes(level)

        def put(part, z, rows, value, level=level):
            phi_ref[level % 2, part, z, rows] = value

        runs = ((level, lo), (hi, EZ - level)) if hi > lo else ((level, EZ - level),)
        for run in runs:
            relax(range(*run), reader(level - 1), put, rhs, weights)

    get = reader(SWEEPS - 1)
    chunk = 4
    copies = []
    for c in range(CZ // chunk):
        for z in range(c * chunk, (c + 1) * chunk):
            for t in range(CY // H):
                rows = tile_rows(t)
                at, up, down = padded_rows(t + 1), padded_rows(t + 1, 1), padded_rows(t + 1, -1)
                main, side = get(0, z + H, at), get(1, z + H, at)
                west = jnp.where(first, roll(side, 1, 1), roll(main, 1, 1))
                east = jnp.where(last, roll(side, -1, 1), roll(main, -1, 1))
                half = DT * 0.5
                vel_buf[0, z, rows] = pred_ref[0, z, rows] - half * (east - west)
                vel_buf[1, z, rows] = pred_ref[1, z, rows] - half * (get(0, z + H, up) - get(0, z + H, down))
                vel_buf[2, z, rows] = pred_ref[2, z, rows] - half * (get(0, z + H + 1, at) - get(0, z + H - 1, at))
                pres_buf[z, rows] = pres_ref[z, rows] + main
        part = pl.ds(c * chunk, chunk)
        copies.append(pltpu.make_async_copy(vel_buf.at[:, part], vel_out.at[:, part], sems.at[2 * c]))
        copies.append(pltpu.make_async_copy(pres_buf.at[part], pres_out.at[part], sems.at[2 * c + 1]))
        for copy in copies[-2:]:
            copy.start()
    for copy in copies:
        copy.wait()


def swap(up, down, axis):
    count = lax.axis_size(axis)
    forward = [(i, (i + 1) % count) for i in range(count)]
    backward = [(j, i) for i, j in forward]
    return lax.ppermute(up, axis, forward), lax.ppermute(down, axis, backward)


def shape(*dims):
    return jax.ShapeDtypeStruct(dims, F32)


SMEM = pl.BlockSpec(memory_space=pltpu.SMEM)
VMEM = pl.BlockSpec(memory_space=pltpu.VMEM)


ANY = pl.BlockSpec(memory_space=pl.ANY)
MIB = 1024 * 1024
ENTRY_LIMIT = 60


def call(kernel, scalars, arrays, outs, scratch=(), in_specs=None, out_specs=None, limit=24, cost=0):
    return pl.pallas_call(
        kernel,
        out_shape=outs,
        in_specs=[SMEM] * len(scalars) + list(in_specs or [VMEM] * len(arrays)),
        out_specs=out_specs or [VMEM] * len(outs),
        scratch_shapes=list(scratch),
        compiler_params=pltpu.CompilerParams(vmem_limit_bytes=limit * MIB),
        cost_estimate=pl.CostEstimate(flops=cost, bytes_accessed=cost // 64, transcendentals=0) if cost else None,
    )(*scalars, *arrays)


def shards(
    velocity, adjoint, pressure, viscosity, disk_cells, disk_turbine, disk_weight, disk_dweight, yaw, thrust_coef, owner_slot,
):
    axes = ("gx", "gy", "gz")
    n_gx, n_gy, n_gz = (lax.axis_size(a) for a in axes)
    n_dev = n_gx * n_gy * n_gz
    dims = (n_dev, n_gx, n_gy, n_gz)
    pos = jnp.stack([lax.axis_index(a) for a in axes]).astype(jnp.int32)
    turbines = owner_slot.shape[0]
    if turbines % CX:
        owner_slot = jnp.pad(owner_slot, (0, CX - turbines % CX))
    owner = owner_slot.reshape(-1, CX)
    cells, turbine, weight = (a.reshape(1, -1) for a in (disk_cells, disk_turbine, disk_weight))

    payload, xr, xl, yr, yl, zr, zl = call(
        functools.partial(entry_kernel, n_dev, n_gy),
        (pos, yaw, thrust_coef),
        (velocity, adjoint, cells, turbine, weight, disk_dweight, owner),
        (
            shape(n_dev, CX), shape(CY, CX), shape(CY, CX), shape(6 * CZ, CX), shape(6 * CZ, CX),
            shape(6, CY, CX), shape(6, CY, CX),
        ),
        (pltpu.VMEM((6, CZ, CY, CX), F32), pltpu.VMEM((n_dev, CX), F32), pltpu.SemaphoreType.DMA((7,))),
        [ANY, ANY] + [VMEM] * 5,
        [ANY] + [VMEM] * 6,
        limit=ENTRY_LIMIT,
    )
    got = lax.all_to_all(payload, axes, 0, 0, tiled=True)
    xlo, xhi = swap(xr, xl, "gx")
    ylo, yhi = swap(yr, yl, "gy")
    xlo, zl = lax.optimization_barrier((xlo, zl))
    zlo, zhi = swap(zr, zl, "gz")
    faces = (xlo, xhi, ylo, yhi, zlo, zhi)

    pred_base, dual_base = call(
        functools.partial(base_kernel, dims),
        (pos,),
        (velocity, adjoint, viscosity, cells, turbine, weight, owner, got),
        (shape(3, CZ, CY, CX), shape(3, CZ, CY, CX)),
        (pltpu.VMEM((3, CZ, CY, CX), F32),),
        cost=1 << 30,
    )
    predicted, dm, ds, xr, xl = call(
        functools.partial(flow_kernel, dims),
        (pos,),
        (pred_base, viscosity) + faces,
        (shape(3, CZ, CY, CX), shape(SZ, EY, CX), shape(SZ, EY, CX), shape(3, EY, CX), shape(3, EY, CX)),
    )
    adjoint_next, yaw_grad, position_grad = call(
        functools.partial(dual_kernel, dims),
        (pos, yaw, thrust_coef),
        (dual_base, viscosity, got) + faces,
        (shape(3, CZ, CY, CX), shape(1, 4), shape(2, 4)),
        (pltpu.VMEM((3, CZ, CY, CX), F32), pltpu.SemaphoreType.DMA((3,))),
        out_specs=[ANY, VMEM, VMEM],
        cost=1 << 30,
    )
    lo, hi = swap(xr, xl, "gx")
    dm, ds, up, down = call(
        functools.partial(x_kernel, dims), (pos,), (dm, ds, lo, hi),
        (shape(SZ, EY, CX), shape(SZ, EY, CX), shape(27, H, CX), shape(27, H, CX)),
    )
    lo, hi = swap(up, down, "gy")
    lo, yaw_grad = lax.optimization_barrier((lo, yaw_grad))
    dm, ds, up, down = call(
        functools.partial(y_kernel, dims), (pos,), (dm, ds, lo, hi),
        (shape(SZ, EY, CX), shape(SZ, EY, CX), shape(H + 2, EY, CX), shape(H + 2, EY, CX)),
    )
    lo, hi = swap(up, down, "gz")
    pre = call(
        functools.partial(inner_kernel, dims), (pos,), (dm, ds), (shape(PRE, 2, EY + 2 * PADR, CX),), cost=1 << 30
    )[0]
    velocity_next, pressure_next = call(
        functools.partial(sweep_kernel, dims), (pos,), (dm, ds, pre, lo, hi, predicted, pressure),
        (shape(3, CZ, CY, CX), shape(CZ, CY, CX)),
        (
            pltpu.VMEM((2, EZ - CZ + 2, EY, CX), F32), pltpu.VMEM((2, 2, EZ, EY + 2 * PADR, CX), F32),
            pltpu.VMEM((3, CZ, CY, CX), F32), pltpu.VMEM((CZ, CY, CX), F32), pltpu.SemaphoreType.DMA((8,)),
        ),
        out_specs=[ANY, ANY],
    )
    return velocity_next, adjoint_next, pressure_next, yaw_grad.reshape(-1), position_grad


def solution(mesh):
    axes = ("gx", "gy", "gz")
    grid = P(None, "gz", "gy", "gx")
    cell = P("gz", "gy", "gx")
    flat = P(axes)
    return jax.shard_map(
        shards,
        mesh=mesh,
        in_specs=(grid, grid, cell, cell, flat, flat, flat, P(None, axes), flat, flat, P()),
        out_specs=(grid, grid, cell, flat, P(None, axes)),
        check_vma=False,
    )
```

```python
import functools

import jax
import jax.numpy as jnp
from jax import lax
from jax.experimental import pallas as pl
from jax.experimental.pallas import tpu as pltpu
from jax.sharding import PartitionSpec as P

SWEEPS = 8
DT = 0.2
F32 = jnp.float32
BF16 = jnp.bfloat16
CZ, CY, CX = 16, 32, 128
KJ = CZ * CY
H = 8
EZ, EY = CZ + 2 * H, CY + 2 * H
SZ = CZ + 2
TILES = EY // H
PADR = 8
PER = 16
WIN = 64
YAW = 112
NN = (((1,), (0,)), ((), ()))
NT = (((1,), (1,)), ((), ()))
TN = (((0,), (0,)), ((), ()))


def iota(shape, dim):
    return lax.broadcasted_iota(jnp.int32, shape, dim)


def pieces(x, count):
    parts = []
    for _ in range(count):
        head = x.astype(BF16)
        parts.append(head)
        x = x - head.astype(F32)
    return parts


def dots(left, right, dims):
    total = None
    for a in left:
        for b in right:
            term = lax.dot_general(a, b, dims, preferred_element_type=F32)
            total = term if total is None else total + term
    return total


def onehot(mask):
    return jnp.where(mask, 1.0, 0.0).astype(BF16)


def roll(x, shift, axis):
    return pltpu.roll(x, shift % x.shape[axis], axis)


def entry_onehots(cells):
    row = lax.shift_right_logical(cells, 7)
    lane = jnp.bitwise_and(cells, CX - 1)
    count = cells.shape[1]
    rows = onehot(iota((KJ, count), 0) == row)
    lanes = iota((CX, count), 0) == lane
    return rows, lanes


def window_lane(turbine, bx, n_gy):
    column_x = lax.shift_right_logical(turbine, 4) // n_gy
    return WIN + (column_x - bx + 1) * PER + jnp.bitwise_and(turbine, PER - 1)


def lookup(table_ref, turbine):
    count = turbine.shape[1]
    table = table_ref[...]
    owner = lax.shift_right_logical(table, 2).astype(F32)
    which = jnp.bitwise_and(table, 3).astype(F32)
    rows = table.shape[0]
    high = lax.shift_right_logical(turbine, 7)
    low = onehot(iota((CX, count), 0) == jnp.bitwise_and(turbine, CX - 1))
    keep = iota((rows, count), 0) == high
    out = []
    for part in (owner, which):
        picked = dots([part.astype(BF16)], [low], NN)
        picked = jnp.sum(jnp.where(keep, picked, 0.0), axis=0, keepdims=True)
        out.append(picked.astype(jnp.int32))
    return out


def entry_kernel(
    n_dev, n_gy, pos_ref, yaw_ref, ct_ref, vel_hbm, adj_hbm, visc_hbm, cells_ref, turb_ref, weight_ref, dweight_ref, owner_ref,
    pay_ref, xr_ref, xl_ref, yr_ref, yl_ref, zr_ref, zl_ref, fld_ref, index_ref, scale_ref, table_ref, out_ref, sems,
):
    order = (0, 3, 4, 1, 2, 5, 6)
    copies = {}
    for f in order:
        hbm = vel_hbm.at[f] if f < 3 else adj_hbm.at[f - 3] if f < 6 else visc_hbm
        copies[f] = pltpu.make_async_copy(hbm, fld_ref.at[f], sems.at[f])
        copies[f].start()
    bx = pos_ref[0]
    cells, turbine, weight = cells_ref[...], turb_ref[...], weight_ref[...]
    index_ref[0:1, :] = cells
    index_ref[1:2, :] = turbine
    scale_ref[...] = weight
    table_ref[...] = owner_ref[...]
    count = cells.shape[1]
    rows, lanes = entry_onehots(cells)
    owner, which = lookup(owner_ref, turbine)
    to_owner = onehot(iota((n_dev, count), 0) == owner)
    in_window = onehot(iota((CX, count), 0) == window_lane(turbine, bx, n_gy))

    columns = []
    for f in order[:3]:
        copies[f].wait()
        columns += pieces(fld_ref[f].reshape(KJ, CX), 2)
    at_row = dots([jnp.concatenate(columns, axis=1)], [rows], TN)
    gathered = []
    for k in range(3):
        both = at_row[2 * k * CX:(2 * k + 1) * CX] + at_row[(2 * k + 1) * CX:(2 * k + 2) * CX]
        gathered.append(jnp.sum(jnp.where(lanes, both, 0.0), axis=0, keepdims=True))
    factors = [weight, dweight_ref[0:1, :], dweight_ref[1:2, :]]
    values = [f * g for f in factors for g in gathered]

    sub = iota((PER, count), 0)
    stacked = jnp.zeros((PER, count), F32)
    for v, value in enumerate(values):
        stacked = jnp.where(sub == v, value, stacked)
    per_slot = jnp.concatenate(
        [jnp.where(which == i, stacked, 0.0) for i in range(4)] + [jnp.zeros((CX - 4 * PER, count), F32)], axis=0
    )
    payload = dots([to_owner], pieces(per_slot, 2), NT)

    speed = jnp.broadcast_to(values[0], (8, count))
    shared = dots(pieces(speed, 2), [in_window], NT)[0:1, :]
    lane = iota((1, CX), 1)
    for i in range(4):
        shared = jnp.where(lane == YAW + i, yaw_ref[i], shared)
        shared = jnp.where(lane == YAW + 4 + i, ct_ref[i], shared)
    out_ref[...] = payload + shared
    leaving = pltpu.make_async_copy(out_ref, pay_ref, sems.at[7])
    leaving.start()

    for f in order[3:]:
        copies[f].wait()
    lane = iota((H, CX), 1)
    for t in range(CY // H):
        at = slice(H * t, H * t + H)
        right = jnp.zeros((H, CX), F32)
        left = jnp.zeros((H, CX), F32)
        for f in range(6):
            for z in range(CZ):
                tile = fld_ref[f, z, at]
                spot = lane == f * CZ + z
                right = jnp.where(spot, roll(tile, f * CZ + z + 1, 1), right)
                left = jnp.where(spot, roll(tile, f * CZ + z, 1), left)
        xr_ref[at] = right
        xl_ref[at] = left
    for f in range(6):
        yr_ref[f * CZ:(f + 1) * CZ, :] = fld_ref[f, :, CY - 1, :]
        yl_ref[f * CZ:(f + 1) * CZ, :] = fld_ref[f, :, 0, :]
        zr_ref[f] = fld_ref[f, CZ - 1]
        zl_ref[f] = fld_ref[f, 0]
    leaving.wait()


def turbine_terms(speed, yaw, thrust_coef):
    cosine = jnp.cos(yaw)
    sine = jnp.sin(yaw)
    magnitude = jnp.abs(speed)
    force = 0.5 * thrust_coef * speed * magnitude * cosine * cosine
    weighting = 1.5 * thrust_coef * speed * magnitude * cosine * cosine * cosine
    return cosine, sine, magnitude, force, weighting


def owner_outputs(got, yaw_ref, ct_ref, yaw_out, pos_out):
    total = jnp.sum(got, axis=0, keepdims=True)
    total = jnp.broadcast_to(total, (8, CX))
    lane = iota((8, CX), 1)
    yaw = jnp.zeros((8, CX), F32)
    ct = jnp.zeros((8, CX), F32)
    for i in range(4):
        yaw = jnp.where(lane == i * PER, yaw_ref[i], yaw)
        ct = jnp.where(lane == i * PER, ct_ref[i], ct)

    def at(v):
        return roll(total, -v, 1)

    speed, dual_x, dual_y = total, at(1), at(2)
    cosine, sine, magnitude, force, weighting = turbine_terms(speed, yaw, ct)
    yaw_grad = -1.5 * ct * magnitude * magnitude * magnitude * cosine * cosine * sine + force * (
        sine * dual_x - cosine * dual_y
    )
    grads = [yaw_grad]
    for r in range(2):
        grads.append(weighting * at(3 + 3 * r) - force * cosine * at(4 + 3 * r) - force * sine * at(5 + 3 * r))
    packed = []
    for grad in grads:
        out = jnp.zeros((8, CX), F32)
        for i in range(4):
            out = jnp.where(lane == i, roll(grad, -(PER - 1) * i, 1), out)
        packed.append(out)
    yaw_out[...] = packed[0][0:1, 0:4]
    pos_out[0:1, :] = packed[1][0:1, 0:4]
    pos_out[1:2, :] = packed[2][0:1, 0:4]


def window_terms(got, n_dev, n_gx, n_gy, n_gz, bx, by, owner_ref):
    lane = iota((1, CX), 1)
    inside = jnp.logical_and(lane >= WIN, lane < WIN + 3 * PER)
    row = iota((n_dev, CX), 0)
    speed = jnp.zeros((1, CX), F32)
    for delta in range(-2, 3):
        base = ((bx + delta) * n_gy + by) * n_gz
        keep = jnp.logical_and(row >= base, row < base + n_gz)
        part = jnp.sum(jnp.where(keep, got, 0.0), axis=0, keepdims=True)
        part = jnp.broadcast_to(jnp.where(inside, part, 0.0), (8, CX))
        speed = speed + roll(part, delta * PER, 1)[0:1, :]
    speed = jnp.where(inside, speed, 0.0)

    table = owner_ref[...]
    sub = iota(table.shape, 0)
    slots = jnp.zeros((1, CX), jnp.int32)
    for j in range(3):
        column_x = jnp.clip(bx - 1 + j, 0, n_gx - 1)
        first = (column_x * n_gy + by) * PER
        picked = jnp.sum(jnp.where(sub == first // CX, table, 0), axis=0, keepdims=True)
        picked = jnp.broadcast_to(picked, (8, CX))
        moved = pltpu.roll(picked, jnp.bitwise_and(WIN + PER * j - first, CX - 1), 1)[0:1, :]
        here = jnp.logical_and(lane >= WIN + PER * j, lane < WIN + PER * (j + 1))
        slots = jnp.where(here, moved, slots)
    owner = onehot(iota((n_dev, CX), 0) == lax.shift_right_logical(slots, 2))
    which = jnp.bitwise_and(slots, 3)
    found = dots(pieces(got, 3), [owner], TN)
    yaw = jnp.zeros((1, CX), F32)
    ct = jnp.zeros((1, CX), F32)
    for i in range(4):
        yaw = jnp.where(which == i, found[YAW + i:YAW + i + 1, :], yaw)
        ct = jnp.where(which == i, found[YAW + 4 + i:YAW + 5 + i, :], ct)
    cosine, sine, magnitude, force, weighting = turbine_terms(speed, yaw, ct)
    keep = lambda x: jnp.where(inside, x, 0.0)
    return keep(force * cosine), keep(force * sine), keep(weighting)


def edges(pos_ref, dims):
    n_dev, n_gx, n_gy, n_gz = dims
    out = []
    for k, count in enumerate((n_gx, n_gy, n_gz)):
        out.append(jnp.where(pos_ref[k] > 0, 1.0, 0.0))
        out.append(jnp.where(pos_ref[k] < count - 1, 1.0, 0.0))
    return out


def tile_rows(t):
    return slice(H * t, H * t + H)


def south_of(ref, index, t, sub):
    if t > 0:
        return ref[index + (slice(H * t - 1, H * t + H - 1),)]
    return jnp.where(sub == 0, 0.0, roll(ref[index + (tile_rows(0),)], 1, 0))


def north_of(ref, index, t, sub):
    if t < CY // H - 1:
        return ref[index + (slice(H * t + 1, H * t + H + 1),)]
    return jnp.where(sub == H - 1, 0.0, roll(ref[index + (tile_rows(t),)], -1, 0))


def base_kernel(
    dims, pos_ref, fld_ref, index_ref, scale_ref, owner_ref, got_ref,
    pred_ref, dual_ref, field_ref,
):
    n_dev, n_gx, n_gy, n_gz = dims
    bx, by = pos_ref[0], pos_ref[1]
    terms = window_terms(got_ref[...], n_dev, n_gx, n_gy, n_gz, bx, by, owner_ref)
    cells, turbine, weight = index_ref[0:1, :], index_ref[1:2, :], scale_ref[...]
    count = cells.shape[1]
    rows, lanes = entry_onehots(cells)
    in_window = onehot(iota((CX, count), 0) == window_lane(turbine, bx, n_gy))
    stacked = jnp.concatenate([jnp.broadcast_to(t, (8, CX)) for t in terms], axis=0)
    per_entry = dots(pieces(stacked, 2), [in_window], NN)
    for c in range(3):
        value = per_entry[8 * c:8 * c + 1, :] * weight
        if c < 2:
            value = -value
        spread = jnp.where(lanes, value, 0.0)
        field_ref[c] = dots([rows], pieces(spread, 2), NT).reshape(CZ, CY, CX)

    lane = iota((H, CX), 1)
    sub = iota((H, CX), 0)
    zero = jnp.zeros((H, CX), F32)
    for t in range(CY // H):
        at = tile_rows(t)
        for f in range(6):
            out, comp = (pred_ref, f) if f < 3 else (dual_ref, f - 3)
            below, tile = zero, fld_ref[f, 0, at]
            for z in range(CZ):
                above = fld_ref[f, z + 1, at] if z < CZ - 1 else zero
                south, north = south_of(fld_ref, (f, z), t, sub), north_of(fld_ref, (f, z), t, sub)
                west = jnp.where(lane == 0, 0.0, roll(tile, 1, 1))
                east = jnp.where(lane == CX - 1, 0.0, roll(tile, -1, 1))
                lap = (above + below) + (north + south) + (east + west) - 6.0 * tile
                rate = fld_ref[6, z, at] * lap
                rate = rate + (west - tile if f < 3 else east - tile)
                if f < 2:
                    rate = rate + field_ref[f, z, at]
                if f == 3:
                    rate = rate + field_ref[2, z, at]
                out[comp, z, at] = tile + DT * rate
                below, tile = tile, above


def add_faces(f, first, out, given, fld_ref, bounds, xlo_ref, xhi_ref, ylo_ref, yhi_ref, zlo_ref, zhi_ref):
    lo_x, hi_x, lo_y, hi_y, lo_z, hi_z = bounds
    lane = iota((H, CX), 1)
    sub = iota((H, CX), 0)
    flow = f < 3
    comp = f - first
    for t in range(CY // H):
        at = tile_rows(t)
        face_lo, face_hi = xlo_ref[at] * lo_x, xhi_ref[at] * hi_x
        for z in range(CZ):
            spot = f * CZ + z
            west = jnp.where(lane == 0, roll(face_lo, -spot, 1), 0.0)
            east = jnp.where(lane == CX - 1, roll(face_hi, CX - 1 - spot, 1), 0.0)
            lap = west + east
            if t == 0:
                lap = lap + jnp.where(sub == 0, ylo_ref[spot:spot + 1, :] * lo_y, 0.0)
            if t == CY // H - 1:
                lap = lap + jnp.where(sub == H - 1, yhi_ref[spot:spot + 1, :] * hi_y, 0.0)
            if z == 0:
                lap = lap + zlo_ref[f, at] * lo_z
            if z == CZ - 1:
                lap = lap + zhi_ref[f, at] * hi_z
            out[comp, z, at] = given[comp, z, at] + DT * (fld_ref[6, z, at] * lap + (west if flow else east))


def fold_shift(z):
    return H + 16 * (z % 8)


def flow_kernel(
    dims, pos_ref, base_ref, fld_ref, xlo_ref, xhi_ref, ylo_ref, yhi_ref, zlo_ref, zhi_ref,
    pred_ref, dm_ref, ds_ref, xr_ref, xl_ref,
):
    bounds = edges(pos_ref, dims)
    for f in range(3):
        add_faces(f, 0, pred_ref, base_ref, fld_ref, bounds, xlo_ref, xhi_ref, ylo_ref, yhi_ref, zlo_ref, zhi_ref)
    lane = iota((H, CX), 1)
    sub = iota((H, CX), 0)
    zero = jnp.zeros((H, CX), F32)
    for r in range(EY // H):
        at = tile_rows(r)
        t = r - 1
        inside = 0 <= t < CY // H
        for k in range(SZ):
            z = k - 1
            main, side = zero, zero
            if inside and 0 <= z < CZ:
                own = tile_rows(t)
                p0 = pred_ref[0, z, own]
                west, east = roll(p0, 1, 1), roll(p0, -1, 1)
                div = jnp.where(lane == CX - 1, 0.0, east) - jnp.where(lane == 0, 0.0, west)
                div = div + (north_of(pred_ref, (1, z), t, sub) - south_of(pred_ref, (1, z), t, sub))
                if z < CZ - 1:
                    div = div + pred_ref[2, z + 1, own]
                if z > 0:
                    div = div - pred_ref[2, z - 1, own]
                main = 0.5 * div
                side = jnp.where(lane == CX - 1, 0.5 * east, jnp.where(lane == 0, -0.5 * west, 0.0))
            elif inside:
                main = 0.5 * pred_ref[2, 0, tile_rows(t)] if z < 0 else -0.5 * pred_ref[2, CZ - 1, tile_rows(t)]
            elif 0 <= z < CZ and t < 0:
                main = jnp.where(sub == H - 1, 0.5 * roll(pred_ref[1, z, 0:H], -1, 0), 0.0)
            elif 0 <= z < CZ:
                main = jnp.where(sub == 0, -0.5 * roll(pred_ref[1, z, CY - H:CY], 1, 0), 0.0)
            dm_ref[k, at] = main
            ds_ref[k, at] = side
    for r in range(EY // H):
        at = tile_rows(r)
        right, left = [zero] * 3, [zero] * 3
        for k in range(SZ):
            if not 0 < r < EY // H - 1 and not 0 < k < SZ - 1:
                continue
            main, side = dm_ref[k, at], ds_ref[k, at]
            g = k % 8
            mine = jnp.logical_and(lane >= 16 * g, lane < 16 * g + 16)
            right[k // 8] = jnp.where(mine, roll(jnp.where(lane < H, side, main), fold_shift(k), 1), right[k // 8])
            left[k // 8] = jnp.where(mine, roll(jnp.where(lane < H, main, side), fold_shift(k), 1), left[k // 8])
        for i in range(3):
            xr_ref[i, at] = right[i]
            xl_ref[i, at] = left[i]


def dual_kernel(
    dims, pos_ref, yaw_ref, ct_ref, base_ref, fld_ref, got_ref, xlo_ref, xhi_ref, ylo_ref, yhi_ref, zlo_ref, zhi_ref,
    dual_out, yaw_out, pos_out, dual_ref, sems,
):
    bounds = edges(pos_ref, dims)
    copies = []
    for f in range(3, 6):
        add_faces(f, 3, dual_ref, base_ref, fld_ref, bounds, xlo_ref, xhi_ref, ylo_ref, yhi_ref, zlo_ref, zhi_ref)
        copies.append(pltpu.make_async_copy(dual_ref.at[f - 3], dual_out.at[f - 3], sems.at[f - 3]))
        copies[-1].start()
    owner_outputs(got_ref[...], yaw_ref, ct_ref, yaw_out, pos_out)
    for copy in copies:
        copy.wait()


def x_kernel(dims, pos_ref, dm_ref, ds_ref, lo_ref, hi_ref, om_ref, os_ref, up_ref, down_ref):
    in_lo, in_hi = edges(pos_ref, dims)[0:2]
    lane = iota((H, CX), 1)
    head, tail = lane < H, lane >= CX - H
    zero = jnp.zeros((H, CX), F32)
    for r in range(EY // H):
        at = tile_rows(r)
        lows = [lo_ref[i, at] * in_lo for i in range(3)]
        highs = [hi_ref[i, at] * in_hi for i in range(3)]
        for z in range(SZ):
            lo = roll(lows[z // 8], -fold_shift(z), 1)
            hi = roll(highs[z // 8], -fold_shift(z), 1)
            om_ref[z, at] = dm_ref[z, at] + jnp.where(head, lo, jnp.where(tail, hi, 0.0))
            os_ref[z, at] = ds_ref[z, at] + jnp.where(tail, lo, jnp.where(head, hi, 0.0))
    for out, row, edge in ((up_ref, CY, H + CY), (down_ref, H, H - 1)):
        for i in range(3):
            fold = zero
            out[18 + i] = zero
            out[24 + i] = zero
            for g in range(min(8, SZ - 8 * i)):
                z = 8 * i + g
                out[z] = om_ref[z, row:row + H]
                mine = jnp.logical_and(lane >= 16 * g, lane < 16 * g + 16)
                fold = jnp.where(mine, roll(os_ref[z, row:row + H], fold_shift(z), 1), fold)
                out[18 + i, g:g + 1] = om_ref[z, edge:edge + 1]
                out[24 + i, g:g + 1] = os_ref[z, edge:edge + 1]
            out[21 + i] = fold


def y_kernel(dims, pos_ref, dm_ref, ds_ref, lo_ref, hi_ref, om_ref, os_ref, up_ref, down_ref):
    in_lo, in_hi = edges(pos_ref, dims)[2:4]
    lane = iota((H, CX), 1)
    sub = iota((H, CX), 0)
    ends = jnp.logical_or(lane < H, lane >= CX - H)
    zero = jnp.zeros((H, CX), F32)
    last = EY // H - 1
    for r in range(EY // H):
        at = tile_rows(r)
        up_fold, down_fold = zero, zero
        for z in range(SZ):
            tile, g = z // 8, z % 8
            main, side = dm_ref[z, at], ds_ref[z, at]
            if r == 0:
                main = main + lo_ref[z] * in_lo
                side = side + jnp.where(ends, roll(lo_ref[21 + tile], -fold_shift(z), 1) * in_lo, 0.0)
            if r == 1:
                main = main + jnp.where(sub == 0, lo_ref[18 + tile, g:g + 1, :] * in_lo, 0.0)
                side = side + jnp.where(sub == 0, lo_ref[24 + tile, g:g + 1, :] * in_lo, 0.0)
            if r == last - 1:
                main = main + jnp.where(sub == H - 1, hi_ref[18 + tile, g:g + 1, :] * in_hi, 0.0)
                side = side + jnp.where(sub == H - 1, hi_ref[24 + tile, g:g + 1, :] * in_hi, 0.0)
            if r == last:
                main = main + hi_ref[z] * in_hi
                side = side + jnp.where(ends, roll(hi_ref[21 + tile], -fold_shift(z), 1) * in_hi, 0.0)
            om_ref[z, at] = main
            os_ref[z, at] = side
            if z >= CZ - H + 1:
                i = z - (CZ - H + 1)
                up_ref[i, at] = main
                shift = 14 * i + 7 if i < H else 120
                mine = jnp.logical_and(lane >= 14 * i, lane < (14 * i + 14 if i < H else CX))
                up_fold = jnp.where(mine, roll(side, shift, 1), up_fold)
            if z <= H:
                i = z - 1 if z > 0 else H
                down_ref[i, at] = main
                shift = 14 * i + 7 if i < H else 120
                mine = jnp.logical_and(lane >= 14 * i, lane < (14 * i + 14 if i < H else CX))
                down_fold = jnp.where(mine, roll(side, shift, 1), down_fold)
        up_ref[H + 1, at] = up_fold
        down_ref[H + 1, at] = down_fold


def pre_planes(level):
    return (H + 1 + level, H + CZ - 1 - level) if level < SWEEPS - 1 else (0, 0)


def pre_index(level, z):
    return sum(CZ - 2 - 2 * i for i in range(level)) + z - pre_planes(level)[0]


PRE = sum(CZ - 2 - 2 * i for i in range(SWEEPS - 1))


def padded_rows(t, shift=0):
    return slice(PADR + H * t + shift, PADR + H * t + H + shift)


def coefficients(pos_ref, dims):
    lo_x, hi_x, lo_y, hi_y, lo_z, hi_z = edges(pos_ref, dims)
    lane = iota((H, CX), 1)
    low, high = jnp.where(lane >= CX - H, lo_x, 1.0), jnp.where(lane < H, hi_x, 1.0)
    main = [jnp.full((H, CX), 1.0 / 6.0, F32)] * TILES
    main[0] = main[0] * lo_y
    main[-1] = main[-1] * hi_y
    return main, [c * (low * high) for c in main]


def relax(planes, get, put, rhs, weights):
    lane = iota((H, CX), 1)
    first, last = lane == 0, lane == CX - 1
    z0 = planes[0]
    carry = [[get(k, z0 - 1 + i, padded_rows(t)) for k in range(2) for i in range(2)] for t in range(TILES)]
    for z in planes:
        main_weight, side_weight = weights(z)
        for t in range(TILES):
            below, main, side_below, side = carry[t]
            at, up, down = padded_rows(t), padded_rows(t, 1), padded_rows(t, -1)
            above, side_above = get(0, z + 1, at), get(1, z + 1, at)
            main_w, side_w = roll(main, 1, 1), roll(side, 1, 1)
            main_e, side_e = roll(main, -1, 1), roll(side, -1, 1)
            total = (above + below) + (get(0, z, up) + get(0, z, down))
            total = total + (jnp.where(first, side_w, main_w) + jnp.where(last, side_e, main_e))
            put(0, z, at, (total - rhs(0, z, tile_rows(t))) * main_weight[t])
            total = (side_above + side_below) + (get(1, z, up) + get(1, z, down))
            total = total + (jnp.where(first, main_w, side_w) + jnp.where(last, main_e, side_e))
            put(1, z, at, (total - rhs(1, z, tile_rows(t))) * side_weight[t])
            carry[t] = [main, above, side, side_above]


def inner_kernel(dims, pos_ref, dm_ref, ds_ref, pre_ref):
    main_coef, side_coef = coefficients(pos_ref, dims)
    scale = 1.0 / DT
    zero = jnp.zeros((H, CX), F32)
    for i in range(PRE):
        for part in range(2):
            pre_ref[i, part, 0:PADR] = zero
            pre_ref[i, part, PADR + EY:PADR + EY + PADR] = zero

    def rhs(part, z, rows):
        return (ds_ref if part else dm_ref)[z - H + 1, rows] * scale

    for z in range(*pre_planes(0)):
        for t in range(TILES):
            pre_ref[pre_index(0, z), 0, padded_rows(t)] = -rhs(0, z, tile_rows(t)) * main_coef[t]
            pre_ref[pre_index(0, z), 1, padded_rows(t)] = -rhs(1, z, tile_rows(t)) * side_coef[t]
    for level in range(1, SWEEPS - 1):
        def get(part, z, rows, level=level):
            return pre_ref[pre_index(level - 1, z), part, rows]

        def put(part, z, rows, value, level=level):
            pre_ref[pre_index(level, z), part, rows] = value

        relax(range(*pre_planes(level)), get, put, rhs, lambda z: (main_coef, side_coef))


def sweep_kernel(
    dims, pos_ref, dm_ref, ds_ref, pre_ref, lo_ref, hi_ref, pred_ref, pres_ref, vel_out, pres_out,
    b_ref, phi_ref, vel_buf, pres_buf, sems,
):
    lo_z, hi_z = edges(pos_ref, dims)[4:6]
    main_coef, side_coef = coefficients(pos_ref, dims)
    scale = 1.0 / DT
    lane = iota((H, CX), 1)
    first, last = lane == 0, lane == CX - 1
    zero = jnp.zeros((H, CX), F32)
    near = jnp.logical_or(lane < H - 1, lane >= CX - H + 1)
    ends = jnp.logical_or(lane < H, lane >= CX - H)
    lo_scale, hi_scale = lo_z * scale, hi_z * scale
    low_coef = [[c * lo_z for c in main_coef], [c * lo_z for c in side_coef]]
    high_coef = [[c * hi_z for c in main_coef], [c * hi_z for c in side_coef]]

    def weights(z):
        return low_coef if z < H else high_coef if z >= H + CZ else (main_coef, side_coef)

    outer = list(range(pre_planes(0)[0])) + list(range(pre_planes(0)[1], EZ))
    place = {z: i for i, z in enumerate(outer)}

    for z in range(EZ):
        for part in range(2):
            for buf in range(2):
                phi_ref[buf, part, z, 0:PADR] = zero
                phi_ref[buf, part, z, PADR + EY:PADR + EY + PADR] = zero
    for t in range(TILES):
        rows = tile_rows(t)
        folded = (lo_ref[H + 1, rows] * lo_scale, hi_ref[H + 1, rows] * hi_scale)
        for z in outer:
            low = z < EZ // 2
            halo, fold, factor = (lo_ref, folded[0], lo_scale) if low else (hi_ref, folded[1], hi_scale)
            if z < H or z >= H + CZ:
                g = z if low else z - H - CZ
                main = halo[g, rows] * factor
                side = jnp.where(near, roll(fold, -(14 * g + 7), 1), 0.0)
                if z in (H - 1, H + CZ):
                    k = 0 if low else SZ - 1
                    main = main + dm_ref[k, rows] * factor
                    side = side + ds_ref[k, rows] * factor
            else:
                main = dm_ref[z - H + 1, rows] * scale + halo[H, rows] * factor
                side = ds_ref[z - H + 1, rows] * scale + jnp.where(ends, roll(fold, -120, 1), 0.0)
            b_ref[0, place[z], rows] = main
            b_ref[1, place[z], rows] = side
            cm, cs = weights(z)
            phi_ref[0, 0, z, padded_rows(t)] = -main * cm[t]
            phi_ref[0, 1, z, padded_rows(t)] = -side * cs[t]

    def rhs(part, z, rows):
        if z in place:
            return b_ref[part, place[z], rows]
        return (ds_ref if part else dm_ref)[z - H + 1, rows] * scale

    def reader(level):
        known = range(*pre_planes(level))

        def get(part, z, rows):
            if z in known:
                return pre_ref[pre_index(level, z), part, rows]
            return phi_ref[level % 2, part, z, rows]

        return get

    for level in range(1, SWEEPS):
        lo, hi = pre_planes(level)

        def put(part, z, rows, value, level=level):
            phi_ref[level % 2, part, z, rows] = value

        runs = ((level, lo), (hi, EZ - level)) if hi > lo else ((level, EZ - level),)
        for run in runs:
            relax(range(*run), reader(level - 1), put, rhs, weights)

    get = reader(SWEEPS - 1)
    chunk = 4
    copies = []
    for c in range(CZ // chunk):
        for z in range(c * chunk, (c + 1) * chunk):
            for t in range(CY // H):
                rows = tile_rows(t)
                at, up, down = padded_rows(t + 1), padded_rows(t + 1, 1), padded_rows(t + 1, -1)
                main, side = get(0, z + H, at), get(1, z + H, at)
                west = jnp.where(first, roll(side, 1, 1), roll(main, 1, 1))
                east = jnp.where(last, roll(side, -1, 1), roll(main, -1, 1))
                half = DT * 0.5
                vel_buf[0, z, rows] = pred_ref[0, z, rows] - half * (east - west)
                vel_buf[1, z, rows] = pred_ref[1, z, rows] - half * (get(0, z + H, up) - get(0, z + H, down))
                vel_buf[2, z, rows] = pred_ref[2, z, rows] - half * (get(0, z + H + 1, at) - get(0, z + H - 1, at))
                pres_buf[z, rows] = pres_ref[z, rows] + main
        part = pl.ds(c * chunk, chunk)
        copies.append(pltpu.make_async_copy(vel_buf.at[:, part], vel_out.at[:, part], sems.at[2 * c]))
        copies.append(pltpu.make_async_copy(pres_buf.at[part], pres_out.at[part], sems.at[2 * c + 1]))
        for copy in copies[-2:]:
            copy.start()
    for copy in copies:
        copy.wait()


def swap(up, down, axis):
    count = lax.axis_size(axis)
    forward = [(i, (i + 1) % count) for i in range(count)]
    backward = [(j, i) for i, j in forward]
    return lax.ppermute(up, axis, forward), lax.ppermute(down, axis, backward)


def shape(*dims):
    return jax.ShapeDtypeStruct(dims, F32)


SMEM = pl.BlockSpec(memory_space=pltpu.SMEM)
VMEM = pl.BlockSpec(memory_space=pltpu.VMEM)


ANY = pl.BlockSpec(memory_space=pl.ANY)


def in_hbm(x):
    return pltpu.with_memory_space_constraint(x, pltpu.HBM)


def in_vmem(*dims, dtype=F32):
    return pltpu.VMEM(dims, dtype)


MIB = 1024 * 1024
ENTRY_LIMIT = 24


class Place:
    def __getitem__(self, k):
        return lax.axis_index(("gx", "gy", "gz")[k])


def call(kernel, scalars, arrays, outs, scratch=(), in_specs=None, out_specs=None, limit=24, cost=0):
    return pl.pallas_call(
        functools.partial(kernel, Place()),
        out_shape=outs,
        in_specs=[SMEM] * len(scalars) + list(in_specs or [VMEM] * len(arrays)),
        out_specs=out_specs or [VMEM] * len(outs),
        scratch_shapes=list(scratch),
        compiler_params=pltpu.CompilerParams(vmem_limit_bytes=limit * MIB),
        cost_estimate=pl.CostEstimate(flops=cost, bytes_accessed=cost // 64, transcendentals=0) if cost else None,
    )(*scalars, *arrays)


def shards(
    velocity, adjoint, pressure, viscosity, disk_cells, disk_turbine, disk_weight, disk_dweight, yaw, thrust_coef, owner_slot,
):
    axes = ("gx", "gy", "gz")
    n_gx, n_gy, n_gz = (lax.axis_size(a) for a in axes)
    n_dev = n_gx * n_gy * n_gz
    dims = (n_dev, n_gx, n_gy, n_gz)
    turbines = owner_slot.shape[0]
    if turbines % CX:
        owner_slot = jnp.pad(owner_slot, (0, CX - turbines % CX))
    owner = owner_slot.reshape(-1, CX)
    cells, turbine, weight = (a.reshape(1, -1) for a in (disk_cells, disk_turbine, disk_weight))

    payload, xr, xl, yr, yl, zr, zl, fields, index, scale, table = call(
        functools.partial(entry_kernel, n_dev, n_gy),
        (in_hbm(yaw), in_hbm(thrust_coef)),
        tuple(in_hbm(a) for a in (velocity, adjoint, viscosity, cells, turbine, weight, disk_dweight, owner)),
        (
            shape(n_dev, CX), in_vmem(CY, CX), in_vmem(CY, CX), in_vmem(6 * CZ, CX), in_vmem(6 * CZ, CX),
            in_vmem(6, CY, CX), in_vmem(6, CY, CX), in_vmem(7, CZ, CY, CX), in_vmem(2, cells.shape[1], dtype=jnp.int32),
            in_vmem(*weight.shape), in_vmem(*owner.shape, dtype=jnp.int32),
        ),
        (pltpu.VMEM((n_dev, CX), F32), pltpu.SemaphoreType.DMA((8,))),
        [ANY, ANY, ANY] + [VMEM] * 5,
        [ANY] + [VMEM] * 10,
        limit=ENTRY_LIMIT,
    )
    got = lax.all_to_all(payload, axes, 0, 0, tiled=True)
    xlo, xhi = swap(xr, xl, "gx")
    ylo, yhi = swap(yr, yl, "gy")
    xlo, zl = lax.optimization_barrier((xlo, zl))
    zlo, zhi = swap(zr, zl, "gz")
    faces = (xlo, xhi, ylo, yhi, zlo, zhi)

    pred_base, dual_base = call(
        functools.partial(base_kernel, dims),
        (),
        (fields, index, scale, table, got),
        (shape(3, CZ, CY, CX), shape(3, CZ, CY, CX)),
        (pltpu.VMEM((3, CZ, CY, CX), F32),),
        cost=1 << 30,
    )
    predicted, dm, ds, xr, xl = call(
        functools.partial(flow_kernel, dims),
        (),
        (pred_base, fields) + faces,
        (shape(3, CZ, CY, CX), shape(SZ, EY, CX), shape(SZ, EY, CX), shape(3, EY, CX), shape(3, EY, CX)),
    )
    adjoint_next, yaw_grad, position_grad = call(
        functools.partial(dual_kernel, dims),
        (in_hbm(yaw), in_hbm(thrust_coef)),
        (dual_base, fields, got) + faces,
        (shape(3, CZ, CY, CX), shape(1, 4), shape(2, 4)),
        (pltpu.VMEM((3, CZ, CY, CX), F32), pltpu.SemaphoreType.DMA((3,))),
        out_specs=[ANY, VMEM, VMEM],
        cost=1 << 30,
    )
    lo, hi = swap(xr, xl, "gx")
    dm, ds, up, down = call(
        functools.partial(x_kernel, dims), (), (dm, ds, lo, hi),
        (shape(SZ, EY, CX), shape(SZ, EY, CX), shape(27, H, CX), shape(27, H, CX)),
    )
    lo, hi = swap(up, down, "gy")
    lo, yaw_grad = lax.optimization_barrier((lo, yaw_grad))
    dm, ds, up, down = call(
        functools.partial(y_kernel, dims), (), (dm, ds, lo, hi),
        (shape(SZ, EY, CX), shape(SZ, EY, CX), shape(H + 2, EY, CX), shape(H + 2, EY, CX)),
    )
    lo, hi = swap(up, down, "gz")
    pre = call(
        functools.partial(inner_kernel, dims), (), (dm, ds), (shape(PRE, 2, EY + 2 * PADR, CX),), cost=1 << 30
    )[0]
    velocity_next, pressure_next = call(
        functools.partial(sweep_kernel, dims), (), (dm, ds, pre, lo, hi, predicted, pressure),
        (shape(3, CZ, CY, CX), shape(CZ, CY, CX)),
        (
            pltpu.VMEM((2, EZ - CZ + 2, EY, CX), F32), pltpu.VMEM((2, 2, EZ, EY + 2 * PADR, CX), F32),
            pltpu.VMEM((3, CZ, CY, CX), F32), pltpu.VMEM((CZ, CY, CX), F32), pltpu.SemaphoreType.DMA((8,)),
        ),
        out_specs=[ANY, ANY],
    )
    return velocity_next, adjoint_next, pressure_next, yaw_grad.reshape(-1), position_grad


def solution(mesh):
    axes = ("gx", "gy", "gz")
    grid = P(None, "gz", "gy", "gx")
    cell = P("gz", "gy", "gx")
    flat = P(axes)
    return jax.shard_map(
        shards,
        mesh=mesh,
        in_specs=(grid, grid, cell, cell, flat, flat, flat, P(None, axes), flat, flat, P()),
        out_specs=(grid, grid, cell, flat, P(None, axes)),
        check_vma=False,
    )
```

```python
import functools

import jax
import jax.numpy as jnp
from jax import lax
from jax.experimental import pallas as pl
from jax.experimental.pallas import tpu as pltpu
from jax.sharding import PartitionSpec as P

SWEEPS = 8
DT = 0.2
F32 = jnp.float32
BF16 = jnp.bfloat16
CZ, CY, CX = 16, 32, 128
KJ = CZ * CY
H = 8
EZ, EY = CZ + 2 * H, CY + 2 * H
SZ = CZ + 2
TILES = EY // H
PADR = 8
PER = 16
WIN = 64
YAW = 112
NN = (((1,), (0,)), ((), ()))
NT = (((1,), (1,)), ((), ()))
TN = (((0,), (0,)), ((), ()))


def iota(shape, dim):
    return lax.broadcasted_iota(jnp.int32, shape, dim)


def pieces(x, count):
    parts = []
    for _ in range(count):
        head = x.astype(BF16)
        parts.append(head)
        x = x - head.astype(F32)
    return parts


def dots(left, right, dims):
    total = None
    for a in left:
        for b in right:
            term = lax.dot_general(a, b, dims, preferred_element_type=F32)
            total = term if total is None else total + term
    return total


def onehot(mask):
    return jnp.where(mask, 1.0, 0.0).astype(BF16)


def roll(x, shift, axis):
    return pltpu.roll(x, shift % x.shape[axis], axis)


def entry_onehots(cells):
    row = lax.shift_right_logical(cells, 7)
    lane = jnp.bitwise_and(cells, CX - 1)
    count = cells.shape[1]
    rows = onehot(iota((KJ, count), 0) == row)
    lanes = iota((CX, count), 0) == lane
    return rows, lanes


def window_lane(turbine, bx, n_gy):
    column_x = lax.shift_right_logical(turbine, 4) // n_gy
    return WIN + (column_x - bx + 1) * PER + jnp.bitwise_and(turbine, PER - 1)


def lookup(table_ref, turbine):
    count = turbine.shape[1]
    table = table_ref[...]
    owner = lax.shift_right_logical(table, 2).astype(F32)
    which = jnp.bitwise_and(table, 3).astype(F32)
    rows = table.shape[0]
    high = lax.shift_right_logical(turbine, 7)
    low = onehot(iota((CX, count), 0) == jnp.bitwise_and(turbine, CX - 1))
    keep = iota((rows, count), 0) == high
    out = []
    for part in (owner, which):
        picked = dots([part.astype(BF16)], [low], NN)
        picked = jnp.sum(jnp.where(keep, picked, 0.0), axis=0, keepdims=True)
        out.append(picked.astype(jnp.int32))
    return out


def entry_kernel(
    n_dev, n_gy, pos_ref, yaw_ref, ct_ref, vel_hbm, adj_hbm, visc_hbm, cells_ref, turb_ref, weight_ref, dweight_ref, owner_ref,
    pay_ref, xr_ref, xl_ref, yr_ref, yl_ref, zr_ref, zl_ref, fld_ref, index_ref, scale_ref, table_ref, out_ref, sems,
):
    order = (0, 3, 4, 1, 2, 5, 6)
    copies = {}
    for f in order:
        hbm = vel_hbm.at[f] if f < 3 else adj_hbm.at[f - 3] if f < 6 else visc_hbm
        copies[f] = pltpu.make_async_copy(hbm, fld_ref.at[f], sems.at[f])
        copies[f].start()
    bx = pos_ref[0]
    cells, turbine, weight = cells_ref[...], turb_ref[...], weight_ref[...]
    index_ref[0:1, :] = cells
    index_ref[1:2, :] = turbine
    scale_ref[...] = weight
    table_ref[...] = owner_ref[...]
    count = cells.shape[1]
    rows, lanes = entry_onehots(cells)
    owner, which = lookup(owner_ref, turbine)
    to_owner = onehot(iota((n_dev, count), 0) == owner)
    in_window = onehot(iota((CX, count), 0) == window_lane(turbine, bx, n_gy))

    columns = []
    for f in order[:3]:
        copies[f].wait()
        columns += pieces(fld_ref[f].reshape(KJ, CX), 2)
    at_row = dots([jnp.concatenate(columns, axis=1)], [rows], TN)
    gathered = []
    for k in range(3):
        both = at_row[2 * k * CX:(2 * k + 1) * CX] + at_row[(2 * k + 1) * CX:(2 * k + 2) * CX]
        gathered.append(jnp.sum(jnp.where(lanes, both, 0.0), axis=0, keepdims=True))
    factors = [weight, dweight_ref[0:1, :], dweight_ref[1:2, :]]
    values = [f * g for f in factors for g in gathered]

    sub = iota((PER, count), 0)
    stacked = jnp.zeros((PER, count), F32)
    for v, value in enumerate(values):
        stacked = jnp.where(sub == v, value, stacked)
    per_slot = jnp.concatenate(
        [jnp.where(which == i, stacked, 0.0) for i in range(4)] + [jnp.zeros((CX - 4 * PER, count), F32)], axis=0
    )
    payload = dots([to_owner], pieces(per_slot, 2), NT)

    speed = jnp.broadcast_to(values[0], (8, count))
    shared = dots(pieces(speed, 2), [in_window], NT)[0:1, :]
    lane = iota((1, CX), 1)
    for i in range(4):
        shared = jnp.where(lane == YAW + i, yaw_ref[i], shared)
        shared = jnp.where(lane == YAW + 4 + i, ct_ref[i], shared)
    out_ref[...] = payload + shared
    leaving = pltpu.make_async_copy(out_ref, pay_ref, sems.at[7])
    leaving.start()

    for f in order[3:]:
        copies[f].wait()
    lane = iota((H, CX), 1)
    for t in range(CY // H):
        at = slice(H * t, H * t + H)
        right = jnp.zeros((H, CX), F32)
        left = jnp.zeros((H, CX), F32)
        for f in range(6):
            for z in range(CZ):
                tile = fld_ref[f, z, at]
                spot = lane == f * CZ + z
                right = jnp.where(spot, roll(tile, f * CZ + z + 1, 1), right)
                left = jnp.where(spot, roll(tile, f * CZ + z, 1), left)
        xr_ref[at] = right
        xl_ref[at] = left
    for f in range(6):
        yr_ref[f * CZ:(f + 1) * CZ, :] = fld_ref[f, :, CY - 1, :]
        yl_ref[f * CZ:(f + 1) * CZ, :] = fld_ref[f, :, 0, :]
        zr_ref[f] = fld_ref[f, CZ - 1]
        zl_ref[f] = fld_ref[f, 0]
    leaving.wait()


def turbine_terms(speed, yaw, thrust_coef):
    cosine = jnp.cos(yaw)
    sine = jnp.sin(yaw)
    magnitude = jnp.abs(speed)
    force = 0.5 * thrust_coef * speed * magnitude * cosine * cosine
    weighting = 1.5 * thrust_coef * speed * magnitude * cosine * cosine * cosine
    return cosine, sine, magnitude, force, weighting


def owner_outputs(got, yaw_ref, ct_ref, yaw_out, pos_out):
    total = jnp.sum(got, axis=0, keepdims=True)
    total = jnp.broadcast_to(total, (8, CX))
    lane = iota((8, CX), 1)
    yaw = jnp.zeros((8, CX), F32)
    ct = jnp.zeros((8, CX), F32)
    for i in range(4):
        yaw = jnp.where(lane == i * PER, yaw_ref[i], yaw)
        ct = jnp.where(lane == i * PER, ct_ref[i], ct)

    def at(v):
        return roll(total, -v, 1)

    speed, dual_x, dual_y = total, at(1), at(2)
    cosine, sine, magnitude, force, weighting = turbine_terms(speed, yaw, ct)
    yaw_grad = -1.5 * ct * magnitude * magnitude * magnitude * cosine * cosine * sine + force * (
        sine * dual_x - cosine * dual_y
    )
    grads = [yaw_grad]
    for r in range(2):
        grads.append(weighting * at(3 + 3 * r) - force * cosine * at(4 + 3 * r) - force * sine * at(5 + 3 * r))
    packed = []
    for grad in grads:
        out = jnp.zeros((8, CX), F32)
        for i in range(4):
            out = jnp.where(lane == i, roll(grad, -(PER - 1) * i, 1), out)
        packed.append(out)
    yaw_out[...] = packed[0][0:1, 0:4]
    pos_out[0:1, :] = packed[1][0:1, 0:4]
    pos_out[1:2, :] = packed[2][0:1, 0:4]


def window_terms(got, n_dev, n_gx, n_gy, n_gz, bx, by, owner_ref):
    lane = iota((1, CX), 1)
    inside = jnp.logical_and(lane >= WIN, lane < WIN + 3 * PER)
    row = iota((n_dev, CX), 0)
    speed = jnp.zeros((1, CX), F32)
    for delta in range(-2, 3):
        base = ((bx + delta) * n_gy + by) * n_gz
        keep = jnp.logical_and(row >= base, row < base + n_gz)
        part = jnp.sum(jnp.where(keep, got, 0.0), axis=0, keepdims=True)
        part = jnp.broadcast_to(jnp.where(inside, part, 0.0), (8, CX))
        speed = speed + roll(part, delta * PER, 1)[0:1, :]
    speed = jnp.where(inside, speed, 0.0)

    table = owner_ref[...]
    sub = iota(table.shape, 0)
    slots = jnp.zeros((1, CX), jnp.int32)
    for j in range(3):
        column_x = jnp.clip(bx - 1 + j, 0, n_gx - 1)
        first = (column_x * n_gy + by) * PER
        picked = jnp.sum(jnp.where(sub == first // CX, table, 0), axis=0, keepdims=True)
        picked = jnp.broadcast_to(picked, (8, CX))
        moved = pltpu.roll(picked, jnp.bitwise_and(WIN + PER * j - first, CX - 1), 1)[0:1, :]
        here = jnp.logical_and(lane >= WIN + PER * j, lane < WIN + PER * (j + 1))
        slots = jnp.where(here, moved, slots)
    owner = onehot(iota((n_dev, CX), 0) == lax.shift_right_logical(slots, 2))
    which = jnp.bitwise_and(slots, 3)
    found = dots(pieces(got, 3), [owner], TN)
    yaw = jnp.zeros((1, CX), F32)
    ct = jnp.zeros((1, CX), F32)
    for i in range(4):
        yaw = jnp.where(which == i, found[YAW + i:YAW + i + 1, :], yaw)
        ct = jnp.where(which == i, found[YAW + 4 + i:YAW + 5 + i, :], ct)
    cosine, sine, magnitude, force, weighting = turbine_terms(speed, yaw, ct)
    keep = lambda x: jnp.where(inside, x, 0.0)
    return keep(force * cosine), keep(force * sine), keep(weighting)


def edges(pos_ref, dims):
    n_dev, n_gx, n_gy, n_gz = dims
    out = []
    for k, count in enumerate((n_gx, n_gy, n_gz)):
        out.append(jnp.where(pos_ref[k] > 0, 1.0, 0.0))
        out.append(jnp.where(pos_ref[k] < count - 1, 1.0, 0.0))
    return out


def tile_rows(t):
    return slice(H * t, H * t + H)


def south_of(ref, index, t, sub):
    if t > 0:
        return ref[index + (slice(H * t - 1, H * t + H - 1),)]
    return jnp.where(sub == 0, 0.0, roll(ref[index + (tile_rows(0),)], 1, 0))


def north_of(ref, index, t, sub):
    if t < CY // H - 1:
        return ref[index + (slice(H * t + 1, H * t + H + 1),)]
    return jnp.where(sub == H - 1, 0.0, roll(ref[index + (tile_rows(t),)], -1, 0))


def force_kernel(dims, pos_ref, index_ref, scale_ref, owner_ref, got_ref, field_ref):
    n_dev, n_gx, n_gy, n_gz = dims
    bx, by = pos_ref[0], pos_ref[1]
    terms = window_terms(got_ref[...], n_dev, n_gx, n_gy, n_gz, bx, by, owner_ref)
    cells, turbine, weight = index_ref[0:1, :], index_ref[1:2, :], scale_ref[...]
    count = cells.shape[1]
    rows, lanes = entry_onehots(cells)
    in_window = onehot(iota((CX, count), 0) == window_lane(turbine, bx, n_gy))
    stacked = jnp.concatenate([jnp.broadcast_to(t, (8, CX)) for t in terms], axis=0)
    per_entry = dots(pieces(stacked, 2), [in_window], NN)
    for c in range(3):
        value = per_entry[8 * c:8 * c + 1, :] * weight
        if c < 2:
            value = -value
        spread = jnp.where(lanes, value, 0.0)
        field_ref[c] = dots([rows], pieces(spread, 2), NT).reshape(CZ, CY, CX)


def stencil_kernel(pos_ref, fld_ref, pred_ref, dual_ref):
    lane = iota((H, CX), 1)
    sub = iota((H, CX), 0)
    zero = jnp.zeros((H, CX), F32)
    for t in range(CY // H):
        at = tile_rows(t)
        for f in range(6):
            out, comp = (pred_ref, f) if f < 3 else (dual_ref, f - 3)
            below, tile = zero, fld_ref[f, 0, at]
            for z in range(CZ):
                above = fld_ref[f, z + 1, at] if z < CZ - 1 else zero
                south, north = south_of(fld_ref, (f, z), t, sub), north_of(fld_ref, (f, z), t, sub)
                west = jnp.where(lane == 0, 0.0, roll(tile, 1, 1))
                east = jnp.where(lane == CX - 1, 0.0, roll(tile, -1, 1))
                lap = (above + below) + (north + south) + (east + west) - 6.0 * tile
                rate = fld_ref[6, z, at] * lap + (west - tile if f < 3 else east - tile)
                out[comp, z, at] = tile + DT * rate
                below, tile = tile, above


def add_faces(f, first, out, given, field_ref, fld_ref, bounds, xlo_ref, xhi_ref, ylo_ref, yhi_ref, zlo_ref, zhi_ref):
    lo_x, hi_x, lo_y, hi_y, lo_z, hi_z = bounds
    lane = iota((H, CX), 1)
    sub = iota((H, CX), 0)
    flow = f < 3
    comp = f - first
    for t in range(CY // H):
        at = tile_rows(t)
        face_lo, face_hi = xlo_ref[at] * lo_x, xhi_ref[at] * hi_x
        for z in range(CZ):
            spot = f * CZ + z
            west = jnp.where(lane == 0, roll(face_lo, -spot, 1), 0.0)
            east = jnp.where(lane == CX - 1, roll(face_hi, CX - 1 - spot, 1), 0.0)
            lap = west + east
            if t == 0:
                lap = lap + jnp.where(sub == 0, ylo_ref[spot:spot + 1, :] * lo_y, 0.0)
            if t == CY // H - 1:
                lap = lap + jnp.where(sub == H - 1, yhi_ref[spot:spot + 1, :] * hi_y, 0.0)
            if z == 0:
                lap = lap + zlo_ref[f, at] * lo_z
            if z == CZ - 1:
                lap = lap + zhi_ref[f, at] * hi_z
            rate = fld_ref[6, z, at] * lap + (west if flow else east)
            if f < 2:
                rate = rate + field_ref[f, z, at]
            if f == 3:
                rate = rate + field_ref[2, z, at]
            out[comp, z, at] = given[comp, z, at] + DT * rate


def fold_shift(z):
    return H + 16 * (z % 8)


def flow_kernel(
    dims, pos_ref, base_ref, field_ref, fld_ref, xlo_ref, xhi_ref, ylo_ref, yhi_ref, zlo_ref, zhi_ref,
    pred_ref, dm_ref, ds_ref, xr_ref, xl_ref,
):
    bounds = edges(pos_ref, dims)
    for f in range(3):
        add_faces(f, 0, pred_ref, base_ref, field_ref, fld_ref, bounds, xlo_ref, xhi_ref, ylo_ref, yhi_ref, zlo_ref, zhi_ref)
    lane = iota((H, CX), 1)
    sub = iota((H, CX), 0)
    zero = jnp.zeros((H, CX), F32)
    for r in range(EY // H):
        at = tile_rows(r)
        t = r - 1
        inside = 0 <= t < CY // H
        for k in range(SZ):
            z = k - 1
            main, side = zero, zero
            if inside and 0 <= z < CZ:
                own = tile_rows(t)
                p0 = pred_ref[0, z, own]
                west, east = roll(p0, 1, 1), roll(p0, -1, 1)
                div = jnp.where(lane == CX - 1, 0.0, east) - jnp.where(lane == 0, 0.0, west)
                div = div + (north_of(pred_ref, (1, z), t, sub) - south_of(pred_ref, (1, z), t, sub))
                if z < CZ - 1:
                    div = div + pred_ref[2, z + 1, own]
                if z > 0:
                    div = div - pred_ref[2, z - 1, own]
                main = 0.5 * div
                side = jnp.where(lane == CX - 1, 0.5 * east, jnp.where(lane == 0, -0.5 * west, 0.0))
            elif inside:
                main = 0.5 * pred_ref[2, 0, tile_rows(t)] if z < 0 else -0.5 * pred_ref[2, CZ - 1, tile_rows(t)]
            elif 0 <= z < CZ and t < 0:
                main = jnp.where(sub == H - 1, 0.5 * roll(pred_ref[1, z, 0:H], -1, 0), 0.0)
            elif 0 <= z < CZ:
                main = jnp.where(sub == 0, -0.5 * roll(pred_ref[1, z, CY - H:CY], 1, 0), 0.0)
            dm_ref[k, at] = main
            ds_ref[k, at] = side
    for r in range(EY // H):
        at = tile_rows(r)
        right, left = [zero] * 3, [zero] * 3
        for k in range(SZ):
            if not 0 < r < EY // H - 1 and not 0 < k < SZ - 1:
                continue
            main, side = dm_ref[k, at], ds_ref[k, at]
            g = k % 8
            mine = jnp.logical_and(lane >= 16 * g, lane < 16 * g + 16)
            right[k // 8] = jnp.where(mine, roll(jnp.where(lane < H, side, main), fold_shift(k), 1), right[k // 8])
            left[k // 8] = jnp.where(mine, roll(jnp.where(lane < H, main, side), fold_shift(k), 1), left[k // 8])
        for i in range(3):
            xr_ref[i, at] = right[i]
            xl_ref[i, at] = left[i]


def dual_kernel(
    dims, pos_ref, yaw_ref, ct_ref, base_ref, field_ref, fld_ref, got_ref, xlo_ref, xhi_ref, ylo_ref, yhi_ref, zlo_ref, zhi_ref,
    dual_out, yaw_out, pos_out, dual_ref, sems,
):
    bounds = edges(pos_ref, dims)
    copies = []
    for f in range(3, 6):
        add_faces(f, 3, dual_ref, base_ref, field_ref, fld_ref, bounds, xlo_ref, xhi_ref, ylo_ref, yhi_ref, zlo_ref, zhi_ref)
        copies.append(pltpu.make_async_copy(dual_ref.at[f - 3], dual_out.at[f - 3], sems.at[f - 3]))
        copies[-1].start()
    owner_outputs(got_ref[...], yaw_ref, ct_ref, yaw_out, pos_out)
    for copy in copies:
        copy.wait()


def x_kernel(
    dims, pos_ref, dm_ref, ds_ref, lo_ref, hi_ref, om_ref, os_ref, up_ref, down_ref, above_ref, below_ref
):
    in_lo, in_hi = edges(pos_ref, dims)[0:2]
    lane = iota((H, CX), 1)
    head, tail = lane < H, lane >= CX - H
    zero = jnp.zeros((H, CX), F32)
    for r in range(EY // H):
        at = tile_rows(r)
        lows = [lo_ref[i, at] * in_lo for i in range(3)]
        highs = [hi_ref[i, at] * in_hi for i in range(3)]
        for z in range(SZ):
            lo = roll(lows[z // 8], -fold_shift(z), 1)
            hi = roll(highs[z // 8], -fold_shift(z), 1)
            om_ref[z, at] = dm_ref[z, at] + jnp.where(head, lo, jnp.where(tail, hi, 0.0))
            os_ref[z, at] = ds_ref[z, at] + jnp.where(tail, lo, jnp.where(head, hi, 0.0))
    for out, row, edge in ((up_ref, CY, H + CY), (down_ref, H, H - 1)):
        for i in range(3):
            fold = zero
            out[18 + i] = zero
            out[24 + i] = zero
            for g in range(min(8, SZ - 8 * i)):
                z = 8 * i + g
                out[z] = om_ref[z, row:row + H]
                mine = jnp.logical_and(lane >= 16 * g, lane < 16 * g + 16)
                fold = jnp.where(mine, roll(os_ref[z, row:row + H], fold_shift(z), 1), fold)
                out[18 + i, g:g + 1] = om_ref[z, edge:edge + 1]
                out[24 + i, g:g + 1] = os_ref[z, edge:edge + 1]
            out[21 + i] = fold
    for out, plane in ((above_ref, up_plane), (below_ref, down_plane)):
        for r in range(1, 1 + CY // H):
            for i in range(H + 1):
                out[i, tile_rows(r - 1)] = om_ref[plane(i), tile_rows(r)]
            out[H + 1, tile_rows(r - 1)] = fold_planes(lambda i: os_ref[plane(i), tile_rows(r)])


def up_plane(i):
    return CZ - H + 1 + i


def down_plane(i):
    return i + 1 if i < H else 0


def fold_planes(side):
    lane = iota((H, CX), 1)
    fold = jnp.zeros((H, CX), F32)
    for i in range(H + 1):
        mine = jnp.logical_and(lane >= 14 * i, lane < (14 * i + 14 if i < H else CX))
        fold = jnp.where(mine, roll(side(i), 14 * i + 7 if i < H else 120, 1), fold)
    return fold


LATE = H + 1 + 2 + 3


def y_kernel(dims, pos_ref, dm_ref, ds_ref, lo_ref, hi_ref, om_ref, os_ref, above_ref, below_ref):
    in_lo, in_hi = edges(pos_ref, dims)[2:4]
    lane = iota((H, CX), 1)
    sub = iota((H, CX), 0)
    ends = jnp.logical_or(lane < H, lane >= CX - H)
    last = EY // H - 1
    for r in range(EY // H):
        at = tile_rows(r)
        for z in range(SZ):
            tile, g = z // 8, z % 8
            main, side = dm_ref[z, at], ds_ref[z, at]
            if r == 0:
                main = main + lo_ref[z] * in_lo
                side = side + jnp.where(ends, roll(lo_ref[21 + tile], -fold_shift(z), 1) * in_lo, 0.0)
            if r == 1:
                main = main + jnp.where(sub == 0, lo_ref[18 + tile, g:g + 1, :] * in_lo, 0.0)
                side = side + jnp.where(sub == 0, lo_ref[24 + tile, g:g + 1, :] * in_lo, 0.0)
            if r == last - 1:
                main = main + jnp.where(sub == H - 1, hi_ref[18 + tile, g:g + 1, :] * in_hi, 0.0)
                side = side + jnp.where(sub == H - 1, hi_ref[24 + tile, g:g + 1, :] * in_hi, 0.0)
            if r == last:
                main = main + hi_ref[z] * in_hi
                side = side + jnp.where(ends, roll(hi_ref[21 + tile], -fold_shift(z), 1) * in_hi, 0.0)
            om_ref[z, at] = main
            os_ref[z, at] = side
    lower, upper = tile_rows(0), tile_rows(last)
    for out, plane, depth in (
        (above_ref, up_plane, lambda i: H - i),
        (below_ref, down_plane, lambda i: i + 1),
    ):
        at_depth = {depth(i): plane(i) for i in range(H)}
        for d in range(1, H):
            out[d - 1] = jnp.where(sub >= d, om_ref[at_depth[d], lower], om_ref[at_depth[H - d], upper])
        out[H - 1] = om_ref[plane(H), lower]
        out[H] = om_ref[plane(H), upper]
        out[H + 1] = fold_planes(lambda i: os_ref[plane(i), lower])
        out[H + 2] = fold_planes(lambda i: os_ref[plane(i), upper])
        out[H + 5] = jnp.zeros((H, CX), F32)
        for given, factor, k in ((lo_ref, in_lo, 0), (hi_ref, in_hi, 1)):
            for i in range(H + 1):
                tile, g = plane(i) // 8, plane(i) % 8
                row = given[18 + tile, g:g + 1, :] * factor
                if i < H:
                    out[H + 3 + k, i:i + 1] = row
                else:
                    out[H + 5, k:k + 1] = row
            side = fold_planes(lambda i: jnp.broadcast_to(given[24 + plane(i) // 8, plane(i) % 8:plane(i) % 8 + 1, :], (H, CX)))
            out[H + 5, 2 + k:3 + k] = side[0:1] * factor


def pre_planes(level):
    return (H + 1 + level, H + CZ - 1 - level) if level < SWEEPS - 1 else (0, 0)


def pre_index(level, z):
    return sum(CZ - 2 - 2 * i for i in range(level)) + z - pre_planes(level)[0]


PRE = sum(CZ - 2 - 2 * i for i in range(SWEEPS - 1))


def padded_rows(t, shift=0):
    return slice(PADR + H * t + shift, PADR + H * t + H + shift)


def coefficients(pos_ref, dims):
    lo_x, hi_x, lo_y, hi_y, lo_z, hi_z = edges(pos_ref, dims)
    lane = iota((H, CX), 1)
    low, high = jnp.where(lane >= CX - H, lo_x, 1.0), jnp.where(lane < H, hi_x, 1.0)
    main = [jnp.full((H, CX), 1.0 / 6.0, F32)] * TILES
    main[0] = main[0] * lo_y
    main[-1] = main[-1] * hi_y
    return main, [c * (low * high) for c in main]


def reached(level, z, t, part):
    depth = max(0, H - z, z - H - CZ + 1)
    return depth + (t in (0, TILES - 1)) + part <= SWEEPS - level


def relax(level, planes, get, put, rhs, weights):
    lane = iota((H, CX), 1)
    first, last = lane == 0, lane == CX - 1
    z0 = planes[0]
    carry = [[get(k, z0 - 1 + i, padded_rows(t)) for k in range(2) for i in range(2)] for t in range(TILES)]
    for z in planes:
        main_weight, side_weight = weights(z)
        for t in range(TILES):
            below, main, side_below, side = carry[t]
            at, up, down = padded_rows(t), padded_rows(t, 1), padded_rows(t, -1)
            above, side_above = get(0, z + 1, at), get(1, z + 1, at)
            main_w, side_w = roll(main, 1, 1), roll(side, 1, 1)
            main_e, side_e = roll(main, -1, 1), roll(side, -1, 1)
            if reached(level, z, t, 0):
                total = (above + below) + (get(0, z, up) + get(0, z, down))
                total = total + (jnp.where(first, side_w, main_w) + jnp.where(last, side_e, main_e))
                put(0, z, at, (total - rhs(0, z, tile_rows(t))) * main_weight[t])
            if reached(level, z, t, 1):
                total = (side_above + side_below) + (get(1, z, up) + get(1, z, down))
                total = total + (jnp.where(first, main_w, side_w) + jnp.where(last, main_e, side_e))
                put(1, z, at, (total - rhs(1, z, tile_rows(t))) * side_weight[t])
            carry[t] = [main, above, side, side_above]


def inner_kernel(dims, pos_ref, dm_ref, ds_ref, pre_ref):
    main_coef, side_coef = coefficients(pos_ref, dims)
    scale = 1.0 / DT
    zero = jnp.zeros((H, CX), F32)
    for i in range(PRE):
        for part in range(2):
            pre_ref[i, part, 0:PADR] = zero
            pre_ref[i, part, PADR + EY:PADR + EY + PADR] = zero

    def rhs(part, z, rows):
        return (ds_ref if part else dm_ref)[z - H + 1, rows] * scale

    for z in range(*pre_planes(0)):
        for t in range(TILES):
            pre_ref[pre_index(0, z), 0, padded_rows(t)] = -rhs(0, z, tile_rows(t)) * main_coef[t]
            pre_ref[pre_index(0, z), 1, padded_rows(t)] = -rhs(1, z, tile_rows(t)) * side_coef[t]
    for level in range(1, SWEEPS - 1):
        def get(part, z, rows, level=level):
            return pre_ref[pre_index(level - 1, z), part, rows]

        def put(part, z, rows, value, level=level):
            pre_ref[pre_index(level, z), part, rows] = value

        relax(level, range(*pre_planes(level)), get, put, rhs, lambda z: (main_coef, side_coef))


def sweep_kernel(
    dims, pos_ref, dm_ref, ds_ref, pre_ref, lo_ref, hi_ref, late_lo_ref, late_hi_ref, pred_ref, pres_ref, vel_out, pres_out,
    b_ref, phi_ref, vel_buf, pres_buf, sems,
):
    lo_z, hi_z = edges(pos_ref, dims)[4:6]
    main_coef, side_coef = coefficients(pos_ref, dims)
    scale = 1.0 / DT
    lane = iota((H, CX), 1)
    first, last = lane == 0, lane == CX - 1
    zero = jnp.zeros((H, CX), F32)
    near = jnp.logical_or(lane < H - 1, lane >= CX - H + 1)
    ends = jnp.logical_or(lane < H, lane >= CX - H)
    lo_scale, hi_scale = lo_z * scale, hi_z * scale
    low_coef = [[c * lo_z for c in main_coef], [c * lo_z for c in side_coef]]
    high_coef = [[c * hi_z for c in main_coef], [c * hi_z for c in side_coef]]

    def weights(z):
        return low_coef if z < H else high_coef if z >= H + CZ else (main_coef, side_coef)

    outer = list(range(pre_planes(0)[0])) + list(range(pre_planes(0)[1], EZ))
    place = {z: i for i, z in enumerate(outer)}

    for z in range(EZ):
        for part in range(2):
            for buf in range(2):
                phi_ref[buf, part, z, 0:PADR] = zero
                phi_ref[buf, part, z, PADR + EY:PADR + EY + PADR] = zero
    sub = iota((H, CX), 0)

    def arrived(early, late, t, low):
        def planes(i):
            depth = H - i if low else i + 1
            if t in (0, TILES - 1):
                if i == H:
                    return late[H - 1 if t == 0 else H]
                depth = depth if t == 0 else H - depth
                return late[depth - 1] if 0 < depth < H else zero
            value = early[i, tile_rows(t - 1)]
            for k, edge, row in ((0, 1, 0), (1, TILES - 2, H - 1)):
                if t == edge:
                    fix = late[H + 3 + k, i:i + 1] if i < H else late[H + 5, k:k + 1]
                    value = value + jnp.where(sub == row, fix, 0.0)
            return value

        if t in (0, TILES - 1):
            fold = late[H + 1 if t == 0 else H + 2]
        else:
            fold = early[H + 1, tile_rows(t - 1)]
            for k, edge, row in ((0, 1, 0), (1, TILES - 2, H - 1)):
                if t == edge:
                    fold = fold + jnp.where(sub == row, late[H + 5, 2 + k:3 + k], 0.0)
        return planes, fold

    for t in range(TILES):
        rows = tile_rows(t)
        lo_planes, lo_fold = arrived(lo_ref, late_lo_ref, t, True)
        hi_planes, hi_fold = arrived(hi_ref, late_hi_ref, t, False)
        folded = (lo_fold * lo_scale, hi_fold * hi_scale)
        for z in outer:
            low = z < EZ // 2
            halo, fold, factor = (lo_planes, folded[0], lo_scale) if low else (hi_planes, folded[1], hi_scale)
            if z < H or z >= H + CZ:
                g = z if low else z - H - CZ
                main = halo(g) * factor
                side = jnp.where(near, roll(fold, -(14 * g + 7), 1), 0.0)
                if z in (H - 1, H + CZ):
                    k = 0 if low else SZ - 1
                    main = main + dm_ref[k, rows] * factor
                    side = side + ds_ref[k, rows] * factor
            else:
                main = dm_ref[z - H + 1, rows] * scale + halo(H) * factor
                side = ds_ref[z - H + 1, rows] * scale + jnp.where(ends, roll(fold, -120, 1), 0.0)
            b_ref[0, place[z], rows] = main
            b_ref[1, place[z], rows] = side
            cm, cs = weights(z)
            phi_ref[0, 0, z, padded_rows(t)] = -main * cm[t]
            phi_ref[0, 1, z, padded_rows(t)] = -side * cs[t]

    def rhs(part, z, rows):
        if z in place:
            return b_ref[part, place[z], rows]
        return (ds_ref if part else dm_ref)[z - H + 1, rows] * scale

    def reader(level):
        known = range(*pre_planes(level))

        def get(part, z, rows):
            if z in known:
                return pre_ref[pre_index(level, z), part, rows]
            return phi_ref[level % 2, part, z, rows]

        return get

    for level in range(1, SWEEPS):
        lo, hi = pre_planes(level)

        def put(part, z, rows, value, level=level):
            phi_ref[level % 2, part, z, rows] = value

        runs = ((level, lo), (hi, EZ - level)) if hi > lo else ((level, EZ - level),)
        for run in runs:
            relax(level, range(*run), reader(level - 1), put, rhs, weights)

    get = reader(SWEEPS - 1)
    chunk = 4
    copies = []
    for c in range(CZ // chunk):
        for z in range(c * chunk, (c + 1) * chunk):
            for t in range(CY // H):
                rows = tile_rows(t)
                at, up, down = padded_rows(t + 1), padded_rows(t + 1, 1), padded_rows(t + 1, -1)
                main, side = get(0, z + H, at), get(1, z + H, at)
                west = jnp.where(first, roll(side, 1, 1), roll(main, 1, 1))
                east = jnp.where(last, roll(side, -1, 1), roll(main, -1, 1))
                half = DT * 0.5
                vel_buf[0, z, rows] = pred_ref[0, z, rows] - half * (east - west)
                vel_buf[1, z, rows] = pred_ref[1, z, rows] - half * (get(0, z + H, up) - get(0, z + H, down))
                vel_buf[2, z, rows] = pred_ref[2, z, rows] - half * (get(0, z + H + 1, at) - get(0, z + H - 1, at))
                pres_buf[z, rows] = pres_ref[z, rows] + main
        part = pl.ds(c * chunk, chunk)
        copies.append(pltpu.make_async_copy(vel_buf.at[:, part], vel_out.at[:, part], sems.at[2 * c]))
        copies.append(pltpu.make_async_copy(pres_buf.at[part], pres_out.at[part], sems.at[2 * c + 1]))
        for copy in copies[-2:]:
            copy.start()
    for copy in copies:
        copy.wait()


def swap(up, down, axis):
    count = lax.axis_size(axis)
    forward = [(i, (i + 1) % count) for i in range(count)]
    backward = [(j, i) for i, j in forward]
    return lax.ppermute(up, axis, forward), lax.ppermute(down, axis, backward)


def shape(*dims):
    return jax.ShapeDtypeStruct(dims, F32)


SMEM = pl.BlockSpec(memory_space=pltpu.SMEM)
VMEM = pl.BlockSpec(memory_space=pltpu.VMEM)


ANY = pl.BlockSpec(memory_space=pl.ANY)


def in_hbm(x):
    return pltpu.with_memory_space_constraint(x, pltpu.HBM)


def in_vmem(*dims, dtype=F32):
    return pltpu.VMEM(dims, dtype)


MIB = 1024 * 1024
ENTRY_LIMIT = 24


class Place:
    def __getitem__(self, k):
        return lax.axis_index(("gx", "gy", "gz")[k])


def call(kernel, scalars, arrays, outs, scratch=(), in_specs=None, out_specs=None, limit=24, cost=0):
    return pl.pallas_call(
        functools.partial(kernel, Place()),
        out_shape=outs,
        in_specs=[SMEM] * len(scalars) + list(in_specs or [VMEM] * len(arrays)),
        out_specs=out_specs or [VMEM] * len(outs),
        scratch_shapes=list(scratch),
        compiler_params=pltpu.CompilerParams(vmem_limit_bytes=limit * MIB),
        cost_estimate=pl.CostEstimate(flops=cost, bytes_accessed=cost // 64, transcendentals=0) if cost else None,
    )(*scalars, *arrays)


def shards(
    velocity, adjoint, pressure, viscosity, disk_cells, disk_turbine, disk_weight, disk_dweight, yaw, thrust_coef, owner_slot,
):
    axes = ("gx", "gy", "gz")
    n_gx, n_gy, n_gz = (lax.axis_size(a) for a in axes)
    n_dev = n_gx * n_gy * n_gz
    dims = (n_dev, n_gx, n_gy, n_gz)
    turbines = owner_slot.shape[0]
    if turbines % CX:
        owner_slot = jnp.pad(owner_slot, (0, CX - turbines % CX))
    owner = owner_slot.reshape(-1, CX)
    cells, turbine, weight = (a.reshape(1, -1) for a in (disk_cells, disk_turbine, disk_weight))

    payload, xr, xl, yr, yl, zr, zl, fields, index, scale, table = call(
        functools.partial(entry_kernel, n_dev, n_gy),
        (in_hbm(yaw), in_hbm(thrust_coef)),
        tuple(in_hbm(a) for a in (velocity, adjoint, viscosity, cells, turbine, weight, disk_dweight, owner)),
        (
            shape(n_dev, CX), in_vmem(CY, CX), in_vmem(CY, CX), in_vmem(6 * CZ, CX), in_vmem(6 * CZ, CX),
            in_vmem(6, CY, CX), in_vmem(6, CY, CX), in_vmem(7, CZ, CY, CX), in_vmem(2, cells.shape[1], dtype=jnp.int32),
            in_vmem(*weight.shape), in_vmem(*owner.shape, dtype=jnp.int32),
        ),
        (pltpu.VMEM((n_dev, CX), F32), pltpu.SemaphoreType.DMA((8,))),
        [ANY, ANY, ANY] + [VMEM] * 5,
        [ANY] + [VMEM] * 10,
        limit=ENTRY_LIMIT,
    )
    got = lax.all_to_all(payload, axes, 0, 0, tiled=True)
    xlo, xhi = swap(xr, xl, "gx")
    ylo, yhi = swap(yr, yl, "gy")
    xlo, zl = lax.optimization_barrier((xlo, zl))
    zlo, zhi = swap(zr, zl, "gz")
    faces = (xlo, xhi, ylo, yhi, zlo, zhi)

    pred_base, dual_base = call(
        stencil_kernel, (), (fields,), (shape(3, CZ, CY, CX), shape(3, CZ, CY, CX)), cost=1 << 30
    )
    force = call(
        functools.partial(force_kernel, dims), (), (index, scale, table, got), (shape(3, CZ, CY, CX),), cost=1 << 30
    )[0]
    predicted, dm, ds, xr, xl = call(
        functools.partial(flow_kernel, dims),
        (),
        (pred_base, force, fields) + faces,
        (shape(3, CZ, CY, CX), shape(SZ, EY, CX), shape(SZ, EY, CX), shape(3, EY, CX), shape(3, EY, CX)),
    )
    adjoint_next, yaw_grad, position_grad = call(
        functools.partial(dual_kernel, dims),
        (in_hbm(yaw), in_hbm(thrust_coef)),
        (dual_base, force, fields, got) + faces,
        (shape(3, CZ, CY, CX), shape(1, 4), shape(2, 4)),
        (pltpu.VMEM((3, CZ, CY, CX), F32), pltpu.SemaphoreType.DMA((3,))),
        out_specs=[ANY, VMEM, VMEM],
        cost=1 << 30,
    )
    lo, hi = swap(xr, xl, "gx")
    dm, ds, up, down, above, below = call(
        functools.partial(x_kernel, dims), (), (dm, ds, lo, hi),
        (
            shape(SZ, EY, CX), shape(SZ, EY, CX), shape(27, H, CX), shape(27, H, CX),
            shape(H + 2, CY, CX), shape(H + 2, CY, CX),
        ),
    )
    lo, hi = swap(up, down, "gy")
    early_lo, early_hi = swap(above, below, "gz")
    lo, yaw_grad = lax.optimization_barrier((lo, yaw_grad))
    dm, ds, above, below = call(
        functools.partial(y_kernel, dims), (), (dm, ds, lo, hi),
        (shape(SZ, EY, CX), shape(SZ, EY, CX), shape(LATE, H, CX), shape(LATE, H, CX)),
    )
    late_lo, late_hi = swap(above, below, "gz")
    pre = call(
        functools.partial(inner_kernel, dims), (), (dm, ds), (shape(PRE, 2, EY + 2 * PADR, CX),), cost=1 << 30
    )[0]
    velocity_next, pressure_next = call(
        functools.partial(sweep_kernel, dims), (), (dm, ds, pre, early_lo, early_hi, late_lo, late_hi, predicted, pressure),
        (shape(3, CZ, CY, CX), shape(CZ, CY, CX)),
        (
            pltpu.VMEM((2, EZ - CZ + 2, EY, CX), F32), pltpu.VMEM((2, 2, EZ, EY + 2 * PADR, CX), F32),
            pltpu.VMEM((3, CZ, CY, CX), F32), pltpu.VMEM((CZ, CY, CX), F32), pltpu.SemaphoreType.DMA((8,)),
        ),
        out_specs=[ANY, ANY],
    )
    return velocity_next, adjoint_next, pressure_next, yaw_grad.reshape(-1), position_grad


def solution(mesh):
    axes = ("gx", "gy", "gz")
    grid = P(None, "gz", "gy", "gx")
    cell = P("gz", "gy", "gx")
    flat = P(axes)
    return jax.shard_map(
        shards,
        mesh=mesh,
        in_specs=(grid, grid, cell, cell, flat, flat, flat, P(None, axes), flat, flat, P()),
        out_specs=(grid, grid, cell, flat, P(None, axes)),
        check_vma=False,
    )
```

```python
import functools

import jax
import jax.numpy as jnp
from jax import lax
from jax.experimental import pallas as pl
from jax.experimental.pallas import tpu as pltpu
from jax.sharding import PartitionSpec as P

SWEEPS = 8
DT = 0.2
F32 = jnp.float32
BF16 = jnp.bfloat16
CZ, CY, CX = 16, 32, 128
KJ = CZ * CY
H = 8
EZ, EY = CZ + 2 * H, CY + 2 * H
SZ = CZ + 2
TILES = EY // H
PADR = 8
PER = 16
WIN = 64
YAW = 112
NN = (((1,), (0,)), ((), ()))
NT = (((1,), (1,)), ((), ()))
TN = (((0,), (0,)), ((), ()))


def iota(shape, dim):
    return lax.broadcasted_iota(jnp.int32, shape, dim)


def pieces(x, count):
    parts = []
    for _ in range(count):
        head = x.astype(BF16)
        parts.append(head)
        x = x - head.astype(F32)
    return parts


def dots(left, right, dims):
    total = None
    for a in left:
        for b in right:
            term = lax.dot_general(a, b, dims, preferred_element_type=F32)
            total = term if total is None else total + term
    return total


def onehot(mask):
    return jnp.where(mask, 1.0, 0.0).astype(BF16)


def roll(x, shift, axis):
    return pltpu.roll(x, shift % x.shape[axis], axis)


def entry_onehots(cells):
    row = lax.shift_right_logical(cells, 7)
    lane = jnp.bitwise_and(cells, CX - 1)
    count = cells.shape[1]
    rows = onehot(iota((KJ, count), 0) == row)
    lanes = iota((CX, count), 0) == lane
    return rows, lanes


def window_lane(turbine, bx, n_gy):
    column_x = lax.shift_right_logical(turbine, 4) // n_gy
    return WIN + (column_x - bx + 1) * PER + jnp.bitwise_and(turbine, PER - 1)


def lookup(table_ref, turbine):
    count = turbine.shape[1]
    table = table_ref[...]
    owner = lax.shift_right_logical(table, 2).astype(F32)
    which = jnp.bitwise_and(table, 3).astype(F32)
    rows = table.shape[0]
    high = lax.shift_right_logical(turbine, 7)
    low = onehot(iota((CX, count), 0) == jnp.bitwise_and(turbine, CX - 1))
    keep = iota((rows, count), 0) == high
    out = []
    for part in (owner, which):
        picked = dots([part.astype(BF16)], [low], NN)
        picked = jnp.sum(jnp.where(keep, picked, 0.0), axis=0, keepdims=True)
        out.append(picked.astype(jnp.int32))
    return out


def entry_kernel(
    n_dev, n_gy, pos_ref, yaw_ref, ct_ref, vel_hbm, adj_hbm, visc_hbm, cells_ref, turb_ref, weight_ref, dweight_ref, owner_ref,
    pay_ref, xr_ref, xl_ref, yr_ref, yl_ref, zr_ref, zl_ref, fld_ref, index_ref, scale_ref, table_ref, out_ref, sems,
):
    order = (0, 3, 4, 1, 2, 5, 6)
    copies = {}
    for f in order:
        hbm = vel_hbm.at[f] if f < 3 else adj_hbm.at[f - 3] if f < 6 else visc_hbm
        copies[f] = pltpu.make_async_copy(hbm, fld_ref.at[f], sems.at[f])
        copies[f].start()
    bx = pos_ref[0]
    cells, turbine, weight = cells_ref[...], turb_ref[...], weight_ref[...]
    index_ref[0:1, :] = cells
    index_ref[1:2, :] = turbine
    scale_ref[...] = weight
    table_ref[...] = owner_ref[...]
    count = cells.shape[1]
    rows, lanes = entry_onehots(cells)
    owner, which = lookup(owner_ref, turbine)
    to_owner = onehot(iota((n_dev, count), 0) == owner)
    in_window = onehot(iota((CX, count), 0) == window_lane(turbine, bx, n_gy))

    columns = []
    for f in order[:3]:
        copies[f].wait()
        columns += pieces(fld_ref[f].reshape(KJ, CX), 2)
    at_row = dots([jnp.concatenate(columns, axis=1)], [rows], TN)
    gathered = []
    for k in range(3):
        both = at_row[2 * k * CX:(2 * k + 1) * CX] + at_row[(2 * k + 1) * CX:(2 * k + 2) * CX]
        gathered.append(jnp.sum(jnp.where(lanes, both, 0.0), axis=0, keepdims=True))
    factors = [weight, dweight_ref[0:1, :], dweight_ref[1:2, :]]
    values = [f * g for f in factors for g in gathered]

    sub = iota((PER, count), 0)
    stacked = jnp.zeros((PER, count), F32)
    for v, value in enumerate(values):
        stacked = jnp.where(sub == v, value, stacked)
    per_slot = jnp.concatenate(
        [jnp.where(which == i, stacked, 0.0) for i in range(4)] + [jnp.zeros((CX - 4 * PER, count), F32)], axis=0
    )
    payload = dots([to_owner], pieces(per_slot, 2), NT)

    speed = jnp.broadcast_to(values[0], (8, count))
    shared = dots(pieces(speed, 2), [in_window], NT)[0:1, :]
    lane = iota((1, CX), 1)
    for i in range(4):
        shared = jnp.where(lane == YAW + i, yaw_ref[i], shared)
        shared = jnp.where(lane == YAW + 4 + i, ct_ref[i], shared)
    out_ref[...] = payload + shared
    leaving = pltpu.make_async_copy(out_ref, pay_ref, sems.at[7])
    leaving.start()

    for f in order[3:]:
        copies[f].wait()
    lane = iota((H, CX), 1)
    for t in range(CY // H):
        at = slice(H * t, H * t + H)
        for half in range(2):
            right = jnp.zeros((H, CX), F32)
            left = jnp.zeros((H, CX), F32)
            for f in range(3):
                for z in range(CZ):
                    spot = 2 * (f * CZ + z) + 1
                    moved = roll(fld_ref[3 * half + f, z, at], spot + 1, 1)
                    right = jnp.where(lane == spot, moved, right)
                    left = jnp.where(lane == spot + 1, moved, left)
            xr_ref[half, at] = right
            xl_ref[half, at] = left
    for f in range(6):
        yr_ref[f * CZ:(f + 1) * CZ, :] = fld_ref[f, :, CY - 1, :]
        yl_ref[f * CZ:(f + 1) * CZ, :] = fld_ref[f, :, 0, :]
        zr_ref[f] = fld_ref[f, CZ - 1]
        zl_ref[f] = fld_ref[f, 0]
    leaving.wait()


def turbine_terms(speed, yaw, thrust_coef):
    cosine = jnp.cos(yaw)
    sine = jnp.sin(yaw)
    magnitude = jnp.abs(speed)
    force = 0.5 * thrust_coef * speed * magnitude * cosine * cosine
    weighting = 1.5 * thrust_coef * speed * magnitude * cosine * cosine * cosine
    return cosine, sine, magnitude, force, weighting


def owner_outputs(got, yaw_ref, ct_ref, yaw_out, pos_out):
    total = jnp.sum(got, axis=0, keepdims=True)
    total = jnp.broadcast_to(total, (8, CX))
    lane = iota((8, CX), 1)
    yaw = jnp.zeros((8, CX), F32)
    ct = jnp.zeros((8, CX), F32)
    for i in range(4):
        yaw = jnp.where(lane == i * PER, yaw_ref[i], yaw)
        ct = jnp.where(lane == i * PER, ct_ref[i], ct)

    def at(v):
        return roll(total, -v, 1)

    speed, dual_x, dual_y = total, at(1), at(2)
    cosine, sine, magnitude, force, weighting = turbine_terms(speed, yaw, ct)
    yaw_grad = -1.5 * ct * magnitude * magnitude * magnitude * cosine * cosine * sine + force * (
        sine * dual_x - cosine * dual_y
    )
    grads = [yaw_grad]
    for r in range(2):
        grads.append(weighting * at(3 + 3 * r) - force * cosine * at(4 + 3 * r) - force * sine * at(5 + 3 * r))
    packed = []
    for grad in grads:
        out = jnp.zeros((8, CX), F32)
        for i in range(4):
            out = jnp.where(lane == i, roll(grad, -(PER - 1) * i, 1), out)
        packed.append(out)
    yaw_out[...] = packed[0][0:1, 0:4]
    pos_out[0:1, :] = packed[1][0:1, 0:4]
    pos_out[1:2, :] = packed[2][0:1, 0:4]


def window_terms(got, n_dev, n_gx, n_gy, n_gz, bx, by, owner_ref):
    lane = iota((1, CX), 1)
    inside = jnp.logical_and(lane >= WIN, lane < WIN + 3 * PER)
    row = iota((n_dev, CX), 0)
    speed = jnp.zeros((1, CX), F32)
    for delta in range(-2, 3):
        base = ((bx + delta) * n_gy + by) * n_gz
        keep = jnp.logical_and(row >= base, row < base + n_gz)
        part = jnp.sum(jnp.where(keep, got, 0.0), axis=0, keepdims=True)
        part = jnp.broadcast_to(jnp.where(inside, part, 0.0), (8, CX))
        speed = speed + roll(part, delta * PER, 1)[0:1, :]
    speed = jnp.where(inside, speed, 0.0)

    table = owner_ref[...]
    sub = iota(table.shape, 0)
    slots = jnp.zeros((1, CX), jnp.int32)
    for j in range(3):
        column_x = jnp.clip(bx - 1 + j, 0, n_gx - 1)
        first = (column_x * n_gy + by) * PER
        picked = jnp.sum(jnp.where(sub == first // CX, table, 0), axis=0, keepdims=True)
        picked = jnp.broadcast_to(picked, (8, CX))
        moved = pltpu.roll(picked, jnp.bitwise_and(WIN + PER * j - first, CX - 1), 1)[0:1, :]
        here = jnp.logical_and(lane >= WIN + PER * j, lane < WIN + PER * (j + 1))
        slots = jnp.where(here, moved, slots)
    owner = onehot(iota((n_dev, CX), 0) == lax.shift_right_logical(slots, 2))
    which = jnp.bitwise_and(slots, 3)
    found = dots(pieces(got, 3), [owner], TN)
    yaw = jnp.zeros((1, CX), F32)
    ct = jnp.zeros((1, CX), F32)
    for i in range(4):
        yaw = jnp.where(which == i, found[YAW + i:YAW + i + 1, :], yaw)
        ct = jnp.where(which == i, found[YAW + 4 + i:YAW + 5 + i, :], ct)
    cosine, sine, magnitude, force, weighting = turbine_terms(speed, yaw, ct)
    keep = lambda x: jnp.where(inside, x, 0.0)
    return keep(force * cosine), keep(force * sine), keep(weighting)


def edges(pos_ref, dims):
    n_dev, n_gx, n_gy, n_gz = dims
    out = []
    for k, count in enumerate((n_gx, n_gy, n_gz)):
        out.append(jnp.where(pos_ref[k] > 0, 1.0, 0.0))
        out.append(jnp.where(pos_ref[k] < count - 1, 1.0, 0.0))
    return out


def tile_rows(t):
    return slice(H * t, H * t + H)


def south_of(ref, index, t, sub):
    if t > 0:
        return ref[index + (slice(H * t - 1, H * t + H - 1),)]
    return jnp.where(sub == 0, 0.0, roll(ref[index + (tile_rows(0),)], 1, 0))


def north_of(ref, index, t, sub):
    if t < CY // H - 1:
        return ref[index + (slice(H * t + 1, H * t + H + 1),)]
    return jnp.where(sub == H - 1, 0.0, roll(ref[index + (tile_rows(t),)], -1, 0))


def force_kernel(dims, pos_ref, index_ref, scale_ref, owner_ref, got_ref, field_ref):
    n_dev, n_gx, n_gy, n_gz = dims
    bx, by = pos_ref[0], pos_ref[1]
    terms = window_terms(got_ref[...], n_dev, n_gx, n_gy, n_gz, bx, by, owner_ref)
    cells, turbine, weight = index_ref[0:1, :], index_ref[1:2, :], scale_ref[...]
    count = cells.shape[1]
    rows, lanes = entry_onehots(cells)
    in_window = onehot(iota((CX, count), 0) == window_lane(turbine, bx, n_gy))
    stacked = jnp.concatenate([jnp.broadcast_to(t, (8, CX)) for t in terms], axis=0)
    per_entry = dots(pieces(stacked, 2), [in_window], NN)
    for c in range(3):
        value = per_entry[8 * c:8 * c + 1, :] * weight
        if c < 2:
            value = -value
        spread = jnp.where(lanes, value, 0.0)
        field_ref[c] = dots([rows], pieces(spread, 2), NT).reshape(CZ, CY, CX)


def stencil_kernel(pos_ref, fld_ref, pred_ref, dual_ref):
    lane = iota((H, CX), 1)
    sub = iota((H, CX), 0)
    zero = jnp.zeros((H, CX), F32)
    for t in range(CY // H):
        at = tile_rows(t)
        for f in range(6):
            out, comp = (pred_ref, f) if f < 3 else (dual_ref, f - 3)
            below, tile = zero, fld_ref[f, 0, at]
            for z in range(CZ):
                above = fld_ref[f, z + 1, at] if z < CZ - 1 else zero
                south, north = south_of(fld_ref, (f, z), t, sub), north_of(fld_ref, (f, z), t, sub)
                west = jnp.where(lane == 0, 0.0, roll(tile, 1, 1))
                east = jnp.where(lane == CX - 1, 0.0, roll(tile, -1, 1))
                lap = (above + below) + (north + south) + (east + west) - 6.0 * tile
                rate = fld_ref[6, z, at] * lap + (west - tile if f < 3 else east - tile)
                out[comp, z, at] = tile + DT * rate
                below, tile = tile, above


def add_faces(f, first, out, given, field_ref, fld_ref, bounds, xlo_ref, xhi_ref, ylo_ref, yhi_ref, zlo_ref, zhi_ref):
    lo_x, hi_x, lo_y, hi_y, lo_z, hi_z = bounds
    lane = iota((H, CX), 1)
    sub = iota((H, CX), 0)
    flow = f < 3
    comp = f - first
    for t in range(CY // H):
        at = tile_rows(t)
        odd = jnp.bitwise_and(lane, 1) == 1
        face = jnp.where(odd, xlo_ref[f // 3, at] * lo_x, roll(xhi_ref[f // 3, at] * hi_x, -2, 1))
        for z in range(CZ):
            spot = f * CZ + z
            moved = roll(face, -(2 * (spot % (3 * CZ)) + 1), 1)
            west = jnp.where(lane == 0, moved, 0.0)
            east = jnp.where(lane == CX - 1, moved, 0.0)
            lap = west + east
            if t == 0:
                lap = lap + jnp.where(sub == 0, ylo_ref[spot:spot + 1, :] * lo_y, 0.0)
            if t == CY // H - 1:
                lap = lap + jnp.where(sub == H - 1, yhi_ref[spot:spot + 1, :] * hi_y, 0.0)
            if z == 0:
                lap = lap + zlo_ref[f, at] * lo_z
            if z == CZ - 1:
                lap = lap + zhi_ref[f, at] * hi_z
            rate = fld_ref[6, z, at] * lap + (west if flow else east)
            if f < 2:
                rate = rate + field_ref[f, z, at]
            if f == 3:
                rate = rate + field_ref[2, z, at]
            out[comp, z, at] = given[comp, z, at] + DT * rate


def fold_shift(z):
    return H + 16 * (z % 8)


def flow_kernel(
    dims, pos_ref, base_ref, field_ref, fld_ref, xlo_ref, xhi_ref, ylo_ref, yhi_ref, zlo_ref, zhi_ref,
    pred_ref, dm_ref, ds_ref, xr_ref, xl_ref,
):
    bounds = edges(pos_ref, dims)
    for f in range(3):
        add_faces(f, 0, pred_ref, base_ref, field_ref, fld_ref, bounds, xlo_ref, xhi_ref, ylo_ref, yhi_ref, zlo_ref, zhi_ref)
    lane = iota((H, CX), 1)
    sub = iota((H, CX), 0)
    zero = jnp.zeros((H, CX), F32)
    for r in range(EY // H):
        at = tile_rows(r)
        t = r - 1
        inside = 0 <= t < CY // H
        for k in range(SZ):
            z = k - 1
            main, side = zero, zero
            if inside and 0 <= z < CZ:
                own = tile_rows(t)
                p0 = pred_ref[0, z, own]
                west, east = roll(p0, 1, 1), roll(p0, -1, 1)
                div = jnp.where(lane == CX - 1, 0.0, east) - jnp.where(lane == 0, 0.0, west)
                div = div + (north_of(pred_ref, (1, z), t, sub) - south_of(pred_ref, (1, z), t, sub))
                if z < CZ - 1:
                    div = div + pred_ref[2, z + 1, own]
                if z > 0:
                    div = div - pred_ref[2, z - 1, own]
                main = 0.5 * div
                side = jnp.where(lane == CX - 1, 0.5 * east, jnp.where(lane == 0, -0.5 * west, 0.0))
            elif inside:
                main = 0.5 * pred_ref[2, 0, tile_rows(t)] if z < 0 else -0.5 * pred_ref[2, CZ - 1, tile_rows(t)]
            elif 0 <= z < CZ and t < 0:
                main = jnp.where(sub == H - 1, 0.5 * roll(pred_ref[1, z, 0:H], -1, 0), 0.0)
            elif 0 <= z < CZ:
                main = jnp.where(sub == 0, -0.5 * roll(pred_ref[1, z, CY - H:CY], 1, 0), 0.0)
            dm_ref[k, at] = main
            ds_ref[k, at] = side
    for r in range(EY // H):
        at = tile_rows(r)
        right, left = [zero] * 3, [zero] * 3
        for k in range(SZ):
            if not 0 < r < EY // H - 1 and not 0 < k < SZ - 1:
                continue
            main, side = dm_ref[k, at], ds_ref[k, at]
            g = k % 8
            mine = jnp.logical_and(lane >= 16 * g, lane < 16 * g + 16)
            right[k // 8] = jnp.where(mine, roll(jnp.where(lane < H, side, main), fold_shift(k), 1), right[k // 8])
            left[k // 8] = jnp.where(mine, roll(jnp.where(lane < H, main, side), fold_shift(k), 1), left[k // 8])
        for i in range(3):
            xr_ref[i, at] = right[i]
            xl_ref[i, at] = left[i]


def dual_kernel(
    dims, pos_ref, yaw_ref, ct_ref, base_ref, field_ref, fld_ref, got_ref, xlo_ref, xhi_ref, ylo_ref, yhi_ref, zlo_ref, zhi_ref,
    dual_out, yaw_out, pos_out, dual_ref, sems,
):
    bounds = edges(pos_ref, dims)
    copies = []
    for f in range(3, 6):
        add_faces(f, 3, dual_ref, base_ref, field_ref, fld_ref, bounds, xlo_ref, xhi_ref, ylo_ref, yhi_ref, zlo_ref, zhi_ref)
        copies.append(pltpu.make_async_copy(dual_ref.at[f - 3], dual_out.at[f - 3], sems.at[f - 3]))
        copies[-1].start()
    owner_outputs(got_ref[...], yaw_ref, ct_ref, yaw_out, pos_out)
    for copy in copies:
        copy.wait()


def x_kernel(
    dims, pos_ref, dm_ref, ds_ref, lo_ref, hi_ref, om_ref, os_ref, up_ref, down_ref, above_ref, below_ref
):
    in_lo, in_hi = edges(pos_ref, dims)[0:2]
    lane = iota((H, CX), 1)
    head, tail = lane < H, lane >= CX - H
    zero = jnp.zeros((H, CX), F32)
    for r in range(EY // H):
        at = tile_rows(r)
        lows = [lo_ref[i, at] * in_lo for i in range(3)]
        highs = [hi_ref[i, at] * in_hi for i in range(3)]
        for z in range(SZ):
            lo = roll(lows[z // 8], -fold_shift(z), 1)
            hi = roll(highs[z // 8], -fold_shift(z), 1)
            om_ref[z, at] = dm_ref[z, at] + jnp.where(head, lo, jnp.where(tail, hi, 0.0))
            os_ref[z, at] = ds_ref[z, at] + jnp.where(tail, lo, jnp.where(head, hi, 0.0))
    for out, row, edge in ((up_ref, CY, H + CY), (down_ref, H, H - 1)):
        for i in range(3):
            fold = zero
            out[18 + i] = zero
            out[24 + i] = zero
            for g in range(min(8, SZ - 8 * i)):
                z = 8 * i + g
                out[z] = om_ref[z, row:row + H]
                mine = jnp.logical_and(lane >= 16 * g, lane < 16 * g + 16)
                fold = jnp.where(mine, roll(os_ref[z, row:row + H], fold_shift(z), 1), fold)
                out[18 + i, g:g + 1] = om_ref[z, edge:edge + 1]
                out[24 + i, g:g + 1] = os_ref[z, edge:edge + 1]
            out[21 + i] = fold
    for out, plane in ((above_ref, up_plane), (below_ref, down_plane)):
        for r in range(1, 1 + CY // H):
            for i in range(H + 1):
                out[i, tile_rows(r - 1)] = om_ref[plane(i), tile_rows(r)]
            out[H + 1, tile_rows(r - 1)] = fold_planes(lambda i: os_ref[plane(i), tile_rows(r)])


def up_plane(i):
    return CZ - H + 1 + i


def down_plane(i):
    return i + 1 if i < H else 0


def fold_planes(side):
    lane = iota((H, CX), 1)
    fold = jnp.zeros((H, CX), F32)
    for i in range(H + 1):
        mine = jnp.logical_and(lane >= 14 * i, lane < (14 * i + 14 if i < H else CX))
        fold = jnp.where(mine, roll(side(i), 14 * i + 7 if i < H else 120, 1), fold)
    return fold


LATE = H + 1 + 2 + 3


def y_kernel(dims, pos_ref, dm_ref, ds_ref, lo_ref, hi_ref, om_ref, os_ref, above_ref, below_ref):
    in_lo, in_hi = edges(pos_ref, dims)[2:4]
    lane = iota((H, CX), 1)
    sub = iota((H, CX), 0)
    ends = jnp.logical_or(lane < H, lane >= CX - H)
    last = EY // H - 1
    for r in range(EY // H):
        at = tile_rows(r)
        for z in range(SZ):
            tile, g = z // 8, z % 8
            main, side = dm_ref[z, at], ds_ref[z, at]
            if r == 0:
                main = main + lo_ref[z] * in_lo
                side = side + jnp.where(ends, roll(lo_ref[21 + tile], -fold_shift(z), 1) * in_lo, 0.0)
            if r == 1:
                main = main + jnp.where(sub == 0, lo_ref[18 + tile, g:g + 1, :] * in_lo, 0.0)
                side = side + jnp.where(sub == 0, lo_ref[24 + tile, g:g + 1, :] * in_lo, 0.0)
            if r == last - 1:
                main = main + jnp.where(sub == H - 1, hi_ref[18 + tile, g:g + 1, :] * in_hi, 0.0)
                side = side + jnp.where(sub == H - 1, hi_ref[24 + tile, g:g + 1, :] * in_hi, 0.0)
            if r == last:
                main = main + hi_ref[z] * in_hi
                side = side + jnp.where(ends, roll(hi_ref[21 + tile], -fold_shift(z), 1) * in_hi, 0.0)
            om_ref[z, at] = main
            os_ref[z, at] = side
    lower, upper = tile_rows(0), tile_rows(last)
    for out, plane, depth in (
        (above_ref, up_plane, lambda i: H - i),
        (below_ref, down_plane, lambda i: i + 1),
    ):
        at_depth = {depth(i): plane(i) for i in range(H)}
        for d in range(1, H):
            out[d - 1] = jnp.where(sub >= d, om_ref[at_depth[d], lower], om_ref[at_depth[H - d], upper])
        out[H - 1] = om_ref[plane(H), lower]
        out[H] = om_ref[plane(H), upper]
        out[H + 1] = fold_planes(lambda i: os_ref[plane(i), lower])
        out[H + 2] = fold_planes(lambda i: os_ref[plane(i), upper])
        out[H + 5] = jnp.zeros((H, CX), F32)
        for given, factor, k in ((lo_ref, in_lo, 0), (hi_ref, in_hi, 1)):
            for i in range(H + 1):
                tile, g = plane(i) // 8, plane(i) % 8
                row = given[18 + tile, g:g + 1, :] * factor
                if i < H:
                    out[H + 3 + k, i:i + 1] = row
                else:
                    out[H + 5, k:k + 1] = row
            side = fold_planes(lambda i: jnp.broadcast_to(given[24 + plane(i) // 8, plane(i) % 8:plane(i) % 8 + 1, :], (H, CX)))
            out[H + 5, 2 + k:3 + k] = side[0:1] * factor


def pre_planes(level):
    return (H + 1 + level, H + CZ - 1 - level) if level < SWEEPS - 1 else (0, 0)


def pre_index(level, z):
    return sum(CZ - 2 - 2 * i for i in range(level)) + z - pre_planes(level)[0]


PRE = sum(CZ - 2 - 2 * i for i in range(SWEEPS - 1))


def padded_rows(t, shift=0):
    return slice(PADR + H * t + shift, PADR + H * t + H + shift)


def coefficients(pos_ref, dims):
    lo_x, hi_x, lo_y, hi_y, lo_z, hi_z = edges(pos_ref, dims)
    lane = iota((H, CX), 1)
    low, high = jnp.where(lane >= CX - H, lo_x, 1.0), jnp.where(lane < H, hi_x, 1.0)
    main = [jnp.full((H, CX), 1.0 / 6.0, F32)] * TILES
    main[0] = main[0] * lo_y
    main[-1] = main[-1] * hi_y
    return main, [c * (low * high) for c in main]


def reached(level, z, t, part):
    depth = max(0, H - z, z - H - CZ + 1)
    return depth + (t in (0, TILES - 1)) + part <= SWEEPS - level


def relax(level, planes, get, put, rhs, weights):
    lane = iota((H, CX), 1)
    first, last = lane == 0, lane == CX - 1
    z0 = planes[0]
    carry = [[get(k, z0 - 1 + i, padded_rows(t)) for k in range(2) for i in range(2)] for t in range(TILES)]
    for z in planes:
        main_weight, side_weight = weights(z)
        for t in range(TILES):
            below, main, side_below, side = carry[t]
            at, up, down = padded_rows(t), padded_rows(t, 1), padded_rows(t, -1)
            above, side_above = get(0, z + 1, at), get(1, z + 1, at)
            main_w, side_w = roll(main, 1, 1), roll(side, 1, 1)
            main_e, side_e = roll(main, -1, 1), roll(side, -1, 1)
            if reached(level, z, t, 0):
                total = (above + below) + (get(0, z, up) + get(0, z, down))
                total = total + (jnp.where(first, side_w, main_w) + jnp.where(last, side_e, main_e))
                put(0, z, at, (total - rhs(0, z, tile_rows(t))) * main_weight[t])
            if reached(level, z, t, 1):
                total = (side_above + side_below) + (get(1, z, up) + get(1, z, down))
                total = total + (jnp.where(first, main_w, side_w) + jnp.where(last, main_e, side_e))
                put(1, z, at, (total - rhs(1, z, tile_rows(t))) * side_weight[t])
            carry[t] = [main, above, side, side_above]


def inner_kernel(dims, pos_ref, dm_ref, ds_ref, pre_ref):
    main_coef, side_coef = coefficients(pos_ref, dims)
    scale = 1.0 / DT
    zero = jnp.zeros((H, CX), F32)
    for i in range(PRE):
        for part in range(2):
            pre_ref[i, part, 0:PADR] = zero
            pre_ref[i, part, PADR + EY:PADR + EY + PADR] = zero

    def rhs(part, z, rows):
        return (ds_ref if part else dm_ref)[z - H + 1, rows] * scale

    for z in range(*pre_planes(0)):
        for t in range(TILES):
            pre_ref[pre_index(0, z), 0, padded_rows(t)] = -rhs(0, z, tile_rows(t)) * main_coef[t]
            pre_ref[pre_index(0, z), 1, padded_rows(t)] = -rhs(1, z, tile_rows(t)) * side_coef[t]
    for level in range(1, SWEEPS - 1):
        def get(part, z, rows, level=level):
            return pre_ref[pre_index(level - 1, z), part, rows]

        def put(part, z, rows, value, level=level):
            pre_ref[pre_index(level, z), part, rows] = value

        relax(level, range(*pre_planes(level)), get, put, rhs, lambda z: (main_coef, side_coef))


def sweep_kernel(
    dims, pos_ref, dm_ref, ds_ref, pre_ref, lo_ref, hi_ref, late_lo_ref, late_hi_ref, pred_ref, pres_ref, vel_out, pres_out,
    b_ref, phi_ref, vel_buf, pres_buf, sems,
):
    lo_z, hi_z = edges(pos_ref, dims)[4:6]
    main_coef, side_coef = coefficients(pos_ref, dims)
    scale = 1.0 / DT
    lane = iota((H, CX), 1)
    first, last = lane == 0, lane == CX - 1
    zero = jnp.zeros((H, CX), F32)
    near = jnp.logical_or(lane < H - 1, lane >= CX - H + 1)
    ends = jnp.logical_or(lane < H, lane >= CX - H)
    lo_scale, hi_scale = lo_z * scale, hi_z * scale
    low_coef = [[c * lo_z for c in main_coef], [c * lo_z for c in side_coef]]
    high_coef = [[c * hi_z for c in main_coef], [c * hi_z for c in side_coef]]

    def weights(z):
        return low_coef if z < H else high_coef if z >= H + CZ else (main_coef, side_coef)

    outer = list(range(pre_planes(0)[0])) + list(range(pre_planes(0)[1], EZ))
    place = {z: i for i, z in enumerate(outer)}

    for z in range(EZ):
        for part in range(2):
            for buf in range(2):
                phi_ref[buf, part, z, 0:PADR] = zero
                phi_ref[buf, part, z, PADR + EY:PADR + EY + PADR] = zero
    sub = iota((H, CX), 0)

    def arrived(early, late, t, low):
        def planes(i):
            depth = H - i if low else i + 1
            if t in (0, TILES - 1):
                if i == H:
                    return late[H - 1 if t == 0 else H]
                depth = depth if t == 0 else H - depth
                return late[depth - 1] if 0 < depth < H else zero
            value = early[i, tile_rows(t - 1)]
            for k, edge, row in ((0, 1, 0), (1, TILES - 2, H - 1)):
                if t == edge:
                    fix = late[H + 3 + k, i:i + 1] if i < H else late[H + 5, k:k + 1]
                    value = value + jnp.where(sub == row, fix, 0.0)
            return value

        if t in (0, TILES - 1):
            fold = late[H + 1 if t == 0 else H + 2]
        else:
            fold = early[H + 1, tile_rows(t - 1)]
            for k, edge, row in ((0, 1, 0), (1, TILES - 2, H - 1)):
                if t == edge:
                    fold = fold + jnp.where(sub == row, late[H + 5, 2 + k:3 + k], 0.0)
        return planes, fold

    for t in range(TILES):
        rows = tile_rows(t)
        lo_planes, lo_fold = arrived(lo_ref, late_lo_ref, t, True)
        hi_planes, hi_fold = arrived(hi_ref, late_hi_ref, t, False)
        folded = (lo_fold * lo_scale, hi_fold * hi_scale)
        for z in outer:
            low = z < EZ // 2
            halo, fold, factor = (lo_planes, folded[0], lo_scale) if low else (hi_planes, folded[1], hi_scale)
            if z < H or z >= H + CZ:
                g = z if low else z - H - CZ
                main = halo(g) * factor
                side = jnp.where(near, roll(fold, -(14 * g + 7), 1), 0.0)
                if z in (H - 1, H + CZ):
                    k = 0 if low else SZ - 1
                    main = main + dm_ref[k, rows] * factor
                    side = side + ds_ref[k, rows] * factor
            else:
                main = dm_ref[z - H + 1, rows] * scale + halo(H) * factor
                side = ds_ref[z - H + 1, rows] * scale + jnp.where(ends, roll(fold, -120, 1), 0.0)
            b_ref[0, place[z], rows] = main
            b_ref[1, place[z], rows] = side
            cm, cs = weights(z)
            phi_ref[0, 0, z, padded_rows(t)] = -main * cm[t]
            phi_ref[0, 1, z, padded_rows(t)] = -side * cs[t]

    def rhs(part, z, rows):
        if z in place:
            return b_ref[part, place[z], rows]
        return (ds_ref if part else dm_ref)[z - H + 1, rows] * scale

    def reader(level):
        known = range(*pre_planes(level))

        def get(part, z, rows):
            if z in known:
                return pre_ref[pre_index(level, z), part, rows]
            return phi_ref[level % 2, part, z, rows]

        return get

    for level in range(1, SWEEPS):
        lo, hi = pre_planes(level)

        def put(part, z, rows, value, level=level):
            phi_ref[level % 2, part, z, rows] = value

        runs = ((level, lo), (hi, EZ - level)) if hi > lo else ((level, EZ - level),)
        for run in runs:
            relax(level, range(*run), reader(level - 1), put, rhs, weights)

    get = reader(SWEEPS - 1)
    chunk = 4
    copies = []
    for c in range(CZ // chunk):
        for z in range(c * chunk, (c + 1) * chunk):
            for t in range(CY // H):
                rows = tile_rows(t)
                at, up, down = padded_rows(t + 1), padded_rows(t + 1, 1), padded_rows(t + 1, -1)
                main, side = get(0, z + H, at), get(1, z + H, at)
                west = jnp.where(first, roll(side, 1, 1), roll(main, 1, 1))
                east = jnp.where(last, roll(side, -1, 1), roll(main, -1, 1))
                half = DT * 0.5
                vel_buf[0, z, rows] = pred_ref[0, z, rows] - half * (east - west)
                vel_buf[1, z, rows] = pred_ref[1, z, rows] - half * (get(0, z + H, up) - get(0, z + H, down))
                vel_buf[2, z, rows] = pred_ref[2, z, rows] - half * (get(0, z + H + 1, at) - get(0, z + H - 1, at))
                pres_buf[z, rows] = pres_ref[z, rows] + main
        part = pl.ds(c * chunk, chunk)
        copies.append(pltpu.make_async_copy(vel_buf.at[:, part], vel_out.at[:, part], sems.at[2 * c]))
        copies.append(pltpu.make_async_copy(pres_buf.at[part], pres_out.at[part], sems.at[2 * c + 1]))
        for copy in copies[-2:]:
            copy.start()
    for copy in copies:
        copy.wait()


def swap(up, down, axis):
    count = lax.axis_size(axis)
    forward = [(i, (i + 1) % count) for i in range(count)]
    backward = [(j, i) for i, j in forward]
    return lax.ppermute(up, axis, forward), lax.ppermute(down, axis, backward)


def shape(*dims):
    return jax.ShapeDtypeStruct(dims, F32)


SMEM = pl.BlockSpec(memory_space=pltpu.SMEM)
VMEM = pl.BlockSpec(memory_space=pltpu.VMEM)


ANY = pl.BlockSpec(memory_space=pl.ANY)


def in_hbm(x):
    return pltpu.with_memory_space_constraint(x, pltpu.HBM)


def in_vmem(*dims, dtype=F32):
    return pltpu.VMEM(dims, dtype)


MIB = 1024 * 1024
ENTRY_LIMIT = 24


class Place:
    def __getitem__(self, k):
        return lax.axis_index(("gx", "gy", "gz")[k])


def call(kernel, scalars, arrays, outs, scratch=(), in_specs=None, out_specs=None, limit=24, cost=0):
    return pl.pallas_call(
        functools.partial(kernel, Place()),
        out_shape=outs,
        in_specs=[SMEM] * len(scalars) + list(in_specs or [VMEM] * len(arrays)),
        out_specs=out_specs or [VMEM] * len(outs),
        scratch_shapes=list(scratch),
        compiler_params=pltpu.CompilerParams(vmem_limit_bytes=limit * MIB),
        cost_estimate=pl.CostEstimate(flops=cost, bytes_accessed=cost // 64, transcendentals=0) if cost else None,
    )(*scalars, *arrays)


def shards(
    velocity, adjoint, pressure, viscosity, disk_cells, disk_turbine, disk_weight, disk_dweight, yaw, thrust_coef, owner_slot,
):
    axes = ("gx", "gy", "gz")
    n_gx, n_gy, n_gz = (lax.axis_size(a) for a in axes)
    n_dev = n_gx * n_gy * n_gz
    dims = (n_dev, n_gx, n_gy, n_gz)
    turbines = owner_slot.shape[0]
    if turbines % CX:
        owner_slot = jnp.pad(owner_slot, (0, CX - turbines % CX))
    owner = owner_slot.reshape(-1, CX)
    cells, turbine, weight = (a.reshape(1, -1) for a in (disk_cells, disk_turbine, disk_weight))

    payload, xr, xl, yr, yl, zr, zl, fields, index, scale, table = call(
        functools.partial(entry_kernel, n_dev, n_gy),
        (in_hbm(yaw), in_hbm(thrust_coef)),
        tuple(in_hbm(a) for a in (velocity, adjoint, viscosity, cells, turbine, weight, disk_dweight, owner)),
        (
            shape(n_dev, CX), in_vmem(2, CY, CX), in_vmem(2, CY, CX), in_vmem(6 * CZ, CX), in_vmem(6 * CZ, CX),
            in_vmem(6, CY, CX), in_vmem(6, CY, CX), in_vmem(7, CZ, CY, CX), in_vmem(2, cells.shape[1], dtype=jnp.int32),
            in_vmem(*weight.shape), in_vmem(*owner.shape, dtype=jnp.int32),
        ),
        (pltpu.VMEM((n_dev, CX), F32), pltpu.SemaphoreType.DMA((8,))),
        [ANY, ANY, ANY] + [VMEM] * 5,
        [ANY] + [VMEM] * 10,
        limit=ENTRY_LIMIT,
    )
    got = lax.all_to_all(payload, axes, 0, 0, tiled=True)
    ylo, yhi = swap(yr, yl, "gy")
    zlo, zhi = swap(zr, zl, "gz")
    count = n_gx
    xlo = lax.ppermute(xr, "gx", [(i, (i + 1) % count) for i in range(count)])
    xlo, xl = lax.optimization_barrier((xlo, xl))
    xhi = lax.ppermute(xl, "gx", [((i + 1) % count, i) for i in range(count)])
    faces = (xlo, xhi, ylo, yhi, zlo, zhi)

    pred_base, dual_base = call(
        stencil_kernel, (), (fields,), (in_vmem(3, CZ, CY, CX), in_vmem(3, CZ, CY, CX)), cost=1 << 30
    )
    force = call(
        functools.partial(force_kernel, dims), (), (index, scale, table, got), (shape(3, CZ, CY, CX),), cost=1 << 30
    )[0]
    predicted, dm, ds, xr, xl = call(
        functools.partial(flow_kernel, dims),
        (),
        (pred_base, force, fields) + faces,
        (shape(3, CZ, CY, CX), shape(SZ, EY, CX), shape(SZ, EY, CX), shape(3, EY, CX), shape(3, EY, CX)),
    )
    adjoint_next, yaw_grad, position_grad = call(
        functools.partial(dual_kernel, dims),
        (in_hbm(yaw), in_hbm(thrust_coef)),
        (dual_base, force, fields, got) + faces,
        (shape(3, CZ, CY, CX), shape(1, 4), shape(2, 4)),
        (pltpu.VMEM((3, CZ, CY, CX), F32), pltpu.SemaphoreType.DMA((3,))),
        out_specs=[ANY, VMEM, VMEM],
        cost=1 << 30,
    )
    lo, hi = swap(xr, xl, "gx")
    dm, ds, up, down, above, below = call(
        functools.partial(x_kernel, dims), (), (dm, ds, lo, hi),
        (
            shape(SZ, EY, CX), shape(SZ, EY, CX), shape(27, H, CX), shape(27, H, CX),
            shape(H + 2, CY, CX), shape(H + 2, CY, CX),
        ),
    )
    lo, hi = swap(up, down, "gy")
    early_lo, early_hi = swap(above, below, "gz")
    lo, yaw_grad = lax.optimization_barrier((lo, yaw_grad))
    dm, ds, above, below = call(
        functools.partial(y_kernel, dims), (), (dm, ds, lo, hi),
        (shape(SZ, EY, CX), shape(SZ, EY, CX), shape(LATE, H, CX), shape(LATE, H, CX)),
    )
    late_lo, late_hi = swap(above, below, "gz")
    pre = call(
        functools.partial(inner_kernel, dims), (), (dm, ds), (shape(PRE, 2, EY + 2 * PADR, CX),), cost=1 << 30
    )[0]
    velocity_next, pressure_next = call(
        functools.partial(sweep_kernel, dims), (), (dm, ds, pre, early_lo, early_hi, late_lo, late_hi, predicted, pressure),
        (shape(3, CZ, CY, CX), shape(CZ, CY, CX)),
        (
            pltpu.VMEM((2, EZ - CZ + 2, EY, CX), F32), pltpu.VMEM((2, 2, EZ, EY + 2 * PADR, CX), F32),
            pltpu.VMEM((3, CZ, CY, CX), F32), pltpu.VMEM((CZ, CY, CX), F32), pltpu.SemaphoreType.DMA((8,)),
        ),
        out_specs=[ANY, ANY],
    )
    return velocity_next, adjoint_next, pressure_next, yaw_grad.reshape(-1), position_grad


def solution(mesh):
    axes = ("gx", "gy", "gz")
    grid = P(None, "gz", "gy", "gx")
    cell = P("gz", "gy", "gx")
    flat = P(axes)
    return jax.shard_map(
        shards,
        mesh=mesh,
        in_specs=(grid, grid, cell, cell, flat, flat, flat, P(None, axes), flat, flat, P()),
        out_specs=(grid, grid, cell, flat, P(None, axes)),
        check_vma=False,
    )
```

```python
import functools

import jax
import jax.numpy as jnp
from jax import lax
from jax.experimental import pallas as pl
from jax.experimental.pallas import tpu as pltpu
from jax.sharding import PartitionSpec as P

SWEEPS = 8
DT = 0.2
F32 = jnp.float32
BF16 = jnp.bfloat16
CZ, CY, CX = 16, 32, 128
KJ = CZ * CY
H = 8
EZ, EY = CZ + 2 * H, CY + 2 * H
SZ = CZ + 2
TILES = EY // H
PADR = 8
PER = 16
WIN = 64
YAW = 112
NN = (((1,), (0,)), ((), ()))
NT = (((1,), (1,)), ((), ()))
TN = (((0,), (0,)), ((), ()))


def iota(shape, dim):
    return lax.broadcasted_iota(jnp.int32, shape, dim)


def pieces(x, count):
    parts = []
    for _ in range(count):
        head = x.astype(BF16)
        parts.append(head)
        x = x - head.astype(F32)
    return parts


def dots(left, right, dims):
    total = None
    for a in left:
        for b in right:
            term = lax.dot_general(a, b, dims, preferred_element_type=F32)
            total = term if total is None else total + term
    return total


def onehot(mask):
    return jnp.where(mask, 1.0, 0.0).astype(BF16)


def roll(x, shift, axis):
    return pltpu.roll(x, shift % x.shape[axis], axis)


def entry_onehots(cells):
    row = lax.shift_right_logical(cells, 7)
    lane = jnp.bitwise_and(cells, CX - 1)
    count = cells.shape[1]
    rows = onehot(iota((KJ, count), 0) == row)
    lanes = iota((CX, count), 0) == lane
    return rows, lanes


def window_lane(turbine, bx, n_gy):
    column_x = lax.shift_right_logical(turbine, 4) // n_gy
    return WIN + (column_x - bx + 1) * PER + jnp.bitwise_and(turbine, PER - 1)


def lookup(table_ref, turbine):
    count = turbine.shape[1]
    table = table_ref[...]
    owner = lax.shift_right_logical(table, 2).astype(F32)
    which = jnp.bitwise_and(table, 3).astype(F32)
    rows = table.shape[0]
    high = lax.shift_right_logical(turbine, 7)
    low = onehot(iota((CX, count), 0) == jnp.bitwise_and(turbine, CX - 1))
    keep = iota((rows, count), 0) == high
    out = []
    for part in (owner, which):
        picked = dots([part.astype(BF16)], [low], NN)
        picked = jnp.sum(jnp.where(keep, picked, 0.0), axis=0, keepdims=True)
        out.append(picked.astype(jnp.int32))
    return out


def entry_kernel(
    n_dev, n_gy, pos_ref, yaw_ref, ct_ref, vel_hbm, adj_hbm, visc_hbm, cells_ref, turb_ref, weight_ref, dweight_ref, owner_ref,
    pay_ref, xr_ref, xl_ref, yr_ref, yl_ref, zr_ref, zl_ref, fld_ref, index_ref, scale_ref, table_ref, out_ref, sems,
):
    order = (0, 3, 4, 1, 2, 5, 6)
    copies = {}
    for f in order:
        hbm = vel_hbm.at[f] if f < 3 else adj_hbm.at[f - 3] if f < 6 else visc_hbm
        copies[f] = pltpu.make_async_copy(hbm, fld_ref.at[f], sems.at[f])
        copies[f].start()
    bx = pos_ref[0]
    cells, turbine, weight = cells_ref[...], turb_ref[...], weight_ref[...]
    index_ref[0:1, :] = cells
    index_ref[1:2, :] = turbine
    scale_ref[...] = weight
    table_ref[...] = owner_ref[...]
    count = cells.shape[1]
    rows, lanes = entry_onehots(cells)
    owner, which = lookup(owner_ref, turbine)
    to_owner = onehot(iota((n_dev, count), 0) == owner)
    in_window = onehot(iota((CX, count), 0) == window_lane(turbine, bx, n_gy))

    columns = []
    for f in order[:3]:
        copies[f].wait()
        columns += pieces(fld_ref[f].reshape(KJ, CX), 2)
    at_row = dots([jnp.concatenate(columns, axis=1)], [rows], TN)
    gathered = []
    for k in range(3):
        both = at_row[2 * k * CX:(2 * k + 1) * CX] + at_row[(2 * k + 1) * CX:(2 * k + 2) * CX]
        gathered.append(jnp.sum(jnp.where(lanes, both, 0.0), axis=0, keepdims=True))
    factors = [weight, dweight_ref[0:1, :], dweight_ref[1:2, :]]
    values = [f * g for f in factors for g in gathered]

    sub = iota((PER, count), 0)
    stacked = jnp.zeros((PER, count), F32)
    for v, value in enumerate(values):
        stacked = jnp.where(sub == v, value, stacked)
    per_slot = jnp.concatenate(
        [jnp.where(which == i, stacked, 0.0) for i in range(4)] + [jnp.zeros((CX - 4 * PER, count), F32)], axis=0
    )
    payload = dots([to_owner], pieces(per_slot, 2), NT)

    speed = jnp.broadcast_to(values[0], (8, count))
    shared = dots(pieces(speed, 2), [in_window], NT)[0:1, :]
    lane = iota((1, CX), 1)
    for i in range(4):
        shared = jnp.where(lane == YAW + i, yaw_ref[i], shared)
        shared = jnp.where(lane == YAW + 4 + i, ct_ref[i], shared)
    out_ref[...] = payload + shared
    leaving = pltpu.make_async_copy(out_ref, pay_ref, sems.at[7])
    leaving.start()

    for f in order[3:]:
        copies[f].wait()
    lane = iota((H, CX), 1)
    for t in range(CY // H):
        at = slice(H * t, H * t + H)
        for half in range(2):
            right = jnp.zeros((H, CX), F32)
            left = jnp.zeros((H, CX), F32)
            for f in range(3):
                for z in range(CZ):
                    spot = 2 * (f * CZ + z) + 1
                    moved = roll(fld_ref[3 * half + f, z, at], spot + 1, 1)
                    right = jnp.where(lane == spot, moved, right)
                    left = jnp.where(lane == spot + 1, moved, left)
            xr_ref[half, at] = right
            xl_ref[half, at] = left
    for f in range(6):
        yr_ref[f * CZ:(f + 1) * CZ, :] = fld_ref[f, :, CY - 1, :]
        yl_ref[f * CZ:(f + 1) * CZ, :] = fld_ref[f, :, 0, :]
        zr_ref[f] = fld_ref[f, CZ - 1]
        zl_ref[f] = fld_ref[f, 0]
    leaving.wait()


def turbine_terms(speed, yaw, thrust_coef):
    cosine = jnp.cos(yaw)
    sine = jnp.sin(yaw)
    magnitude = jnp.abs(speed)
    force = 0.5 * thrust_coef * speed * magnitude * cosine * cosine
    weighting = 1.5 * thrust_coef * speed * magnitude * cosine * cosine * cosine
    return cosine, sine, magnitude, force, weighting


def owner_outputs(got, yaw_ref, ct_ref, yaw_out, pos_out):
    total = jnp.sum(got, axis=0, keepdims=True)
    total = jnp.broadcast_to(total, (8, CX))
    lane = iota((8, CX), 1)
    yaw = jnp.zeros((8, CX), F32)
    ct = jnp.zeros((8, CX), F32)
    for i in range(4):
        yaw = jnp.where(lane == i * PER, yaw_ref[i], yaw)
        ct = jnp.where(lane == i * PER, ct_ref[i], ct)

    def at(v):
        return roll(total, -v, 1)

    speed, dual_x, dual_y = total, at(1), at(2)
    cosine, sine, magnitude, force, weighting = turbine_terms(speed, yaw, ct)
    yaw_grad = -1.5 * ct * magnitude * magnitude * magnitude * cosine * cosine * sine + force * (
        sine * dual_x - cosine * dual_y
    )
    grads = [yaw_grad]
    for r in range(2):
        grads.append(weighting * at(3 + 3 * r) - force * cosine * at(4 + 3 * r) - force * sine * at(5 + 3 * r))
    packed = []
    for grad in grads:
        out = jnp.zeros((8, CX), F32)
        for i in range(4):
            out = jnp.where(lane == i, roll(grad, -(PER - 1) * i, 1), out)
        packed.append(out)
    yaw_out[...] = packed[0][0:1, 0:4]
    pos_out[0:1, :] = packed[1][0:1, 0:4]
    pos_out[1:2, :] = packed[2][0:1, 0:4]


def window_terms(got, n_dev, n_gx, n_gy, n_gz, bx, by, owner_ref):
    lane = iota((1, CX), 1)
    inside = jnp.logical_and(lane >= WIN, lane < WIN + 3 * PER)
    row = iota((n_dev, CX), 0)
    speed = jnp.zeros((1, CX), F32)
    for delta in range(-2, 3):
        base = ((bx + delta) * n_gy + by) * n_gz
        keep = jnp.logical_and(row >= base, row < base + n_gz)
        part = jnp.sum(jnp.where(keep, got, 0.0), axis=0, keepdims=True)
        part = jnp.broadcast_to(jnp.where(inside, part, 0.0), (8, CX))
        speed = speed + roll(part, delta * PER, 1)[0:1, :]
    speed = jnp.where(inside, speed, 0.0)

    table = owner_ref[...]
    sub = iota(table.shape, 0)
    slots = jnp.zeros((1, CX), jnp.int32)
    for j in range(3):
        column_x = jnp.clip(bx - 1 + j, 0, n_gx - 1)
        first = (column_x * n_gy + by) * PER
        picked = jnp.sum(jnp.where(sub == first // CX, table, 0), axis=0, keepdims=True)
        picked = jnp.broadcast_to(picked, (8, CX))
        moved = pltpu.roll(picked, jnp.bitwise_and(WIN + PER * j - first, CX - 1), 1)[0:1, :]
        here = jnp.logical_and(lane >= WIN + PER * j, lane < WIN + PER * (j + 1))
        slots = jnp.where(here, moved, slots)
    owner = onehot(iota((n_dev, CX), 0) == lax.shift_right_logical(slots, 2))
    which = jnp.bitwise_and(slots, 3)
    found = dots(pieces(got, 3), [owner], TN)
    yaw = jnp.zeros((1, CX), F32)
    ct = jnp.zeros((1, CX), F32)
    for i in range(4):
        yaw = jnp.where(which == i, found[YAW + i:YAW + i + 1, :], yaw)
        ct = jnp.where(which == i, found[YAW + 4 + i:YAW + 5 + i, :], ct)
    cosine, sine, magnitude, force, weighting = turbine_terms(speed, yaw, ct)
    keep = lambda x: jnp.where(inside, x, 0.0)
    return keep(force * cosine), keep(force * sine), keep(weighting)


def edges(pos_ref, dims):
    n_dev, n_gx, n_gy, n_gz = dims
    out = []
    for k, count in enumerate((n_gx, n_gy, n_gz)):
        out.append(jnp.where(pos_ref[k] > 0, 1.0, 0.0))
        out.append(jnp.where(pos_ref[k] < count - 1, 1.0, 0.0))
    return out


def tile_rows(t):
    return slice(H * t, H * t + H)


def south_of(ref, index, t, sub):
    if t > 0:
        return ref[index + (slice(H * t - 1, H * t + H - 1),)]
    return jnp.where(sub == 0, 0.0, roll(ref[index + (tile_rows(0),)], 1, 0))


def north_of(ref, index, t, sub):
    if t < CY // H - 1:
        return ref[index + (slice(H * t + 1, H * t + H + 1),)]
    return jnp.where(sub == H - 1, 0.0, roll(ref[index + (tile_rows(t),)], -1, 0))


def force_kernel(dims, pos_ref, index_ref, scale_ref, owner_ref, got_ref, field_ref):
    n_dev, n_gx, n_gy, n_gz = dims
    bx, by = pos_ref[0], pos_ref[1]
    terms = window_terms(got_ref[...], n_dev, n_gx, n_gy, n_gz, bx, by, owner_ref)
    cells, turbine, weight = index_ref[0:1, :], index_ref[1:2, :], scale_ref[...]
    count = cells.shape[1]
    rows, lanes = entry_onehots(cells)
    in_window = onehot(iota((CX, count), 0) == window_lane(turbine, bx, n_gy))
    stacked = jnp.concatenate([jnp.broadcast_to(t, (8, CX)) for t in terms], axis=0)
    per_entry = dots(pieces(stacked, 2), [in_window], NN)
    for c in range(3):
        value = per_entry[8 * c:8 * c + 1, :] * weight
        if c < 2:
            value = -value
        spread = jnp.where(lanes, value, 0.0)
        field_ref[c] = dots([rows], pieces(spread, 2), NT).reshape(CZ, CY, CX)


def stencil(fld_ref, f, out, comp):
    lane = iota((H, CX), 1)
    sub = iota((H, CX), 0)
    zero = jnp.zeros((H, CX), F32)
    for t in range(CY // H):
        at = tile_rows(t)
        below, tile = zero, fld_ref[f, 0, at]
        for z in range(CZ):
            above = fld_ref[f, z + 1, at] if z < CZ - 1 else zero
            south, north = south_of(fld_ref, (f, z), t, sub), north_of(fld_ref, (f, z), t, sub)
            west = jnp.where(lane == 0, 0.0, roll(tile, 1, 1))
            east = jnp.where(lane == CX - 1, 0.0, roll(tile, -1, 1))
            lap = (above + below) + (north + south) + (east + west) - 6.0 * tile
            rate = fld_ref[6, z, at] * lap + (west - tile if f < 3 else east - tile)
            out[comp, z, at] = tile + DT * rate
            below, tile = tile, above


def stencil_kernel(pos_ref, fld_ref, pred_ref):
    for f in range(3):
        stencil(fld_ref, f, pred_ref, f)


def merge_faces(face_ref, half, xlo_ref, xhi_ref, bounds):
    odd = jnp.bitwise_and(iota((H, CX), 1), 1) == 1
    for t in range(CY // H):
        at = tile_rows(t)
        face_ref[at] = jnp.where(odd, xlo_ref[half, at] * bounds[0], roll(xhi_ref[half, at] * bounds[1], -2, 1))


def add_faces(f, first, out, given, field_ref, fld_ref, bounds, face_ref, ylo_ref, yhi_ref, zlo_ref, zhi_ref):
    lo_x, hi_x, lo_y, hi_y, lo_z, hi_z = bounds
    lane = iota((H, CX), 1)
    sub = iota((H, CX), 0)
    flow = f < 3
    comp = f - first
    for t in range(CY // H):
        at = tile_rows(t)
        for z in range(CZ):
            spot = f * CZ + z
            moved = roll(face_ref[at], -(2 * (spot % (3 * CZ)) + 1), 1)
            west = jnp.where(lane == 0, moved, 0.0)
            east = jnp.where(lane == CX - 1, moved, 0.0)
            lap = west + east
            if t == 0:
                lap = lap + jnp.where(sub == 0, ylo_ref[spot:spot + 1, :] * lo_y, 0.0)
            if t == CY // H - 1:
                lap = lap + jnp.where(sub == H - 1, yhi_ref[spot:spot + 1, :] * hi_y, 0.0)
            if z == 0:
                lap = lap + zlo_ref[f, at] * lo_z
            if z == CZ - 1:
                lap = lap + zhi_ref[f, at] * hi_z
            rate = fld_ref[6, z, at] * lap + (west if flow else east)
            if f < 2:
                rate = rate + field_ref[f, z, at]
            if f == 3:
                rate = rate + field_ref[2, z, at]
            out[comp, z, at] = given[comp, z, at] + DT * rate


def fold_shift(z):
    return H + 16 * (z % 8)


def flow_kernel(
    dims, pos_ref, base_ref, field_ref, fld_ref, xlo_ref, xhi_ref, ylo_ref, yhi_ref, zlo_ref, zhi_ref,
    pred_ref, dm_ref, ds_ref, xr_ref, xl_ref, face_ref,
):
    bounds = edges(pos_ref, dims)
    merge_faces(face_ref, 0, xlo_ref, xhi_ref, bounds)
    for f in range(3):
        add_faces(f, 0, pred_ref, base_ref, field_ref, fld_ref, bounds, face_ref, ylo_ref, yhi_ref, zlo_ref, zhi_ref)
    lane = iota((H, CX), 1)
    sub = iota((H, CX), 0)
    zero = jnp.zeros((H, CX), F32)
    for r in range(EY // H):
        at = tile_rows(r)
        t = r - 1
        inside = 0 <= t < CY // H
        for k in range(SZ):
            z = k - 1
            main, side = zero, zero
            if inside and 0 <= z < CZ:
                own = tile_rows(t)
                p0 = pred_ref[0, z, own]
                west, east = roll(p0, 1, 1), roll(p0, -1, 1)
                div = jnp.where(lane == CX - 1, 0.0, east) - jnp.where(lane == 0, 0.0, west)
                div = div + (north_of(pred_ref, (1, z), t, sub) - south_of(pred_ref, (1, z), t, sub))
                if z < CZ - 1:
                    div = div + pred_ref[2, z + 1, own]
                if z > 0:
                    div = div - pred_ref[2, z - 1, own]
                main = 0.5 * div
                side = jnp.where(lane == CX - 1, 0.5 * east, jnp.where(lane == 0, -0.5 * west, 0.0))
            elif inside:
                main = 0.5 * pred_ref[2, 0, tile_rows(t)] if z < 0 else -0.5 * pred_ref[2, CZ - 1, tile_rows(t)]
            elif 0 <= z < CZ and t < 0:
                main = jnp.where(sub == H - 1, 0.5 * roll(pred_ref[1, z, 0:H], -1, 0), 0.0)
            elif 0 <= z < CZ:
                main = jnp.where(sub == 0, -0.5 * roll(pred_ref[1, z, CY - H:CY], 1, 0), 0.0)
            dm_ref[k, at] = main
            ds_ref[k, at] = side
    for r in range(EY // H):
        at = tile_rows(r)
        right, left = [zero] * 3, [zero] * 3
        for k in range(SZ):
            if not 0 < r < EY // H - 1 and not 0 < k < SZ - 1:
                continue
            main, side = dm_ref[k, at], ds_ref[k, at]
            g = k % 8
            mine = jnp.logical_and(lane >= 16 * g, lane < 16 * g + 16)
            right[k // 8] = jnp.where(mine, roll(jnp.where(lane < H, side, main), fold_shift(k), 1), right[k // 8])
            left[k // 8] = jnp.where(mine, roll(jnp.where(lane < H, main, side), fold_shift(k), 1), left[k // 8])
        for i in range(3):
            xr_ref[i, at] = right[i]
            xl_ref[i, at] = left[i]


def dual_kernel(
    dims, pos_ref, field_ref, fld_ref, xlo_ref, xhi_ref, ylo_ref, yhi_ref, zlo_ref, zhi_ref,
    dual_out, dual_ref, face_ref, sems,
):
    bounds = edges(pos_ref, dims)
    merge_faces(face_ref, 1, xlo_ref, xhi_ref, bounds)
    copies = []
    for f in range(3, 6):
        stencil(fld_ref, f, dual_ref, f - 3)
        add_faces(f, 3, dual_ref, dual_ref, field_ref, fld_ref, bounds, face_ref, ylo_ref, yhi_ref, zlo_ref, zhi_ref)
        copies.append(pltpu.make_async_copy(dual_ref.at[f - 3], dual_out.at[f - 3], sems.at[f - 3]))
        copies[-1].start()
    for copy in copies:
        copy.wait()


def owner_kernel(pos_ref, yaw_ref, ct_ref, got_ref, yaw_out, pos_out):
    owner_outputs(got_ref[...], yaw_ref, ct_ref, yaw_out, pos_out)


def x_kernel(
    dims, pos_ref, dm_ref, ds_ref, lo_ref, hi_ref, om_ref, os_ref, up_ref, down_ref, above_ref, below_ref
):
    in_lo, in_hi = edges(pos_ref, dims)[0:2]
    lane = iota((H, CX), 1)
    head, tail = lane < H, lane >= CX - H
    zero = jnp.zeros((H, CX), F32)
    for r in range(EY // H):
        at = tile_rows(r)
        lows = [lo_ref[i, at] * in_lo for i in range(3)]
        highs = [hi_ref[i, at] * in_hi for i in range(3)]
        for z in range(SZ):
            lo = roll(lows[z // 8], -fold_shift(z), 1)
            hi = roll(highs[z // 8], -fold_shift(z), 1)
            om_ref[z, at] = dm_ref[z, at] + jnp.where(head, lo, jnp.where(tail, hi, 0.0))
            os_ref[z, at] = ds_ref[z, at] + jnp.where(tail, lo, jnp.where(head, hi, 0.0))
    for out, row, edge in ((up_ref, CY, H + CY), (down_ref, H, H - 1)):
        for i in range(3):
            fold = zero
            out[18 + i] = zero
            out[24 + i] = zero
            for g in range(min(8, SZ - 8 * i)):
                z = 8 * i + g
                out[z] = om_ref[z, row:row + H]
                mine = jnp.logical_and(lane >= 16 * g, lane < 16 * g + 16)
                fold = jnp.where(mine, roll(os_ref[z, row:row + H], fold_shift(z), 1), fold)
                out[18 + i, g:g + 1] = om_ref[z, edge:edge + 1]
                out[24 + i, g:g + 1] = os_ref[z, edge:edge + 1]
            out[21 + i] = fold
    for out, plane in ((above_ref, up_plane), (below_ref, down_plane)):
        for r in range(1, 1 + CY // H):
            for i in range(H + 1):
                out[i, tile_rows(r - 1)] = om_ref[plane(i), tile_rows(r)]
            out[H + 1, tile_rows(r - 1)] = fold_planes(lambda i: os_ref[plane(i), tile_rows(r)])


def up_plane(i):
    return CZ - H + 1 + i


def down_plane(i):
    return i + 1 if i < H else 0


def fold_planes(side):
    lane = iota((H, CX), 1)
    fold = jnp.zeros((H, CX), F32)
    for i in range(H + 1):
        mine = jnp.logical_and(lane >= 14 * i, lane < (14 * i + 14 if i < H else CX))
        fold = jnp.where(mine, roll(side(i), 14 * i + 7 if i < H else 120, 1), fold)
    return fold


LATE = H + 1 + 2 + 3


def y_kernel(dims, pos_ref, dm_ref, ds_ref, lo_ref, hi_ref, om_ref, os_ref, above_ref, below_ref):
    in_lo, in_hi = edges(pos_ref, dims)[2:4]
    lane = iota((H, CX), 1)
    sub = iota((H, CX), 0)
    ends = jnp.logical_or(lane < H, lane >= CX - H)
    last = EY // H - 1
    for r in range(EY // H):
        at = tile_rows(r)
        for z in range(SZ):
            tile, g = z // 8, z % 8
            main, side = dm_ref[z, at], ds_ref[z, at]
            if r == 0:
                main = main + lo_ref[z] * in_lo
                side = side + jnp.where(ends, roll(lo_ref[21 + tile], -fold_shift(z), 1) * in_lo, 0.0)
            if r == 1:
                main = main + jnp.where(sub == 0, lo_ref[18 + tile, g:g + 1, :] * in_lo, 0.0)
                side = side + jnp.where(sub == 0, lo_ref[24 + tile, g:g + 1, :] * in_lo, 0.0)
            if r == last - 1:
                main = main + jnp.where(sub == H - 1, hi_ref[18 + tile, g:g + 1, :] * in_hi, 0.0)
                side = side + jnp.where(sub == H - 1, hi_ref[24 + tile, g:g + 1, :] * in_hi, 0.0)
            if r == last:
                main = main + hi_ref[z] * in_hi
                side = side + jnp.where(ends, roll(hi_ref[21 + tile], -fold_shift(z), 1) * in_hi, 0.0)
            om_ref[z, at] = main
            os_ref[z, at] = side
    lower, upper = tile_rows(0), tile_rows(last)
    for out, plane, depth in (
        (above_ref, up_plane, lambda i: H - i),
        (below_ref, down_plane, lambda i: i + 1),
    ):
        at_depth = {depth(i): plane(i) for i in range(H)}
        for d in range(1, H):
            out[d - 1] = jnp.where(sub >= d, om_ref[at_depth[d], lower], om_ref[at_depth[H - d], upper])
        out[H - 1] = om_ref[plane(H), lower]
        out[H] = om_ref[plane(H), upper]
        out[H + 1] = fold_planes(lambda i: os_ref[plane(i), lower])
        out[H + 2] = fold_planes(lambda i: os_ref[plane(i), upper])
        out[H + 5] = jnp.zeros((H, CX), F32)
        for given, factor, k in ((lo_ref, in_lo, 0), (hi_ref, in_hi, 1)):
            for i in range(H + 1):
                tile, g = plane(i) // 8, plane(i) % 8
                row = given[18 + tile, g:g + 1, :] * factor
                if i < H:
                    out[H + 3 + k, i:i + 1] = row
                else:
                    out[H + 5, k:k + 1] = row
            side = fold_planes(lambda i: jnp.broadcast_to(given[24 + plane(i) // 8, plane(i) % 8:plane(i) % 8 + 1, :], (H, CX)))
            out[H + 5, 2 + k:3 + k] = side[0:1] * factor


def pre_planes(level):
    return (H + 1 + level, H + CZ - 1 - level) if level < SWEEPS - 1 else (0, 0)


def pre_index(level, z):
    return sum(CZ - 2 - 2 * i for i in range(level)) + z - pre_planes(level)[0]


PRE = sum(CZ - 2 - 2 * i for i in range(SWEEPS - 1))


def padded_rows(t, shift=0):
    return slice(PADR + H * t + shift, PADR + H * t + H + shift)


def coefficients(pos_ref, dims):
    lo_x, hi_x, lo_y, hi_y, lo_z, hi_z = edges(pos_ref, dims)
    lane = iota((H, CX), 1)
    low, high = jnp.where(lane >= CX - H, lo_x, 1.0), jnp.where(lane < H, hi_x, 1.0)
    main = [jnp.full((H, CX), 1.0 / 6.0, F32)] * TILES
    main[0] = main[0] * lo_y
    main[-1] = main[-1] * hi_y
    return main, [c * (low * high) for c in main]


def reached(level, z, t, part):
    depth = max(0, H - z, z - H - CZ + 1)
    return depth + (t in (0, TILES - 1)) + part <= SWEEPS - level


def relax(level, planes, get, put, rhs, weights):
    lane = iota((H, CX), 1)
    first, last = lane == 0, lane == CX - 1
    z0 = planes[0]
    carry = [[get(k, z0 - 1 + i, padded_rows(t)) for k in range(2) for i in range(2)] for t in range(TILES)]
    for z in planes:
        main_weight, side_weight = weights(z)
        for t in range(TILES):
            below, main, side_below, side = carry[t]
            at, up, down = padded_rows(t), padded_rows(t, 1), padded_rows(t, -1)
            above, side_above = get(0, z + 1, at), get(1, z + 1, at)
            main_w, side_w = roll(main, 1, 1), roll(side, 1, 1)
            main_e, side_e = roll(main, -1, 1), roll(side, -1, 1)
            if reached(level, z, t, 0):
                total = (above + below) + (get(0, z, up) + get(0, z, down))
                total = total + (jnp.where(first, side_w, main_w) + jnp.where(last, side_e, main_e))
                put(0, z, at, (total - rhs(0, z, tile_rows(t))) * main_weight[t])
            if reached(level, z, t, 1):
                total = (side_above + side_below) + (get(1, z, up) + get(1, z, down))
                total = total + (jnp.where(first, main_w, side_w) + jnp.where(last, main_e, side_e))
                put(1, z, at, (total - rhs(1, z, tile_rows(t))) * side_weight[t])
            carry[t] = [main, above, side, side_above]


def inner_kernel(dims, pos_ref, dm_ref, ds_ref, pre_ref):
    main_coef, side_coef = coefficients(pos_ref, dims)
    scale = 1.0 / DT
    zero = jnp.zeros((H, CX), F32)
    for i in range(PRE):
        for part in range(2):
            pre_ref[i, part, 0:PADR] = zero
            pre_ref[i, part, PADR + EY:PADR + EY + PADR] = zero

    def rhs(part, z, rows):
        return (ds_ref if part else dm_ref)[z - H + 1, rows] * scale

    for z in range(*pre_planes(0)):
        for t in range(TILES):
            pre_ref[pre_index(0, z), 0, padded_rows(t)] = -rhs(0, z, tile_rows(t)) * main_coef[t]
            pre_ref[pre_index(0, z), 1, padded_rows(t)] = -rhs(1, z, tile_rows(t)) * side_coef[t]
    for level in range(1, SWEEPS - 1):
        def get(part, z, rows, level=level):
            return pre_ref[pre_index(level - 1, z), part, rows]

        def put(part, z, rows, value, level=level):
            pre_ref[pre_index(level, z), part, rows] = value

        relax(level, range(*pre_planes(level)), get, put, rhs, lambda z: (main_coef, side_coef))


def sweep_kernel(
    dims, pos_ref, dm_ref, ds_ref, pre_ref, lo_ref, hi_ref, late_lo_ref, late_hi_ref, pred_ref, pres_ref, vel_out, pres_out,
    b_ref, phi_ref, vel_buf, pres_buf, sems,
):
    lo_z, hi_z = edges(pos_ref, dims)[4:6]
    main_coef, side_coef = coefficients(pos_ref, dims)
    scale = 1.0 / DT
    lane = iota((H, CX), 1)
    first, last = lane == 0, lane == CX - 1
    zero = jnp.zeros((H, CX), F32)
    near = jnp.logical_or(lane < H - 1, lane >= CX - H + 1)
    ends = jnp.logical_or(lane < H, lane >= CX - H)
    lo_scale, hi_scale = lo_z * scale, hi_z * scale
    low_coef = [[c * lo_z for c in main_coef], [c * lo_z for c in side_coef]]
    high_coef = [[c * hi_z for c in main_coef], [c * hi_z for c in side_coef]]

    def weights(z):
        return low_coef if z < H else high_coef if z >= H + CZ else (main_coef, side_coef)

    outer = list(range(pre_planes(0)[0])) + list(range(pre_planes(0)[1], EZ))
    place = {z: i for i, z in enumerate(outer)}

    for z in range(EZ):
        for part in range(2):
            for buf in range(2):
                phi_ref[buf, part, z, 0:PADR] = zero
                phi_ref[buf, part, z, PADR + EY:PADR + EY + PADR] = zero
    sub = iota((H, CX), 0)

    def arrived(early, late, t, low):
        def planes(i):
            depth = H - i if low else i + 1
            if t in (0, TILES - 1):
                if i == H:
                    return late[H - 1 if t == 0 else H]
                depth = depth if t == 0 else H - depth
                return late[depth - 1] if 0 < depth < H else zero
            value = early[i, tile_rows(t - 1)]
            for k, edge, row in ((0, 1, 0), (1, TILES - 2, H - 1)):
                if t == edge:
                    fix = late[H + 3 + k, i:i + 1] if i < H else late[H + 5, k:k + 1]
                    value = value + jnp.where(sub == row, fix, 0.0)
            return value

        if t in (0, TILES - 1):
            fold = late[H + 1 if t == 0 else H + 2]
        else:
            fold = early[H + 1, tile_rows(t - 1)]
            for k, edge, row in ((0, 1, 0), (1, TILES - 2, H - 1)):
                if t == edge:
                    fold = fold + jnp.where(sub == row, late[H + 5, 2 + k:3 + k], 0.0)
        return planes, fold

    for t in range(TILES):
        rows = tile_rows(t)
        lo_planes, lo_fold = arrived(lo_ref, late_lo_ref, t, True)
        hi_planes, hi_fold = arrived(hi_ref, late_hi_ref, t, False)
        folded = (lo_fold * lo_scale, hi_fold * hi_scale)
        for z in outer:
            low = z < EZ // 2
            halo, fold, factor = (lo_planes, folded[0], lo_scale) if low else (hi_planes, folded[1], hi_scale)
            if z < H or z >= H + CZ:
                g = z if low else z - H - CZ
                main = halo(g) * factor
                side = jnp.where(near, roll(fold, -(14 * g + 7), 1), 0.0)
                if z in (H - 1, H + CZ):
                    k = 0 if low else SZ - 1
                    main = main + dm_ref[k, rows] * factor
                    side = side + ds_ref[k, rows] * factor
            else:
                main = dm_ref[z - H + 1, rows] * scale + halo(H) * factor
                side = ds_ref[z - H + 1, rows] * scale + jnp.where(ends, roll(fold, -120, 1), 0.0)
            b_ref[0, place[z], rows] = main
            b_ref[1, place[z], rows] = side
            cm, cs = weights(z)
            phi_ref[0, 0, z, padded_rows(t)] = -main * cm[t]
            phi_ref[0, 1, z, padded_rows(t)] = -side * cs[t]

    def rhs(part, z, rows):
        if z in place:
            return b_ref[part, place[z], rows]
        return (ds_ref if part else dm_ref)[z - H + 1, rows] * scale

    def reader(level):
        known = range(*pre_planes(level))

        def get(part, z, rows):
            if z in known:
                return pre_ref[pre_index(level, z), part, rows]
            return phi_ref[level % 2, part, z, rows]

        return get

    for level in range(1, SWEEPS):
        lo, hi = pre_planes(level)

        def put(part, z, rows, value, level=level):
            phi_ref[level % 2, part, z, rows] = value

        runs = ((level, lo), (hi, EZ - level)) if hi > lo else ((level, EZ - level),)
        for run in runs:
            relax(level, range(*run), reader(level - 1), put, rhs, weights)

    get = reader(SWEEPS - 1)
    chunk = 4
    copies = []
    for c in range(CZ // chunk):
        for z in range(c * chunk, (c + 1) * chunk):
            for t in range(CY // H):
                rows = tile_rows(t)
                at, up, down = padded_rows(t + 1), padded_rows(t + 1, 1), padded_rows(t + 1, -1)
                main, side = get(0, z + H, at), get(1, z + H, at)
                west = jnp.where(first, roll(side, 1, 1), roll(main, 1, 1))
                east = jnp.where(last, roll(side, -1, 1), roll(main, -1, 1))
                half = DT * 0.5
                vel_buf[0, z, rows] = pred_ref[0, z, rows] - half * (east - west)
                vel_buf[1, z, rows] = pred_ref[1, z, rows] - half * (get(0, z + H, up) - get(0, z + H, down))
                vel_buf[2, z, rows] = pred_ref[2, z, rows] - half * (get(0, z + H + 1, at) - get(0, z + H - 1, at))
                pres_buf[z, rows] = pres_ref[z, rows] + main
        part = pl.ds(c * chunk, chunk)
        copies.append(pltpu.make_async_copy(vel_buf.at[:, part], vel_out.at[:, part], sems.at[2 * c]))
        copies.append(pltpu.make_async_copy(pres_buf.at[part], pres_out.at[part], sems.at[2 * c + 1]))
        for copy in copies[-2:]:
            copy.start()
    for copy in copies:
        copy.wait()


def swap(up, down, axis):
    count = lax.axis_size(axis)
    forward = [(i, (i + 1) % count) for i in range(count)]
    backward = [(j, i) for i, j in forward]
    return lax.ppermute(up, axis, forward), lax.ppermute(down, axis, backward)


def shape(*dims):
    return jax.ShapeDtypeStruct(dims, F32)


SMEM = pl.BlockSpec(memory_space=pltpu.SMEM)
VMEM = pl.BlockSpec(memory_space=pltpu.VMEM)


ANY = pl.BlockSpec(memory_space=pl.ANY)


def in_hbm(x):
    return pltpu.with_memory_space_constraint(x, pltpu.HBM)


def in_vmem(*dims, dtype=F32):
    return pltpu.VMEM(dims, dtype)


MIB = 1024 * 1024
ENTRY_LIMIT = 24


class Place:
    def __getitem__(self, k):
        return lax.axis_index(("gx", "gy", "gz")[k])


def call(kernel, scalars, arrays, outs, scratch=(), in_specs=None, out_specs=None, limit=24, cost=0):
    return pl.pallas_call(
        functools.partial(kernel, Place()),
        out_shape=outs,
        in_specs=[SMEM] * len(scalars) + list(in_specs or [VMEM] * len(arrays)),
        out_specs=out_specs or [VMEM] * len(outs),
        scratch_shapes=list(scratch),
        compiler_params=pltpu.CompilerParams(vmem_limit_bytes=limit * MIB),
        cost_estimate=pl.CostEstimate(flops=cost, bytes_accessed=cost // 64, transcendentals=0) if cost else None,
    )(*scalars, *arrays)


def shards(
    velocity, adjoint, pressure, viscosity, disk_cells, disk_turbine, disk_weight, disk_dweight, yaw, thrust_coef, owner_slot,
):
    axes = ("gx", "gy", "gz")
    n_gx, n_gy, n_gz = (lax.axis_size(a) for a in axes)
    n_dev = n_gx * n_gy * n_gz
    dims = (n_dev, n_gx, n_gy, n_gz)
    turbines = owner_slot.shape[0]
    if turbines % CX:
        owner_slot = jnp.pad(owner_slot, (0, CX - turbines % CX))
    owner = owner_slot.reshape(-1, CX)
    cells, turbine, weight = (a.reshape(1, -1) for a in (disk_cells, disk_turbine, disk_weight))

    payload, xr, xl, yr, yl, zr, zl, fields, index, scale, table = call(
        functools.partial(entry_kernel, n_dev, n_gy),
        (in_hbm(yaw), in_hbm(thrust_coef)),
        tuple(in_hbm(a) for a in (velocity, adjoint, viscosity, cells, turbine, weight, disk_dweight, owner)),
        (
            shape(n_dev, CX), in_vmem(2, CY, CX), in_vmem(2, CY, CX), in_vmem(6 * CZ, CX), in_vmem(6 * CZ, CX),
            in_vmem(6, CY, CX), in_vmem(6, CY, CX), in_vmem(7, CZ, CY, CX), in_vmem(2, cells.shape[1], dtype=jnp.int32),
            in_vmem(*weight.shape), in_vmem(*owner.shape, dtype=jnp.int32),
        ),
        (pltpu.VMEM((n_dev, CX), F32), pltpu.SemaphoreType.DMA((8,))),
        [ANY, ANY, ANY] + [VMEM] * 5,
        [ANY] + [VMEM] * 10,
        limit=ENTRY_LIMIT,
    )
    got = lax.all_to_all(payload, axes, 0, 0, tiled=True)
    ylo, yhi = swap(yr, yl, "gy")
    zlo, zhi = swap(zr, zl, "gz")
    count = n_gx
    xlo = lax.ppermute(xr, "gx", [(i, (i + 1) % count) for i in range(count)])
    xlo, xl = lax.optimization_barrier((xlo, xl))
    xhi = lax.ppermute(xl, "gx", [((i + 1) % count, i) for i in range(count)])
    faces = (xlo, xhi, ylo, yhi, zlo, zhi)

    pred_base = call(
        stencil_kernel, (), (fields,), (in_vmem(3, CZ, CY, CX),), cost=1 << 30
    )[0]
    force = call(
        functools.partial(force_kernel, dims), (), (index, scale, table, got), (shape(3, CZ, CY, CX),), cost=1 << 30
    )[0]
    predicted, dm, ds, xr, xl = call(
        functools.partial(flow_kernel, dims),
        (),
        (pred_base, force, fields) + faces,
        (shape(3, CZ, CY, CX), shape(SZ, EY, CX), shape(SZ, EY, CX), shape(3, EY, CX), shape(3, EY, CX)),
        (pltpu.VMEM((CY, CX), F32),),
    )
    lo, hi = swap(xr, xl, "gx")
    yaw_grad, position_grad = call(
        owner_kernel, (in_hbm(yaw), in_hbm(thrust_coef)), (got,), (shape(1, 4), shape(2, 4)), cost=1 << 29
    )
    lo, yaw_grad = lax.optimization_barrier((lo, yaw_grad))
    dm, ds, up, down, above, below = call(
        functools.partial(x_kernel, dims), (), (dm, ds, lo, hi),
        (
            shape(SZ, EY, CX), shape(SZ, EY, CX), shape(27, H, CX), shape(27, H, CX),
            shape(H + 2, CY, CX), shape(H + 2, CY, CX),
        ),
    )
    lo, hi = swap(up, down, "gy")
    early_lo, early_hi = swap(above, below, "gz")
    dm, ds, above, below = call(
        functools.partial(y_kernel, dims), (), (dm, ds, lo, hi),
        (shape(SZ, EY, CX), shape(SZ, EY, CX), shape(LATE, H, CX), shape(LATE, H, CX)),
    )
    late_lo, late_hi = swap(above, below, "gz")
    pre = call(
        functools.partial(inner_kernel, dims), (), (dm, ds), (shape(PRE, 2, EY + 2 * PADR, CX),), cost=1 << 30
    )[0]
    pre, force = lax.optimization_barrier((pre, force))
    adjoint_next = call(
        functools.partial(dual_kernel, dims),
        (),
        (force, fields) + faces,
        (shape(3, CZ, CY, CX),),
        (pltpu.VMEM((3, CZ, CY, CX), F32), pltpu.VMEM((CY, CX), F32), pltpu.SemaphoreType.DMA((3,))),
        out_specs=[ANY],
        cost=1 << 30,
    )[0]
    predicted, adjoint_next = lax.optimization_barrier((predicted, adjoint_next))
    velocity_next, pressure_next = call(
        functools.partial(sweep_kernel, dims), (), (dm, ds, pre, early_lo, early_hi, late_lo, late_hi, predicted, pressure),
        (shape(3, CZ, CY, CX), shape(CZ, CY, CX)),
        (
            pltpu.VMEM((2, EZ - CZ + 2, EY, CX), F32), pltpu.VMEM((2, 2, EZ, EY + 2 * PADR, CX), F32),
            pltpu.VMEM((3, CZ, CY, CX), F32), pltpu.VMEM((CZ, CY, CX), F32), pltpu.SemaphoreType.DMA((8,)),
        ),
        out_specs=[ANY, ANY],
    )
    return velocity_next, adjoint_next, pressure_next, yaw_grad.reshape(-1), position_grad


def solution(mesh):
    axes = ("gx", "gy", "gz")
    grid = P(None, "gz", "gy", "gx")
    cell = P("gz", "gy", "gx")
    flat = P(axes)
    return jax.shard_map(
        shards,
        mesh=mesh,
        in_specs=(grid, grid, cell, cell, flat, flat, flat, P(None, axes), flat, flat, P()),
        out_specs=(grid, grid, cell, flat, P(None, axes)),
        check_vma=False,
    )
```

```python
import functools

import jax
import jax.numpy as jnp
from jax import lax
from jax.experimental import pallas as pl
from jax.experimental.pallas import tpu as pltpu
from jax.sharding import PartitionSpec as P

SWEEPS = 8
DT = 0.2
F32 = jnp.float32
BF16 = jnp.bfloat16
CZ, CY, CX = 16, 32, 128
KJ = CZ * CY
H = 8
EZ, EY = CZ + 2 * H, CY + 2 * H
SZ = CZ + 2
TILES = EY // H
PADR = 8
PER = 16
WIN = 64
YAW = 112
NN = (((1,), (0,)), ((), ()))
NT = (((1,), (1,)), ((), ()))
TN = (((0,), (0,)), ((), ()))


def iota(shape, dim):
    return lax.broadcasted_iota(jnp.int32, shape, dim)


def pieces(x, count):
    parts = []
    for _ in range(count):
        head = x.astype(BF16)
        parts.append(head)
        x = x - head.astype(F32)
    return parts


def dots(left, right, dims):
    total = None
    for a in left:
        for b in right:
            term = lax.dot_general(a, b, dims, preferred_element_type=F32)
            total = term if total is None else total + term
    return total


def onehot(mask):
    return jnp.where(mask, 1.0, 0.0).astype(BF16)


def roll(x, shift, axis):
    return pltpu.roll(x, shift % x.shape[axis], axis)


def entry_onehots(cells):
    row = lax.shift_right_logical(cells, 7)
    lane = jnp.bitwise_and(cells, CX - 1)
    count = cells.shape[1]
    rows = onehot(iota((KJ, count), 0) == row)
    lanes = iota((CX, count), 0) == lane
    return rows, lanes


def window_lane(turbine, bx, n_gy):
    column_x = lax.shift_right_logical(turbine, 4) // n_gy
    return WIN + (column_x - bx + 1) * PER + jnp.bitwise_and(turbine, PER - 1)


def lookup(table_ref, turbine):
    count = turbine.shape[1]
    table = table_ref[...]
    owner = lax.shift_right_logical(table, 2).astype(F32)
    which = jnp.bitwise_and(table, 3).astype(F32)
    rows = table.shape[0]
    high = lax.shift_right_logical(turbine, 7)
    low = onehot(iota((CX, count), 0) == jnp.bitwise_and(turbine, CX - 1))
    keep = iota((rows, count), 0) == high
    out = []
    for part in (owner, which):
        picked = dots([part.astype(BF16)], [low], NN)
        picked = jnp.sum(jnp.where(keep, picked, 0.0), axis=0, keepdims=True)
        out.append(picked.astype(jnp.int32))
    return out


def entry_kernel(
    n_dev, n_gy, pos_ref, yaw_ref, ct_ref, vel_hbm, adj_hbm, visc_hbm, cells_ref, turb_ref, weight_ref, dweight_ref, owner_ref,
    pay_ref, xr_ref, xl_ref, yr_ref, yl_ref, zr_ref, zl_ref, fld_ref, index_ref, scale_ref, table_ref, out_ref, sems,
):
    order = (0, 3, 4, 1, 2, 5, 6)
    copies = {}
    for f in order:
        hbm = vel_hbm.at[f] if f < 3 else adj_hbm.at[f - 3] if f < 6 else visc_hbm
        copies[f] = pltpu.make_async_copy(hbm, fld_ref.at[f], sems.at[f])
        copies[f].start()
    bx = pos_ref[0]
    cells, turbine, weight = cells_ref[...], turb_ref[...], weight_ref[...]
    index_ref[0:1, :] = cells
    index_ref[1:2, :] = turbine
    scale_ref[...] = weight
    table_ref[...] = owner_ref[...]
    count = cells.shape[1]
    rows, lanes = entry_onehots(cells)
    owner, which = lookup(owner_ref, turbine)
    to_owner = onehot(iota((n_dev, count), 0) == owner)
    in_window = onehot(iota((CX, count), 0) == window_lane(turbine, bx, n_gy))

    columns = []
    for f in order[:3]:
        copies[f].wait()
        columns += pieces(fld_ref[f].reshape(KJ, CX), 2)
    at_row = dots([jnp.concatenate(columns, axis=1)], [rows], TN)
    gathered = []
    for k in range(3):
        both = at_row[2 * k * CX:(2 * k + 1) * CX] + at_row[(2 * k + 1) * CX:(2 * k + 2) * CX]
        gathered.append(jnp.sum(jnp.where(lanes, both, 0.0), axis=0, keepdims=True))
    factors = [weight, dweight_ref[0:1, :], dweight_ref[1:2, :]]
    values = [f * g for f in factors for g in gathered]

    sub = iota((PER, count), 0)
    stacked = jnp.zeros((PER, count), F32)
    for v, value in enumerate(values):
        stacked = jnp.where(sub == v, value, stacked)
    per_slot = jnp.concatenate(
        [jnp.where(which == i, stacked, 0.0) for i in range(4)] + [jnp.zeros((CX - 4 * PER, count), F32)], axis=0
    )
    payload = dots([to_owner], pieces(per_slot, 2), NT)

    speed = jnp.broadcast_to(values[0], (8, count))
    shared = dots(pieces(speed, 2), [in_window], NT)[0:1, :]
    lane = iota((1, CX), 1)
    for i in range(4):
        shared = jnp.where(lane == YAW + i, yaw_ref[i], shared)
        shared = jnp.where(lane == YAW + 4 + i, ct_ref[i], shared)
    out_ref[...] = payload + shared
    leaving = pltpu.make_async_copy(out_ref, pay_ref, sems.at[7])
    leaving.start()

    for f in order[3:]:
        copies[f].wait()
    lane = iota((H, CX), 1)
    for t in range(CY // H):
        at = slice(H * t, H * t + H)
        for half in range(2):
            right = jnp.zeros((H, CX), F32)
            left = jnp.zeros((H, CX), F32)
            for f in range(3):
                for z in range(CZ):
                    spot = 2 * (f * CZ + z) + 1
                    moved = roll(fld_ref[3 * half + f, z, at], spot + 1, 1)
                    right = jnp.where(lane == spot, moved, right)
                    left = jnp.where(lane == spot + 1, moved, left)
            xr_ref[half, at] = right
            xl_ref[half, at] = left
    for f in range(6):
        yr_ref[f * CZ:(f + 1) * CZ, :] = fld_ref[f, :, CY - 1, :]
        yl_ref[f * CZ:(f + 1) * CZ, :] = fld_ref[f, :, 0, :]
        zr_ref[f] = fld_ref[f, CZ - 1]
        zl_ref[f] = fld_ref[f, 0]
    leaving.wait()


def turbine_terms(speed, yaw, thrust_coef):
    cosine = jnp.cos(yaw)
    sine = jnp.sin(yaw)
    magnitude = jnp.abs(speed)
    force = 0.5 * thrust_coef * speed * magnitude * cosine * cosine
    weighting = 1.5 * thrust_coef * speed * magnitude * cosine * cosine * cosine
    return cosine, sine, magnitude, force, weighting


def owner_outputs(got, yaw_ref, ct_ref, yaw_out, pos_out):
    total = jnp.sum(got, axis=0, keepdims=True)
    total = jnp.broadcast_to(total, (8, CX))
    lane = iota((8, CX), 1)
    yaw = jnp.zeros((8, CX), F32)
    ct = jnp.zeros((8, CX), F32)
    for i in range(4):
        yaw = jnp.where(lane == i * PER, yaw_ref[i], yaw)
        ct = jnp.where(lane == i * PER, ct_ref[i], ct)

    def at(v):
        return roll(total, -v, 1)

    speed, dual_x, dual_y = total, at(1), at(2)
    cosine, sine, magnitude, force, weighting = turbine_terms(speed, yaw, ct)
    yaw_grad = -1.5 * ct * magnitude * magnitude * magnitude * cosine * cosine * sine + force * (
        sine * dual_x - cosine * dual_y
    )
    grads = [yaw_grad]
    for r in range(2):
        grads.append(weighting * at(3 + 3 * r) - force * cosine * at(4 + 3 * r) - force * sine * at(5 + 3 * r))
    packed = []
    for grad in grads:
        out = jnp.zeros((8, CX), F32)
        for i in range(4):
            out = jnp.where(lane == i, roll(grad, -(PER - 1) * i, 1), out)
        packed.append(out)
    yaw_out[...] = packed[0][0:1, 0:4]
    pos_out[0:1, :] = packed[1][0:1, 0:4]
    pos_out[1:2, :] = packed[2][0:1, 0:4]


def window_terms(got, n_dev, n_gx, n_gy, n_gz, bx, by, owner_ref):
    lane = iota((1, CX), 1)
    inside = jnp.logical_and(lane >= WIN, lane < WIN + 3 * PER)
    row = iota((n_dev, CX), 0)
    speed = jnp.zeros((1, CX), F32)
    for delta in range(-2, 3):
        base = ((bx + delta) * n_gy + by) * n_gz
        keep = jnp.logical_and(row >= base, row < base + n_gz)
        part = jnp.sum(jnp.where(keep, got, 0.0), axis=0, keepdims=True)
        part = jnp.broadcast_to(jnp.where(inside, part, 0.0), (8, CX))
        speed = speed + roll(part, delta * PER, 1)[0:1, :]
    speed = jnp.where(inside, speed, 0.0)

    table = owner_ref[...]
    sub = iota(table.shape, 0)
    slots = jnp.zeros((1, CX), jnp.int32)
    for j in range(3):
        column_x = jnp.clip(bx - 1 + j, 0, n_gx - 1)
        first = (column_x * n_gy + by) * PER
        picked = jnp.sum(jnp.where(sub == first // CX, table, 0), axis=0, keepdims=True)
        picked = jnp.broadcast_to(picked, (8, CX))
        moved = pltpu.roll(picked, jnp.bitwise_and(WIN + PER * j - first, CX - 1), 1)[0:1, :]
        here = jnp.logical_and(lane >= WIN + PER * j, lane < WIN + PER * (j + 1))
        slots = jnp.where(here, moved, slots)
    owner = onehot(iota((n_dev, CX), 0) == lax.shift_right_logical(slots, 2))
    which = jnp.bitwise_and(slots, 3)
    found = dots(pieces(got, 3), [owner], TN)
    yaw = jnp.zeros((1, CX), F32)
    ct = jnp.zeros((1, CX), F32)
    for i in range(4):
        yaw = jnp.where(which == i, found[YAW + i:YAW + i + 1, :], yaw)
        ct = jnp.where(which == i, found[YAW + 4 + i:YAW + 5 + i, :], ct)
    cosine, sine, magnitude, force, weighting = turbine_terms(speed, yaw, ct)
    keep = lambda x: jnp.where(inside, x, 0.0)
    return keep(force * cosine), keep(force * sine), keep(weighting)


def edges(pos_ref, dims):
    n_dev, n_gx, n_gy, n_gz = dims
    out = []
    for k, count in enumerate((n_gx, n_gy, n_gz)):
        out.append(jnp.where(pos_ref[k] > 0, 1.0, 0.0))
        out.append(jnp.where(pos_ref[k] < count - 1, 1.0, 0.0))
    return out


def tile_rows(t):
    return slice(H * t, H * t + H)


def south_of(ref, index, t, sub):
    if t > 0:
        return ref[index + (slice(H * t - 1, H * t + H - 1),)]
    return jnp.where(sub == 0, 0.0, roll(ref[index + (tile_rows(0),)], 1, 0))


def north_of(ref, index, t, sub):
    if t < CY // H - 1:
        return ref[index + (slice(H * t + 1, H * t + H + 1),)]
    return jnp.where(sub == H - 1, 0.0, roll(ref[index + (tile_rows(t),)], -1, 0))


def force_kernel(dims, pos_ref, index_ref, scale_ref, owner_ref, got_ref, field_ref):
    n_dev, n_gx, n_gy, n_gz = dims
    bx, by = pos_ref[0], pos_ref[1]
    terms = window_terms(got_ref[...], n_dev, n_gx, n_gy, n_gz, bx, by, owner_ref)
    cells, turbine, weight = index_ref[0:1, :], index_ref[1:2, :], scale_ref[...]
    count = cells.shape[1]
    rows, lanes = entry_onehots(cells)
    in_window = onehot(iota((CX, count), 0) == window_lane(turbine, bx, n_gy))
    stacked = jnp.concatenate([jnp.broadcast_to(t, (8, CX)) for t in terms], axis=0)
    per_entry = dots(pieces(stacked, 2), [in_window], NN)
    for c in range(3):
        value = per_entry[8 * c:8 * c + 1, :] * weight
        if c < 2:
            value = -value
        spread = jnp.where(lanes, value, 0.0)
        field_ref[c] = dots([rows], pieces(spread, 2), NT).reshape(CZ, CY, CX)


def stencil(fld_ref, f, out, comp):
    lane = iota((H, CX), 1)
    sub = iota((H, CX), 0)
    zero = jnp.zeros((H, CX), F32)
    for t in range(CY // H):
        at = tile_rows(t)
        below, tile = zero, fld_ref[f, 0, at]
        for z in range(CZ):
            above = fld_ref[f, z + 1, at] if z < CZ - 1 else zero
            south, north = south_of(fld_ref, (f, z), t, sub), north_of(fld_ref, (f, z), t, sub)
            west = jnp.where(lane == 0, 0.0, roll(tile, 1, 1))
            east = jnp.where(lane == CX - 1, 0.0, roll(tile, -1, 1))
            lap = (above + below) + (north + south) + (east + west) - 6.0 * tile
            rate = fld_ref[6, z, at] * lap + (west - tile if f < 3 else east - tile)
            out[comp, z, at] = tile + DT * rate
            below, tile = tile, above


def stencil_kernel(pos_ref, fld_ref, pred_ref):
    for f in range(3):
        stencil(fld_ref, f, pred_ref, f)


def merge_faces(face_ref, half, xlo_ref, xhi_ref, bounds):
    odd = jnp.bitwise_and(iota((H, CX), 1), 1) == 1
    for t in range(CY // H):
        at = tile_rows(t)
        face_ref[at] = jnp.where(odd, xlo_ref[half, at] * bounds[0], roll(xhi_ref[half, at] * bounds[1], -2, 1))


def add_faces(f, first, out, given, field_ref, fld_ref, bounds, face_ref, ylo_ref, yhi_ref, zlo_ref, zhi_ref):
    lo_x, hi_x, lo_y, hi_y, lo_z, hi_z = bounds
    lane = iota((H, CX), 1)
    sub = iota((H, CX), 0)
    flow = f < 3
    comp = f - first
    for t in range(CY // H):
        at = tile_rows(t)
        for z in range(CZ):
            spot = f * CZ + z
            moved = roll(face_ref[at], -(2 * (spot % (3 * CZ)) + 1), 1)
            west = jnp.where(lane == 0, moved, 0.0)
            east = jnp.where(lane == CX - 1, moved, 0.0)
            lap = west + east
            if t == 0:
                lap = lap + jnp.where(sub == 0, ylo_ref[spot:spot + 1, :] * lo_y, 0.0)
            if t == CY // H - 1:
                lap = lap + jnp.where(sub == H - 1, yhi_ref[spot:spot + 1, :] * hi_y, 0.0)
            if z == 0:
                lap = lap + zlo_ref[f, at] * lo_z
            if z == CZ - 1:
                lap = lap + zhi_ref[f, at] * hi_z
            rate = fld_ref[6, z, at] * lap + (west if flow else east)
            if f < 2:
                rate = rate + field_ref[f, z, at]
            if f == 3:
                rate = rate + field_ref[2, z, at]
            out[comp, z, at] = given[comp, z, at] + DT * rate


def fold_shift(z):
    return H + 16 * (z % 8)


def flow_kernel(
    dims, pos_ref, base_ref, field_ref, fld_ref, xlo_ref, xhi_ref, ylo_ref, yhi_ref, zlo_ref, zhi_ref,
    pred_ref, dm_ref, ds_ref, xr_ref, xl_ref, face_ref,
):
    bounds = edges(pos_ref, dims)
    merge_faces(face_ref, 0, xlo_ref, xhi_ref, bounds)
    for f in range(3):
        add_faces(f, 0, pred_ref, base_ref, field_ref, fld_ref, bounds, face_ref, ylo_ref, yhi_ref, zlo_ref, zhi_ref)
    lane = iota((H, CX), 1)
    sub = iota((H, CX), 0)
    zero = jnp.zeros((H, CX), F32)
    for r in range(EY // H):
        at = tile_rows(r)
        t = r - 1
        inside = 0 <= t < CY // H
        for k in range(SZ):
            z = k - 1
            main, side = zero, zero
            if inside and 0 <= z < CZ:
                own = tile_rows(t)
                p0 = pred_ref[0, z, own]
                west, east = roll(p0, 1, 1), roll(p0, -1, 1)
                div = jnp.where(lane == CX - 1, 0.0, east) - jnp.where(lane == 0, 0.0, west)
                div = div + (north_of(pred_ref, (1, z), t, sub) - south_of(pred_ref, (1, z), t, sub))
                if z < CZ - 1:
                    div = div + pred_ref[2, z + 1, own]
                if z > 0:
                    div = div - pred_ref[2, z - 1, own]
                main = 0.5 * div
                side = jnp.where(lane == CX - 1, 0.5 * east, jnp.where(lane == 0, -0.5 * west, 0.0))
            elif inside:
                main = 0.5 * pred_ref[2, 0, tile_rows(t)] if z < 0 else -0.5 * pred_ref[2, CZ - 1, tile_rows(t)]
            elif 0 <= z < CZ and t < 0:
                main = jnp.where(sub == H - 1, 0.5 * roll(pred_ref[1, z, 0:H], -1, 0), 0.0)
            elif 0 <= z < CZ:
                main = jnp.where(sub == 0, -0.5 * roll(pred_ref[1, z, CY - H:CY], 1, 0), 0.0)
            dm_ref[k, at] = main
            ds_ref[k, at] = side
    for r in range(EY // H):
        at = tile_rows(r)
        right, left = [zero] * 3, [zero] * 3
        for k in range(SZ):
            if not 0 < r < EY // H - 1 and not 0 < k < SZ - 1:
                continue
            main, side = dm_ref[k, at], ds_ref[k, at]
            g = k % 8
            mine = jnp.logical_and(lane >= 16 * g, lane < 16 * g + 16)
            right[k // 8] = jnp.where(mine, roll(jnp.where(lane < H, side, main), fold_shift(k), 1), right[k // 8])
            left[k // 8] = jnp.where(mine, roll(jnp.where(lane < H, main, side), fold_shift(k), 1), left[k // 8])
        for i in range(3):
            xr_ref[i, at] = right[i]
            xl_ref[i, at] = left[i]


def dual_kernel(
    dims, pos_ref, field_ref, fld_ref, xlo_ref, xhi_ref, ylo_ref, yhi_ref, zlo_ref, zhi_ref,
    dual_out, dual_ref, face_ref, sems,
):
    bounds = edges(pos_ref, dims)
    merge_faces(face_ref, 1, xlo_ref, xhi_ref, bounds)
    copies = []
    for f in range(3, 6):
        stencil(fld_ref, f, dual_ref, f - 3)
        add_faces(f, 3, dual_ref, dual_ref, field_ref, fld_ref, bounds, face_ref, ylo_ref, yhi_ref, zlo_ref, zhi_ref)
        copies.append(pltpu.make_async_copy(dual_ref.at[f - 3], dual_out.at[f - 3], sems.at[f - 3]))
        copies[-1].start()
    for copy in copies:
        copy.wait()


def owner_kernel(pos_ref, yaw_ref, ct_ref, got_ref, yaw_out, pos_out):
    owner_outputs(got_ref[...], yaw_ref, ct_ref, yaw_out, pos_out)


def x_kernel(
    dims, pos_ref, dm_ref, ds_ref, lo_ref, hi_ref, om_ref, os_ref, up_ref, down_ref, above_ref, below_ref
):
    in_lo, in_hi = edges(pos_ref, dims)[0:2]
    lane = iota((H, CX), 1)
    head, tail = lane < H, lane >= CX - H
    zero = jnp.zeros((H, CX), F32)
    for r in range(EY // H):
        at = tile_rows(r)
        lows = [lo_ref[i, at] * in_lo for i in range(3)]
        highs = [hi_ref[i, at] * in_hi for i in range(3)]
        for z in range(SZ):
            lo = roll(lows[z // 8], -fold_shift(z), 1)
            hi = roll(highs[z // 8], -fold_shift(z), 1)
            om_ref[z, at] = dm_ref[z, at] + jnp.where(head, lo, jnp.where(tail, hi, 0.0))
            os_ref[z, at] = ds_ref[z, at] + jnp.where(tail, lo, jnp.where(head, hi, 0.0))
    for out, row, edge in ((up_ref, CY, H + CY), (down_ref, H, H - 1)):
        for i in range(3):
            fold = zero
            out[18 + i] = zero
            out[24 + i] = zero
            for g in range(min(8, SZ - 8 * i)):
                z = 8 * i + g
                out[z] = om_ref[z, row:row + H]
                mine = jnp.logical_and(lane >= 16 * g, lane < 16 * g + 16)
                fold = jnp.where(mine, roll(os_ref[z, row:row + H], fold_shift(z), 1), fold)
                out[18 + i, g:g + 1] = om_ref[z, edge:edge + 1]
                out[24 + i, g:g + 1] = os_ref[z, edge:edge + 1]
            out[21 + i] = fold
    for out, plane in ((above_ref, up_plane), (below_ref, down_plane)):
        for r in range(1, 1 + CY // H):
            for i in range(H + 1):
                out[i, tile_rows(r - 1)] = om_ref[plane(i), tile_rows(r)]
            out[H + 1, tile_rows(r - 1)] = fold_planes(lambda i: os_ref[plane(i), tile_rows(r)])


def up_plane(i):
    return CZ - H + 1 + i


def down_plane(i):
    return i + 1 if i < H else 0


def fold_planes(side):
    lane = iota((H, CX), 1)
    fold = jnp.zeros((H, CX), F32)
    for i in range(H + 1):
        mine = jnp.logical_and(lane >= 14 * i, lane < (14 * i + 14 if i < H else CX))
        fold = jnp.where(mine, roll(side(i), 14 * i + 7 if i < H else 120, 1), fold)
    return fold


LATE = H + 1 + 2 + 3


def y_kernel(dims, pos_ref, dm_ref, ds_ref, lo_ref, hi_ref, om_ref, os_ref, above_ref, below_ref):
    in_lo, in_hi = edges(pos_ref, dims)[2:4]
    lane = iota((H, CX), 1)
    sub = iota((H, CX), 0)
    ends = jnp.logical_or(lane < H, lane >= CX - H)
    last = EY // H - 1
    for r in range(EY // H):
        at = tile_rows(r)
        for z in range(SZ):
            tile, g = z // 8, z % 8
            main, side = dm_ref[z, at], ds_ref[z, at]
            if r == 0:
                main = main + lo_ref[z] * in_lo
                side = side + jnp.where(ends, roll(lo_ref[21 + tile], -fold_shift(z), 1) * in_lo, 0.0)
            if r == 1:
                main = main + jnp.where(sub == 0, lo_ref[18 + tile, g:g + 1, :] * in_lo, 0.0)
                side = side + jnp.where(sub == 0, lo_ref[24 + tile, g:g + 1, :] * in_lo, 0.0)
            if r == last - 1:
                main = main + jnp.where(sub == H - 1, hi_ref[18 + tile, g:g + 1, :] * in_hi, 0.0)
                side = side + jnp.where(sub == H - 1, hi_ref[24 + tile, g:g + 1, :] * in_hi, 0.0)
            if r == last:
                main = main + hi_ref[z] * in_hi
                side = side + jnp.where(ends, roll(hi_ref[21 + tile], -fold_shift(z), 1) * in_hi, 0.0)
            om_ref[z, at] = main
            os_ref[z, at] = side
    lower, upper = tile_rows(0), tile_rows(last)
    for out, plane, depth in (
        (above_ref, up_plane, lambda i: H - i),
        (below_ref, down_plane, lambda i: i + 1),
    ):
        at_depth = {depth(i): plane(i) for i in range(H)}
        for d in range(1, H):
            out[d - 1] = jnp.where(sub >= d, om_ref[at_depth[d], lower], om_ref[at_depth[H - d], upper])
        out[H - 1] = om_ref[plane(H), lower]
        out[H] = om_ref[plane(H), upper]
        out[H + 1] = fold_planes(lambda i: os_ref[plane(i), lower])
        out[H + 2] = fold_planes(lambda i: os_ref[plane(i), upper])
        out[H + 5] = jnp.zeros((H, CX), F32)
        for given, factor, k in ((lo_ref, in_lo, 0), (hi_ref, in_hi, 1)):
            for i in range(H + 1):
                tile, g = plane(i) // 8, plane(i) % 8
                row = given[18 + tile, g:g + 1, :] * factor
                if i < H:
                    out[H + 3 + k, i:i + 1] = row
                else:
                    out[H + 5, k:k + 1] = row
            side = fold_planes(lambda i: jnp.broadcast_to(given[24 + plane(i) // 8, plane(i) % 8:plane(i) % 8 + 1, :], (H, CX)))
            out[H + 5, 2 + k:3 + k] = side[0:1] * factor


def pre_planes(level):
    return (H + 1 + level, H + CZ - 1 - level) if level < SWEEPS - 1 else (0, 0)


def pre_index(level, z):
    return sum(CZ - 2 - 2 * i for i in range(level)) + z - pre_planes(level)[0]


PRE = sum(CZ - 2 - 2 * i for i in range(SWEEPS - 1))


def padded_rows(t, shift=0):
    return slice(PADR + H * t + shift, PADR + H * t + H + shift)


def coefficients(pos_ref, dims):
    lo_x, hi_x, lo_y, hi_y, lo_z, hi_z = edges(pos_ref, dims)
    lane = iota((H, CX), 1)
    low, high = jnp.where(lane >= CX - H, lo_x, 1.0), jnp.where(lane < H, hi_x, 1.0)
    main = [jnp.full((H, CX), 1.0 / 6.0, F32)] * TILES
    main[0] = main[0] * lo_y
    main[-1] = main[-1] * hi_y
    return main, [c * (low * high) for c in main]


def reached(level, z, t, part):
    depth = max(0, H - z, z - H - CZ + 1)
    return depth + (t in (0, TILES - 1)) + part <= SWEEPS - level


def relax(level, planes, get, put, rhs, weights):
    lane = iota((H, CX), 1)
    first, last = lane == 0, lane == CX - 1
    z0 = planes[0]
    carry = [[get(k, z0 - 1 + i, padded_rows(t)) for k in range(2) for i in range(2)] for t in range(TILES)]
    for z in planes:
        main_weight, side_weight = weights(z)
        for t in range(TILES):
            below, main, side_below, side = carry[t]
            at, up, down = padded_rows(t), padded_rows(t, 1), padded_rows(t, -1)
            above, side_above = get(0, z + 1, at), get(1, z + 1, at)
            main_w, side_w = roll(main, 1, 1), roll(side, 1, 1)
            main_e, side_e = roll(main, -1, 1), roll(side, -1, 1)
            if reached(level, z, t, 0):
                total = (above + below) + (get(0, z, up) + get(0, z, down))
                total = total + (jnp.where(first, side_w, main_w) + jnp.where(last, side_e, main_e))
                put(0, z, at, (total - rhs(0, z, tile_rows(t))) * main_weight[t])
            if reached(level, z, t, 1):
                total = (side_above + side_below) + (get(1, z, up) + get(1, z, down))
                total = total + (jnp.where(first, main_w, side_w) + jnp.where(last, main_e, side_e))
                put(1, z, at, (total - rhs(1, z, tile_rows(t))) * side_weight[t])
            carry[t] = [main, above, side, side_above]


def inner_kernel(dims, pos_ref, dm_ref, ds_ref, pre_ref):
    main_coef, side_coef = coefficients(pos_ref, dims)
    scale = 1.0 / DT
    zero = jnp.zeros((H, CX), F32)
    for i in range(PRE):
        for part in range(2):
            pre_ref[i, part, 0:PADR] = zero
            pre_ref[i, part, PADR + EY:PADR + EY + PADR] = zero

    def rhs(part, z, rows):
        return (ds_ref if part else dm_ref)[z - H + 1, rows] * scale

    for z in range(*pre_planes(0)):
        for t in range(TILES):
            pre_ref[pre_index(0, z), 0, padded_rows(t)] = -rhs(0, z, tile_rows(t)) * main_coef[t]
            pre_ref[pre_index(0, z), 1, padded_rows(t)] = -rhs(1, z, tile_rows(t)) * side_coef[t]
    for level in range(1, SWEEPS - 1):
        def get(part, z, rows, level=level):
            return pre_ref[pre_index(level - 1, z), part, rows]

        def put(part, z, rows, value, level=level):
            pre_ref[pre_index(level, z), part, rows] = value

        relax(level, range(*pre_planes(level)), get, put, rhs, lambda z: (main_coef, side_coef))


def sweep_kernel(
    dims, pos_ref, dm_ref, ds_ref, pre_ref, lo_ref, hi_ref, late_lo_ref, late_hi_ref, pred_ref, pres_ref, vel_out, pres_out,
    b_ref, phi_ref, vel_buf, pres_buf, sems,
):
    lo_z, hi_z = edges(pos_ref, dims)[4:6]
    main_coef, side_coef = coefficients(pos_ref, dims)
    scale = 1.0 / DT
    lane = iota((H, CX), 1)
    first, last = lane == 0, lane == CX - 1
    zero = jnp.zeros((H, CX), F32)
    near = jnp.logical_or(lane < H - 1, lane >= CX - H + 1)
    ends = jnp.logical_or(lane < H, lane >= CX - H)
    lo_scale, hi_scale = lo_z * scale, hi_z * scale
    low_coef = [[c * lo_z for c in main_coef], [c * lo_z for c in side_coef]]
    high_coef = [[c * hi_z for c in main_coef], [c * hi_z for c in side_coef]]

    def weights(z):
        return low_coef if z < H else high_coef if z >= H + CZ else (main_coef, side_coef)

    outer = list(range(pre_planes(0)[0])) + list(range(pre_planes(0)[1], EZ))
    place = {z: i for i, z in enumerate(outer)}

    for z in range(EZ):
        for part in range(2):
            for buf in range(2):
                phi_ref[buf, part, z, 0:PADR] = zero
                phi_ref[buf, part, z, PADR + EY:PADR + EY + PADR] = zero
    sub = iota((H, CX), 0)

    def arrived(early, late, t, low):
        def planes(i):
            depth = H - i if low else i + 1
            if t in (0, TILES - 1):
                if i == H:
                    return late[H - 1 if t == 0 else H]
                depth = depth if t == 0 else H - depth
                return late[depth - 1] if 0 < depth < H else zero
            value = early[i, tile_rows(t - 1)]
            for k, edge, row in ((0, 1, 0), (1, TILES - 2, H - 1)):
                if t == edge:
                    fix = late[H + 3 + k, i:i + 1] if i < H else late[H + 5, k:k + 1]
                    value = value + jnp.where(sub == row, fix, 0.0)
            return value

        if t in (0, TILES - 1):
            fold = late[H + 1 if t == 0 else H + 2]
        else:
            fold = early[H + 1, tile_rows(t - 1)]
            for k, edge, row in ((0, 1, 0), (1, TILES - 2, H - 1)):
                if t == edge:
                    fold = fold + jnp.where(sub == row, late[H + 5, 2 + k:3 + k], 0.0)
        return planes, fold

    for t in range(TILES):
        rows = tile_rows(t)
        lo_planes, lo_fold = arrived(lo_ref, late_lo_ref, t, True)
        hi_planes, hi_fold = arrived(hi_ref, late_hi_ref, t, False)
        folded = (lo_fold * lo_scale, hi_fold * hi_scale)
        for z in outer:
            low = z < EZ // 2
            halo, fold, factor = (lo_planes, folded[0], lo_scale) if low else (hi_planes, folded[1], hi_scale)
            if z < H or z >= H + CZ:
                g = z if low else z - H - CZ
                main = halo(g) * factor
                side = jnp.where(near, roll(fold, -(14 * g + 7), 1), 0.0)
                if z in (H - 1, H + CZ):
                    k = 0 if low else SZ - 1
                    main = main + dm_ref[k, rows] * factor
                    side = side + ds_ref[k, rows] * factor
            else:
                main = dm_ref[z - H + 1, rows] * scale + halo(H) * factor
                side = ds_ref[z - H + 1, rows] * scale + jnp.where(ends, roll(fold, -120, 1), 0.0)
            b_ref[0, place[z], rows] = main
            b_ref[1, place[z], rows] = side
            cm, cs = weights(z)
            phi_ref[0, 0, z, padded_rows(t)] = -main * cm[t]
            phi_ref[0, 1, z, padded_rows(t)] = -side * cs[t]

    def rhs(part, z, rows):
        if z in place:
            return b_ref[part, place[z], rows]
        return (ds_ref if part else dm_ref)[z - H + 1, rows] * scale

    def reader(level):
        known = range(*pre_planes(level))

        def get(part, z, rows):
            if z in known:
                return pre_ref[pre_index(level, z), part, rows]
            return phi_ref[level % 2, part, z, rows]

        return get

    for level in range(1, SWEEPS - 1):
        lo, hi = pre_planes(level)

        def put(part, z, rows, value, level=level):
            phi_ref[level % 2, part, z, rows] = value

        for run in ((level, lo), (hi, EZ - level)):
            relax(level, range(*run), reader(level - 1), put, rhs, weights)

    def put_last(part, z, rows, value):
        phi_ref[(SWEEPS - 1) % 2, part, z, rows] = value

    get = reader(SWEEPS - 1)
    chunk = 4
    copies = []
    for c in range(CZ // chunk):
        begin = H - 1 if c == 0 else H + 1 + c * chunk
        relax(
            SWEEPS - 1, range(begin, H + 1 + (c + 1) * chunk), reader(SWEEPS - 2), put_last, rhs, weights
        )
        for z in range(c * chunk, (c + 1) * chunk):
            for t in range(CY // H):
                rows = tile_rows(t)
                at, up, down = padded_rows(t + 1), padded_rows(t + 1, 1), padded_rows(t + 1, -1)
                main, side = get(0, z + H, at), get(1, z + H, at)
                west = jnp.where(first, roll(side, 1, 1), roll(main, 1, 1))
                east = jnp.where(last, roll(side, -1, 1), roll(main, -1, 1))
                half = DT * 0.5
                vel_buf[0, z, rows] = pred_ref[0, z, rows] - half * (east - west)
                vel_buf[1, z, rows] = pred_ref[1, z, rows] - half * (get(0, z + H, up) - get(0, z + H, down))
                vel_buf[2, z, rows] = pred_ref[2, z, rows] - half * (get(0, z + H + 1, at) - get(0, z + H - 1, at))
                pres_buf[z, rows] = pres_ref[z, rows] + main
        part = pl.ds(c * chunk, chunk)
        copies.append(pltpu.make_async_copy(vel_buf.at[:, part], vel_out.at[:, part], sems.at[2 * c]))
        copies.append(pltpu.make_async_copy(pres_buf.at[part], pres_out.at[part], sems.at[2 * c + 1]))
        for copy in copies[-2:]:
            copy.start()
    for copy in copies:
        copy.wait()


def swap(up, down, axis):
    count = lax.axis_size(axis)
    forward = [(i, (i + 1) % count) for i in range(count)]
    backward = [(j, i) for i, j in forward]
    return lax.ppermute(up, axis, forward), lax.ppermute(down, axis, backward)


def shape(*dims):
    return jax.ShapeDtypeStruct(dims, F32)


SMEM = pl.BlockSpec(memory_space=pltpu.SMEM)
VMEM = pl.BlockSpec(memory_space=pltpu.VMEM)


ANY = pl.BlockSpec(memory_space=pl.ANY)


def in_hbm(x):
    return pltpu.with_memory_space_constraint(x, pltpu.HBM)


def in_vmem(*dims, dtype=F32):
    return pltpu.VMEM(dims, dtype)


MIB = 1024 * 1024
ENTRY_LIMIT = 24


class Place:
    def __getitem__(self, k):
        return lax.axis_index(("gx", "gy", "gz")[k])


def call(kernel, scalars, arrays, outs, scratch=(), in_specs=None, out_specs=None, limit=24, cost=0):
    return pl.pallas_call(
        functools.partial(kernel, Place()),
        out_shape=outs,
        in_specs=[SMEM] * len(scalars) + list(in_specs or [VMEM] * len(arrays)),
        out_specs=out_specs or [VMEM] * len(outs),
        scratch_shapes=list(scratch),
        compiler_params=pltpu.CompilerParams(vmem_limit_bytes=limit * MIB),
        cost_estimate=pl.CostEstimate(flops=cost, bytes_accessed=cost // 64, transcendentals=0) if cost else None,
    )(*scalars, *arrays)


def shards(
    velocity, adjoint, pressure, viscosity, disk_cells, disk_turbine, disk_weight, disk_dweight, yaw, thrust_coef, owner_slot,
):
    axes = ("gx", "gy", "gz")
    n_gx, n_gy, n_gz = (lax.axis_size(a) for a in axes)
    n_dev = n_gx * n_gy * n_gz
    dims = (n_dev, n_gx, n_gy, n_gz)
    turbines = owner_slot.shape[0]
    if turbines % CX:
        owner_slot = jnp.pad(owner_slot, (0, CX - turbines % CX))
    owner = owner_slot.reshape(-1, CX)
    cells, turbine, weight = (a.reshape(1, -1) for a in (disk_cells, disk_turbine, disk_weight))

    payload, xr, xl, yr, yl, zr, zl, fields, index, scale, table = call(
        functools.partial(entry_kernel, n_dev, n_gy),
        (in_hbm(yaw), in_hbm(thrust_coef)),
        tuple(in_hbm(a) for a in (velocity, adjoint, viscosity, cells, turbine, weight, disk_dweight, owner)),
        (
            shape(n_dev, CX), in_vmem(2, CY, CX), in_vmem(2, CY, CX), in_vmem(6 * CZ, CX), in_vmem(6 * CZ, CX),
            in_vmem(6, CY, CX), in_vmem(6, CY, CX), in_vmem(7, CZ, CY, CX), in_vmem(2, cells.shape[1], dtype=jnp.int32),
            in_vmem(*weight.shape), in_vmem(*owner.shape, dtype=jnp.int32),
        ),
        (pltpu.VMEM((n_dev, CX), F32), pltpu.SemaphoreType.DMA((8,))),
        [ANY, ANY, ANY] + [VMEM] * 5,
        [ANY] + [VMEM] * 10,
        limit=ENTRY_LIMIT,
    )
    got = lax.all_to_all(payload, axes, 0, 0, tiled=True)
    ylo, yhi = swap(yr, yl, "gy")
    zlo, zhi = swap(zr, zl, "gz")
    count = n_gx
    xlo = lax.ppermute(xr, "gx", [(i, (i + 1) % count) for i in range(count)])
    xlo, xl = lax.optimization_barrier((xlo, xl))
    xhi = lax.ppermute(xl, "gx", [((i + 1) % count, i) for i in range(count)])
    faces = (xlo, xhi, ylo, yhi, zlo, zhi)

    pred_base = call(
        stencil_kernel, (), (fields,), (in_vmem(3, CZ, CY, CX),), cost=1 << 30
    )[0]
    force = call(
        functools.partial(force_kernel, dims), (), (index, scale, table, got), (shape(3, CZ, CY, CX),), cost=1 << 30
    )[0]
    predicted, dm, ds, xr, xl = call(
        functools.partial(flow_kernel, dims),
        (),
        (pred_base, force, fields) + faces,
        (shape(3, CZ, CY, CX), shape(SZ, EY, CX), shape(SZ, EY, CX), shape(3, EY, CX), shape(3, EY, CX)),
        (pltpu.VMEM((CY, CX), F32),),
    )
    lo, hi = swap(xr, xl, "gx")
    yaw_grad, position_grad = call(
        owner_kernel, (in_hbm(yaw), in_hbm(thrust_coef)), (got,), (shape(1, 4), shape(2, 4)), cost=1 << 29
    )
    lo, yaw_grad = lax.optimization_barrier((lo, yaw_grad))
    dm, ds, up, down, above, below = call(
        functools.partial(x_kernel, dims), (), (dm, ds, lo, hi),
        (
            shape(SZ, EY, CX), shape(SZ, EY, CX), shape(27, H, CX), shape(27, H, CX),
            shape(H + 2, CY, CX), shape(H + 2, CY, CX),
        ),
    )
    lo, hi = swap(up, down, "gy")
    early_lo, early_hi = swap(above, below, "gz")
    dm, ds, above, below = call(
        functools.partial(y_kernel, dims), (), (dm, ds, lo, hi),
        (shape(SZ, EY, CX), shape(SZ, EY, CX), shape(LATE, H, CX), shape(LATE, H, CX)),
    )
    late_lo, late_hi = swap(above, below, "gz")
    pre = call(
        functools.partial(inner_kernel, dims), (), (dm, ds), (shape(PRE, 2, EY + 2 * PADR, CX),), cost=1 << 30
    )[0]
    pre, force = lax.optimization_barrier((pre, force))
    adjoint_next = call(
        functools.partial(dual_kernel, dims),
        (),
        (force, fields) + faces,
        (shape(3, CZ, CY, CX),),
        (pltpu.VMEM((3, CZ, CY, CX), F32), pltpu.VMEM((CY, CX), F32), pltpu.SemaphoreType.DMA((3,))),
        out_specs=[ANY],
        cost=1 << 30,
    )[0]
    predicted, adjoint_next = lax.optimization_barrier((predicted, adjoint_next))
    velocity_next, pressure_next = call(
        functools.partial(sweep_kernel, dims), (), (dm, ds, pre, early_lo, early_hi, late_lo, late_hi, predicted, pressure),
        (shape(3, CZ, CY, CX), shape(CZ, CY, CX)),
        (
            pltpu.VMEM((2, EZ - CZ + 2, EY, CX), F32), pltpu.VMEM((2, 2, EZ, EY + 2 * PADR, CX), F32),
            pltpu.VMEM((3, CZ, CY, CX), F32), pltpu.VMEM((CZ, CY, CX), F32), pltpu.SemaphoreType.DMA((8,)),
        ),
        out_specs=[ANY, ANY],
    )
    return velocity_next, adjoint_next, pressure_next, yaw_grad.reshape(-1), position_grad


def solution(mesh):
    axes = ("gx", "gy", "gz")
    grid = P(None, "gz", "gy", "gx")
    cell = P("gz", "gy", "gx")
    flat = P(axes)
    return jax.shard_map(
        shards,
        mesh=mesh,
        in_specs=(grid, grid, cell, cell, flat, flat, flat, P(None, axes), flat, flat, P()),
        out_specs=(grid, grid, cell, flat, P(None, axes)),
        check_vma=False,
    )
```
